128 devices in a mesh: comp: 2 (over x_lo), tile: 64 (over z, x_hi, y, core).
Axes of the slice: x: 4 (x_hi: 2, x_lo: 2; x = x_hi * 2 + x_lo), y: 4, z: 4, core: 2. Of those that a mesh axis runs over, the one named last changes fastest.
Arguments:
- atm_state: bfloat16 [256, 4096, 256], P(None, ('comp', 'tile')), may hold values from -6 to 6
- atm_sea: int32 [4096, 256], P(('comp', 'tile')), may hold values 0 or 1
- zonal_courant: float32 [256], replicated, may hold values from 0.05 to 0.45
- atm_vertical: bfloat16 [256, 256], replicated, may hold values from -1 to 1
- ocean_state: float32 [160, 2048, 128], P(None, ('comp', 'tile')), may hold values from -6 to 6
- ocean_sea: int32 [2048, 128], P(('comp', 'tile')), may hold values 0 or 1
- flux_in: float32 [2, 2048, 128], P(None, ('comp', 'tile')), may hold values from -6 to 6
- ocean_vertical: float32 [160, 160], replicated, may hold values from -1 to 1
- remap_owner: int32 [8192, 4], P(('comp', 'tile')), may hold values from 0 to 127, all different within a row; in each aligned block of 64 rows (0 to 63, 64 to 127, ...) at most 4 rows name the same one
- remap_block: int32 [8192, 4], P(('comp', 'tile')), may hold values from 0 to 15
- remap_weight: bfloat16 [8192, 4, 128, 128], P(('comp', 'tile')), may hold values from 0 to 0.00390625
Outputs:
- atm_next: bfloat16 [256, 4096, 256], P(None, ('comp', 'tile'))
- ocean_next: float32 [160, 2048, 128], P(None, ('comp', 'tile'))
- ocean_flux: float32 [2, 2048, 128], P(None, ('comp', 'tile'))
The draws below stay inside these ranges and needn't reach their ends.
Inputs may be any that keep to these rules, and one draw needn't show every extreme that they name: `remap_owner`: in each row 4 different owners; among the 64 rows of one device no owner appears more than 4 times, a bound that some block reaches.
All inputs are finite; a program needn't handle non-finite values. No bound on the sum of `atm_sea` or of `ocean_sea` on one device may be relied on, other than what follows from the above.
Results may differ from the reference program's by a relative error of at most 0.0056.
Values may be sent and summed in bfloat16 or wider, within the bound.
No kernel may reach another device: no remote copies, remote signals or barrier semaphores. Data moves between devices by JAX's collectives and lax.ppermute only.
A program may use at most 128 MiB of HBM per device.

```python
import math
import jax
import jax.numpy as jnp
import numpy as np
from jax import lax

LA = 128
LO = 80
AX = 32
AY = 256
BLK = 128
K = 4
OY = 128
NAX = 4096
NOX = 2048
ABLK = 64
OBLK = 16
ATM_BLOCKS = 8192
CAP = 4
OWNERS = 128


def draw_atm_vertical(key, part):
    order = 2 * LA
    spread = 0.5 * math.sqrt(3.0 / order)
    noise = jax.random.uniform(key, (order, order), jnp.float32, -1.0, 1.0) * spread
    return (0.7 * jnp.eye(order, dtype=jnp.float32) + noise).astype(jnp.bfloat16)


def draw_ocean_vertical(key, part):
    order = 2 * LO
    spread = 0.5 * math.sqrt(3.0 / order)
    noise = jax.random.uniform(jax.random.fold_in(key, 7), (order, order), jnp.float32, -1.0, 1.0) * spread
    return 0.7 * jnp.eye(order, dtype=jnp.float32) + noise


def touch_ends(drawn, rng, smallest, largest):
    spot = [jax.random.randint(jax.random.fold_in(rng, axis), (), 0, length) for axis, length in enumerate(drawn.shape)]
    longest = drawn.shape.index(max(drawn.shape))
    beside = spot[:longest] + [(spot[longest] + 1) % drawn.shape[longest]] + spot[longest + 1:]
    return drawn.at[tuple(spot)].set(smallest).at[tuple(beside)].set(largest)


def steps_of(rng, extent, cuts, low, high):
    level = 1.0
    for axis_at, parts in cuts:
        heights = jax.random.uniform(jax.random.fold_in(jax.random.fold_in(rng, 6), axis_at), (parts,), jnp.float32, low / len(cuts), high / len(cuts))
        level = level * jnp.repeat(jnp.exp(heights), extent[axis_at] // parts).reshape((-1,) + (1,) * (len(extent) - 1 - axis_at))
    return level


def assign_block(stream_key, own, number, rows, count, top, bound, lean):
    ranking = jax.random.permutation(stream_key, count)
    packed, ordinary = load_shares(count, rows * top, bound, lean, True), load_shares(count, rows * top, bound, lean, False)
    places = jnp.arange(count)

    def named(sizes, turn):
        used = int((sizes > 0).sum())
        fixed = max(1, used // 4)
        passed = fixed + (places - fixed + turn * (used - fixed)) % max(1, count - fixed)
        return jnp.zeros((count,), jnp.int32).at[ranking[jnp.where(places < fixed, places, passed)]].set(jnp.asarray(sizes, jnp.int32))

    sizes = jnp.where(number % 4 == 0, named(packed, number // 4), named(ordinary, number - number // 4 - 1))
    mixed = jax.random.permutation(jax.random.fold_in(own, 3), count)
    source_of, receiver = mixed[0:count // 2 * 2:2], mixed[1:count // 2 * 2:2]
    margin = jnp.minimum(sizes[source_of] - 1, bound - sizes[receiver]) // 2
    margin = jnp.where((source_of == ranking[0]) | (receiver == ranking[0]) | (sizes[receiver] == 0), 0, jnp.maximum(margin, 0))
    passed = jax.random.randint(jax.random.fold_in(own, 4), (count // 2,), 0, 1 << 20) % (margin + 1)
    sizes = sizes.at[source_of].add(-passed).at[receiver].add(passed)
    items = jnp.searchsorted(jnp.cumsum(sizes), jnp.arange(rows * top), side="right").astype(jnp.int32)
    table = items.reshape(top, rows).T
    table = table[jax.random.permutation(jax.random.fold_in(own, 1), rows)]
    turn = jax.random.randint(jax.random.fold_in(own, 2), (rows, 1), 0, top)
    return jnp.take_along_axis(table, (jnp.arange(top)[None, :] + turn) % top, axis=1)


def load_shares(count, total, reach, slope, full):
    weights = [(1 << 20) // math.isqrt(grade ** slope) + 1 for grade in range(1, count + 1)]
    largest = reach if full else min(reach, max(-(-total // count), total * weights[0] // sum(weights)))
    least = 1 if total - largest >= count - 1 else 0
    holding, surplus = [largest] + [least] * (count - 1), total - largest - least * (count - 1)
    while surplus > 0:
        movable = [i for i in range(1, count) if holding[i] < largest] or [i for i in range(1, count) if holding[i] < reach]
        mass, left = sum([weights[i] for i in movable]), surplus
        for i in movable:
            more = min(reach - holding[i], max(1, left * weights[i] // mass), surplus)
            holding[i] = holding[i] + more
            surplus = surplus - more
    return np.array(holding)


def scatter_about(own_key, shape, deviation, bound, cuts=(), held_as=jnp.bfloat16):
    factor_of = steps_of(own_key, shape, cuts, -0.22, 0.18) if cuts else 1.0
    drawn = jax.random.normal(own_key, shape, jnp.float32) * deviation * factor_of
    return jnp.minimum(jnp.maximum(drawn, -bound), bound).astype(held_as)


def setup_inputs(seed: int = 0) -> dict:
    streams_of = jax.random.split(jax.random.key(seed), 12)
    atm_state = scatter_about(streams_of[0], (2 * LA, NAX, AY), 1.0, 6.0, ((1, 128),))
    atm_sea = touch_ends((jax.random.randint(streams_of[1], (NAX, AY), 0, 3) < 2).astype(jnp.int32), jax.random.fold_in(streams_of[1], 1), 0, 1)
    zonal_courant = jnp.clip(jnp.exp(jax.random.uniform(streams_of[2], (2 * LA,), jnp.float32, math.log(0.05), math.log(0.45))), 0.05, 0.45)
    atm_vertical = draw_atm_vertical(jax.random.fold_in(streams_of[11], 71), 0)
    ocean_state = scatter_about(streams_of[4], (2 * LO, NOX, OY), 1.0, 6.0, ((1, 128),), jnp.float32)
    ocean_sea = touch_ends((jax.random.randint(streams_of[5], (NOX, OY), 0, 4) < 3).astype(jnp.int32), jax.random.fold_in(streams_of[5], 1), 0, 1)
    flux_in = scatter_about(streams_of[6], (2, NOX, OY), 1.0, 6.0, ((1, 128),), jnp.float32)
    ocean_vertical = draw_ocean_vertical(jax.random.fold_in(streams_of[11], 71), 0)
    remap_owner_keys = jax.random.split(jax.random.fold_in(streams_of[8], 1), ATM_BLOCKS // ABLK)
    remap_owner_turns = jax.random.permutation(jax.random.fold_in(streams_of[8], 3), ATM_BLOCKS // ABLK)
    remap_owner = jax.vmap(lambda own, number: assign_block(jax.random.fold_in(streams_of[8], 2), own, number, ABLK, OWNERS, K, CAP, 1))(remap_owner_keys, remap_owner_turns).reshape((ATM_BLOCKS, K))
    remap_block = touch_ends(jax.random.randint(streams_of[9], (ATM_BLOCKS, K), 0, OBLK), jax.random.fold_in(streams_of[9], 1), 0, OBLK - 1).astype(jnp.int32)
    remap_weight = jnp.clip(0.00390625 * jax.random.uniform(streams_of[10], (ATM_BLOCKS, K, BLK, BLK), jnp.float32) ** steps_of(streams_of[10], (ATM_BLOCKS, K, BLK, BLK), ((0, 128),), -0.2, 0.2), 0.0, 0.00390625).astype(jnp.bfloat16)
    return {"atm_state": atm_state, "atm_sea": atm_sea, "zonal_courant": zonal_courant, "atm_vertical": atm_vertical, "ocean_state": ocean_state, "ocean_sea": ocean_sea, "flux_in": flux_in, "ocean_vertical": ocean_vertical, "remap_owner": remap_owner, "remap_block": remap_block, "remap_weight": remap_weight}


ATM_DIFFUSION = 0.1
OCEAN_DIFFUSION = 0.15
EXCHANGE_RATE = 0.3
FLUX_GAIN = 0.5


def lateral_sum(center):
    north = jnp.concatenate([center[:, :, 1:], center[:, :, -1:]], axis=2)
    south = jnp.concatenate([center[:, :, :1], center[:, :, :-1]], axis=2)
    return north + south


def atmos_advance(padded, sea_temp, sea_frac, courant, vertical):
    height = padded.shape[0]
    levels = height // 2
    center = padded[:, 1:-1].astype(jnp.float32)
    west_side = padded[:, :-2].astype(jnp.float32)
    east_side = padded[:, 2:].astype(jnp.float32)
    tendency = east_side + west_side + lateral_sum(center) - 4.0 * center
    updated = center - courant[:, None, None] * (center - west_side) + ATM_DIFFUSION * tendency
    heat_flux = EXCHANGE_RATE * sea_frac * (sea_temp - updated[levels - 1])
    moist_flux = EXCHANGE_RATE * sea_frac * (0.5 * sea_temp - updated[2 * levels - 1])
    rows = lax.broadcasted_iota(jnp.int32, (height, 1, 1), 0)
    added = jnp.where(rows == levels - 1, heat_flux[None], jnp.where(rows == 2 * levels - 1, moist_flux[None], jnp.zeros_like(heat_flux)[None]))
    forced = (updated + added).astype(jnp.bfloat16)
    mixed = jnp.dot(vertical, forced.reshape(height, -1), preferred_element_type=jnp.float32)
    return mixed.reshape(forced.shape).astype(jnp.bfloat16), heat_flux, moist_flux


def ocean_advance(padded, sea_frac, flux_old, vertical):
    height = padded.shape[0]
    levels = height // 2
    center = padded[:, 1:-1]
    tendency = padded[:, 2:] + padded[:, :-2] + lateral_sum(center) - 4.0 * center
    rows = lax.broadcasted_iota(jnp.int32, (height, 1, 1), 0)
    heat_in = FLUX_GAIN * sea_frac * flux_old[0]
    fresh_in = FLUX_GAIN * sea_frac * flux_old[1]
    added = jnp.where(rows == 0, heat_in[None], jnp.where(rows == levels, fresh_in[None], jnp.zeros_like(heat_in)[None]))
    updated = (center + OCEAN_DIFFUSION * tendency) * sea_frac + added
    mixed = jnp.dot(vertical, updated.reshape(height, -1), precision=lax.Precision.HIGHEST, preferred_element_type=jnp.float32)
    return mixed.reshape(updated.shape)


def wrap_columns(field):
    return jnp.concatenate([field[:, -1:], field, field[:, :1]], axis=1)


def atmos_global(state, sea_temp, sea_atm, courant, vertical):
    groups = state.shape[1] // AX
    wrapped = wrap_columns(state)

    def advance_group(index):
        start = (index * AX).astype(jnp.int32)
        padded = lax.dynamic_slice_in_dim(wrapped, start, AX + 2, 1)
        temps = lax.dynamic_slice_in_dim(sea_temp, start, AX, 0)
        fracs = lax.dynamic_slice_in_dim(sea_atm, start, AX, 0)
        new_part, heat_part, moist_part = atmos_advance(padded, temps, fracs, courant, vertical)
        return new_part, jnp.stack([heat_part, moist_part])

    new_parts, flux_parts = lax.map(advance_group, jnp.arange(groups, dtype=jnp.int32))
    new_state = jnp.moveaxis(new_parts, 0, 1).reshape(state.shape)
    fluxes = jnp.moveaxis(flux_parts, 0, 1).reshape((2,) + sea_atm.shape)
    return new_state, fluxes


def reference(atm_state, atm_sea, zonal_courant, atm_vertical, ocean_state, ocean_sea, flux_in, ocean_vertical, remap_owner, remap_block, remap_weight):
    sea_atm = atm_sea.astype(jnp.float32)
    sea_ocean = ocean_sea.astype(jnp.float32)
    ocean_blocks = ocean_state[0].reshape(-1, BLK).astype(jnp.bfloat16)
    targets = (remap_owner * OBLK + remap_block).astype(jnp.int32)
    groups = ATM_BLOCKS // ABLK
    weights = remap_weight.reshape(groups, ABLK, K, BLK, BLK)
    fetched = ocean_blocks[targets].reshape(groups, ABLK, K, BLK)

    def pull(pair):
        weight_part, fetched_part = pair
        return jnp.einsum("jkao,jko->ja", weight_part.astype(jnp.float32), fetched_part.astype(jnp.float32), precision=lax.Precision.HIGHEST)

    sea_temp = lax.map(pull, (weights, fetched)).reshape(atm_sea.shape)
    state = atm_state
    flux_sum = jnp.zeros((2,) + atm_sea.shape, jnp.float32)
    for which_step in range(2):
        state, fluxes = atmos_global(state, sea_temp, sea_atm, zonal_courant, atm_vertical)
        flux_sum = flux_sum + 0.5 * fluxes
    flux_blocks = flux_sum.astype(jnp.bfloat16).reshape(2, groups, ABLK, BLK)

    def push(pair):
        weight_part, flux_part = pair
        return jnp.einsum("jkao,vja->jkvo", weight_part.astype(jnp.float32), flux_part.astype(jnp.float32), precision=lax.Precision.HIGHEST)

    shares = lax.map(push, (weights, jnp.moveaxis(flux_blocks, 1, 0)))
    summed = jax.ops.segment_sum(shares.reshape(-1, 2, BLK), targets.reshape(-1), num_segments=ocean_blocks.shape[0])
    ocean_flux = jnp.moveaxis(summed, 1, 0).reshape((2,) + ocean_sea.shape) * sea_ocean
    new_ocean = ocean_advance(wrap_columns(ocean_state), sea_ocean, flux_in, ocean_vertical)
    return state, new_ocean, ocean_flux
```

```python
import functools

import jax
import jax.numpy as jnp
from jax import lax
from jax.experimental import pallas as pl
from jax.experimental.pallas import tpu as pltpu
from jax.sharding import PartitionSpec as P

ATM_DIFFUSION = 0.1
OCEAN_DIFFUSION = 0.15
EXCHANGE_RATE = 0.3
FLUX_GAIN = 0.5

F32 = jnp.float32
BF16 = jnp.bfloat16
VM = pltpu.VMEM
BOTH = ("comp", "tile")
HEAD = 24


def call(kernel, outs, *args, scratch=(), spaces=None, flops=0, touched=0, limit=48):
    spaces = spaces or [VM] * len(args)
    return pl.pallas_call(
        kernel,
        out_shape=outs,
        in_specs=[pl.BlockSpec(memory_space=s) for s in spaces],
        out_specs=jax.tree.map(lambda _: pl.BlockSpec(memory_space=VM), outs),
        scratch_shapes=list(scratch),
        compiler_params=pltpu.CompilerParams(vmem_limit_bytes=limit << 20),
        cost_estimate=pl.CostEstimate(flops=flops, bytes_accessed=touched, transcendentals=0),
    )(*args)


def shape(dims, dtype):
    return jax.ShapeDtypeStruct(dims, dtype)


def iota(dims, axis):
    return lax.broadcasted_iota(jnp.int32, dims, axis)


def columns(ref):
    return jnp.concatenate([ref[:, k : k + 1] for k in range(ref.shape[1])], axis=0)


def plan_kernel(owner_ref, block_ref, surface_ref, head_ref, place_ref, slot_rows):
    devices = head_ref.shape[0]
    owner, block = columns(owner_ref), columns(block_ref)
    pairs = owner.shape[0]
    hits = (owner == iota((pairs, devices), 1)).astype(F32)
    earlier = (iota((pairs, pairs), 1) < iota((pairs, pairs), 0)).astype(F32)
    before = jnp.dot(earlier.astype(BF16), hits.astype(BF16), preferred_element_type=F32)
    slot = jnp.sum(before * hits, axis=1, keepdims=True)
    marked = jnp.where(
        slot == iota((pairs, 128), 1).astype(F32), (block + 1).astype(F32), 0.0
    )
    wanted = jnp.dot(
        jnp.transpose(hits).astype(BF16), marked.astype(BF16), preferred_element_type=F32
    )
    place = owner.astype(F32) * 8.0 + slot
    spread = jnp.transpose(jnp.broadcast_to(place, (pairs, 128)))
    place_ref[...] = spread[:8].astype(jnp.int32)
    slot_rows[...] = jnp.zeros_like(slot_rows)
    slot_rows[pl.ds(0, devices, stride=8), :] = wanted
    surface = surface_ref[...].astype(BF16)
    head_ref[:, 0:16, :] = jnp.broadcast_to(surface[None], (devices, 16, 128))
    head_ref[:, 16:24, :] = slot_rows[...].reshape(devices, 8, 128).astype(BF16)


def turn_kernel(state_ref, turned_ref, first_ref, last_ref):
    rows, cells = state_ref.shape[0], state_ref.shape[1]
    step = 16

    @pl.loop(0, rows // step)
    def _(i):
        at = pl.multiple_of(i * step, step)
        part = state_ref[pl.ds(at, step)].astype(F32)
        turned_ref[:, pl.ds(at, step), :] = jnp.swapaxes(part, 0, 1).astype(BF16)

    first_ref[...] = turned_ref[0]
    last_ref[...] = turned_ref[cells - 1]


def lateral_matrix(size):
    row, col = iota((size, size), 0), iota((size, size), 1)
    near = jnp.where(jnp.abs(row - col) == 1, 1.0, 0.0)
    edge = jnp.where((row == 0) | (row == size - 1), -3.0, -4.0)
    return (near + jnp.where(row == col, edge, 0.0)).astype(BF16)


def without_forced(vertical):
    height = vertical.shape[0]
    col = iota(vertical.shape, 1)
    keep = (col != height // 2 - 1) & (col != height - 1)
    return jnp.where(keep, vertical.astype(F32), 0.0).astype(BF16)


def stencil(west, center, east, lateral, courant):
    w, c, e = west.astype(F32), center.astype(F32), east.astype(F32)
    side = jnp.dot(center, lateral, preferred_element_type=F32)
    return c + courant * (w - c) + ATM_DIFFUSION * (w + e + side)


def first_step_kernel(
    turned_ref, left_ref, right_ref, courant_ref, vertical_ref,
    mixed_ref, first_ref, last_ref, upper_ref, lower_ref, upper_mix_ref, lower_mix_ref,
):
    cells, height = turned_ref.shape[0], turned_ref.shape[1]
    top, low = height // 2 - 1, height - 1
    lateral = lateral_matrix(turned_ref.shape[2])
    vertical = without_forced(vertical_ref[...])
    courant = courant_ref[...]

    def body(x, west, center, east):
        updated = stencil(west, center, east, lateral, courant)
        upper_ref[pl.ds(x, 1), :] = updated[top : top + 1]
        lower_ref[pl.ds(x, 1), :] = updated[low : low + 1]
        mixed = jnp.dot(vertical, updated.astype(BF16), preferred_element_type=F32)
        upper_mix_ref[pl.ds(x, 1), :] = mixed[top : top + 1]
        lower_mix_ref[pl.ds(x, 1), :] = mixed[low : low + 1]
        mixed_ref[x] = mixed.astype(BF16)

    body(0, left_ref[...], turned_ref[0], turned_ref[1])

    @pl.loop(1, cells - 1)
    def _(x):
        body(x, turned_ref[x - 1], turned_ref[x], turned_ref[x + 1])

    body(cells - 1, turned_ref[cells - 2], turned_ref[cells - 1], right_ref[...])
    first_ref[...] = mixed_ref[0]
    last_ref[...] = mixed_ref[cells - 1]


def ocean_kernel(ocean_ref, left_ref, right_ref, sea_ref, flux_ref, vertical_ref, out_ref):
    cells, width = sea_ref.shape
    height = ocean_ref.shape[0] // cells
    vertical = vertical_ref[...]
    high = vertical.astype(BF16)
    low = (vertical - high.astype(F32)).astype(BF16)
    lane = iota((height, width), 1)
    row = iota((height, width), 0)

    def column(x):
        if x < 0:
            return left_ref[...]
        if x >= cells:
            return right_ref[...]
        return ocean_ref[pl.ds(x, height, stride=cells), :]

    for x in range(cells):
        west, center, east = column(x - 1), column(x), column(x + 1)
        north = jnp.where(lane == width - 1, center, pltpu.roll(center, width - 1, 1))
        south = jnp.where(lane == 0, center, pltpu.roll(center, 1, 1))
        wet = sea_ref[x : x + 1, :].astype(F32)
        near = east + west + (north + south) - 4.0 * center
        heat = FLUX_GAIN * wet * flux_ref[0, x : x + 1, :]
        fresh = FLUX_GAIN * wet * flux_ref[1, x : x + 1, :]
        added = jnp.where(row == 0, heat, jnp.where(row == height // 2, fresh, 0.0))
        updated = (center + OCEAN_DIFFUSION * near) * wet + added
        upper = updated.astype(BF16)
        rest = (updated - upper.astype(F32)).astype(BF16)
        mixed = jnp.dot(high, upper, preferred_element_type=F32)
        mixed += jnp.dot(high, rest, preferred_element_type=F32)
        mixed += jnp.dot(low, upper, preferred_element_type=F32)
        out_ref[pl.ds(x, height, stride=cells), :] = mixed


def edges_kernel(ocean_ref, first_ref, last_ref):
    height = first_ref.shape[0]
    cells = ocean_ref.shape[0] // height
    first_ref[...] = ocean_ref[pl.ds(0, height, stride=cells), :]
    last_ref[...] = ocean_ref[pl.ds(cells - 1, height, stride=cells), :]


PARTS = 8


def weight_copies(weight_ref, held, sems):
    step = weight_ref.shape[0] // PARTS
    return [
        pltpu.make_async_copy(
            weight_ref.at[pl.ds(i * step, step)], held.at[pl.ds(i * step, step)], sems.at[i]
        )
        for i in range(PARTS)
    ]


def pull_kernel(
    head_ref, owner_ref, block_ref, weight_ref, sea_ref, upper_ref, lower_ref,
    temp_ref, upper_forced_ref, lower_forced_ref, first_ref, last_ref, slots_ref,
    held, sems, slot_rows, by_block,
):
    copies = weight_copies(weight_ref, held, sems)
    for c in copies:
        c.start()
    devices = head_ref.shape[0]
    surface = head_ref[:, 0:16, :].reshape(devices * 16, 128)
    slot_rows[...] = head_ref[:, 16:24, :].astype(F32).reshape(devices * 8, 128)
    slots_ref[...] = jnp.transpose(slot_rows[pl.ds(0, devices, stride=8), :])[:8]
    blocks, sources = owner_ref.shape
    goal = columns(owner_ref) * 16 + columns(block_ref)
    pick = (goal == iota((blocks * sources, devices * 16), 1)).astype(F32).astype(BF16)
    fetched = jnp.dot(pick, surface, preferred_element_type=F32)
    wanted = jnp.concatenate(
        [jnp.transpose(fetched[k * blocks : (k + 1) * blocks]) for k in range(sources)], axis=0
    ).astype(BF16)
    lane = iota((128, blocks), 1)
    step = blocks // PARTS

    def add(j, total):
        rows = jnp.concatenate([held[j, k] for k in range(sources)], axis=1)
        product = jnp.dot(rows, wanted, preferred_element_type=F32)
        return jnp.where(lane == j, product, total)

    total = jnp.zeros((128, blocks), F32)
    for i, c in enumerate(copies):
        c.wait()
        total = lax.fori_loop(i * step, (i + 1) * step, add, total, unroll=True)
    by_block[...] = jnp.transpose(total)
    half = blocks // 2
    temp = jnp.concatenate(
        [by_block[pl.ds(h, half, stride=2), :] for h in range(2)], axis=1
    )
    temp_ref[...] = temp
    exchange = EXCHANGE_RATE * sea_ref[...].astype(F32)
    upper, lower = upper_ref[...], lower_ref[...]
    upper = (upper + exchange * (temp - upper)).astype(BF16).astype(F32)
    lower = (lower + exchange * (0.5 * temp - lower)).astype(BF16).astype(F32)
    upper_forced_ref[...] = upper
    lower_forced_ref[...] = lower
    two = iota((8, upper.shape[1]), 0) == 0
    first_ref[...] = jnp.where(two, upper[0:1], lower[0:1])
    last_ref[...] = jnp.where(two, upper[half - 1 : half], lower[half - 1 : half])


def push_kernel(
    place_ref, weight_ref, sea_ref, temp_ref, upper_ref, lower_ref,
    upper_forced_ref, lower_forced_ref, upper_mix_ref, lower_mix_ref,
    left_forced_ref, right_forced_ref, left_mix_ref, right_mix_ref,
    courant_ref, vertical_ref, out_ref,
    held, sems, flux_rows, shares,
):
    copies = weight_copies(weight_ref, held, sems)
    for c in copies:
        c.start()
    height = vertical_ref.shape[0]
    top, low = height // 2 - 1, height - 1
    cells, width = sea_ref.shape
    sub, lane = iota((cells, width), 0), iota((cells, width), 1)

    def row_of(r, mix, upper, lower):
        a = vertical_ref[pl.ds(r - 7, 8), :].astype(F32)[7:8]
        kept = mix.astype(BF16).astype(F32)
        return (kept + a[:, top : top + 1] * upper + a[:, low : low + 1] * lower).astype(BF16).astype(F32)

    def updated(r, mix_ref):
        center = row_of(r, mix_ref[...], upper_forced_ref[...], lower_forced_ref[...])
        sides = [
            row_of(r, m[pl.ds(r - 7, 8), :].astype(F32)[7:8], f[0:1], f[1:2])
            for m, f in ((left_mix_ref, left_forced_ref), (right_mix_ref, right_forced_ref))
        ]
        west = jnp.where(sub == 0, sides[0], pltpu.roll(center, 1, 0))
        east = jnp.where(sub == cells - 1, sides[1], pltpu.roll(center, cells - 1, 0))
        north = jnp.where(lane == width - 1, center, pltpu.roll(center, width - 1, 1))
        south = jnp.where(lane == 0, center, pltpu.roll(center, 1, 1))
        near = east + west + (north + south) - 4.0 * center
        courant = courant_ref[pl.ds(r - 7, 8), :][7:8]
        return center - courant * (center - west) + ATM_DIFFUSION * near

    exchange = EXCHANGE_RATE * sea_ref[...].astype(F32)
    temp = temp_ref[...]
    heat = 0.5 * (exchange * (temp - upper_ref[...])) + 0.5 * (
        exchange * (temp - updated(top, upper_mix_ref))
    )
    moist = 0.5 * (exchange * (0.5 * temp - lower_ref[...])) + 0.5 * (
        exchange * (0.5 * temp - updated(low, lower_mix_ref))
    )
    flux_rows[...] = jnp.zeros_like(flux_rows)
    for v, flux in enumerate((heat, moist)):
        for h in range(2):
            flux_rows[pl.ds(h * 8 + v, cells, stride=16), :] = flux[:, h * 128 : (h + 1) * 128]
    blocks, sources = held.shape[0], held.shape[1]
    step = blocks // PARTS

    for i, c in enumerate(copies):
        c.wait()

        @pl.loop(i * step, (i + 1) * step, unroll=True)
        def _(j):
            rows = flux_rows[pl.ds(pl.multiple_of(j * 8, 8), 8), :].astype(BF16)
            for k in range(sources):
                got = jnp.dot(rows, held[j, k], preferred_element_type=F32)
                shares[pl.ds(pl.multiple_of((k * blocks + j) * 8, 8), 8), :] = got

    pairs = blocks * sources
    place = place_ref[0:1, :]
    rows = iota((out_ref.shape[0], pairs), 0)
    total = jnp.zeros(out_ref.shape, F32)
    for v in range(2):
        pick = (rows == place + 4 * v).astype(F32).astype(BF16)
        share = shares[pl.ds(v, pairs, stride=8), :].astype(BF16)
        total += jnp.dot(pick, share, preferred_element_type=F32)
    out_ref[...] = total.astype(BF16)


def second_step_kernel(
    mixed_ref, left_ref, right_ref, courant_ref, vertical_ref, sea_ref, temp_ref,
    upper_forced_ref, lower_forced_ref, left_forced_ref, right_forced_ref,
    out_ref, state, result,
):
    cells, height = mixed_ref.shape[0], mixed_ref.shape[1]
    top, low = height // 2 - 1, height - 1
    lateral = lateral_matrix(mixed_ref.shape[2])
    vertical = vertical_ref[...]
    upper_column = vertical[:, top : top + 1].astype(F32)
    lower_column = vertical[:, low : low + 1].astype(F32)
    courant = courant_ref[...]

    def complete(mixed, upper, lower):
        return (mixed.astype(F32) + upper_column * upper + lower_column * lower).astype(BF16)

    state[0] = complete(left_ref[...], left_forced_ref[0:1], left_forced_ref[1:2])
    state[cells + 1] = complete(right_ref[...], right_forced_ref[0:1], right_forced_ref[1:2])

    @pl.loop(0, cells)
    def _(x):
        state[x + 1] = complete(
            mixed_ref[x], upper_forced_ref[pl.ds(x, 1), :], lower_forced_ref[pl.ds(x, 1), :]
        )

    last = iota((8, mixed_ref.shape[2]), 0) == 7

    @pl.loop(0, cells)
    def _(x):
        updated = stencil(state[x], state[x + 1], state[x + 2], lateral, courant)
        exchange = EXCHANGE_RATE * sea_ref[pl.ds(x, 1), :].astype(F32)
        temp = temp_ref[pl.ds(x, 1), :]
        upper = updated[top - 7 : top + 1]
        lower = updated[low - 7 : low + 1]
        upper = jnp.where(last, upper + exchange * (temp - upper), upper)
        lower = jnp.where(last, lower + exchange * (0.5 * temp - lower), lower)
        forced = jnp.concatenate(
            [updated[: top - 7], upper, updated[top + 1 : low - 7], lower], axis=0
        ).astype(BF16)
        result[x] = jnp.dot(vertical, forced, preferred_element_type=F32).astype(BF16)

    step = 16

    @pl.loop(0, height // step)
    def _(i):
        at = pl.multiple_of(i * step, step)
        part = result[:, pl.ds(at, step), :].astype(F32)
        out_ref[pl.ds(at, step)] = jnp.swapaxes(part, 0, 1).astype(BF16)


def land_kernel(incoming_ref, slots_ref, sea_ref, out_ref, wide):
    devices = slots_ref.shape[1]
    cells = sea_ref.shape[0]
    wide[...] = incoming_ref[...].astype(F32)
    wet = sea_ref[...].astype(F32)
    here = (iota((cells, devices), 0) + 1).astype(F32)
    picks = [(slots_ref[s : s + 1, :] == here).astype(F32).astype(BF16) for s in range(4)]
    for v in range(2):
        total = jnp.zeros((cells, 128), F32)
        for s in range(4):
            part = wide[pl.ds(v * 4 + s, devices, stride=8), :].astype(BF16)
            total += jnp.dot(picks[s], part, preferred_element_type=F32)
        out_ref[v] = total * wet


def swap(first, last):
    peers = lax.axis_size(BOTH)
    up = [(i, (i + 1) % peers) for i in range(peers)]
    down = [(j, i) for i, j in up]
    return lax.ppermute(last, BOTH, up), lax.ppermute(first, BOTH, down)


def per_device(
    atm_state, atm_sea, zonal_courant, atm_vertical, ocean_state, ocean_sea,
    flux_in, ocean_vertical, remap_owner, remap_block, remap_weight,
):
    devices = lax.axis_size(BOTH)
    height, cells, width = atm_state.shape
    blocks, sources = remap_owner.shape
    pairs = blocks * sources
    courant = zonal_courant.reshape(height, 1)
    layers, ocean_cells, ocean_width = ocean_state.shape
    ocean_rows = ocean_state.reshape(layers * ocean_cells, ocean_width)

    head, place = call(
        plan_kernel,
        (shape((devices, HEAD, 128), BF16), shape((8, pairs), jnp.int32)),
        remap_owner, remap_block, ocean_state[0],
        scratch=[pltpu.VMEM((devices * 8, 128), F32)],
        touched=1 << 20,
    )
    gathered = lax.all_to_all(head, BOTH, split_axis=0, concat_axis=0, tiled=True)

    column = shape((height, width), BF16)
    turned, first, last = call(
        turn_kernel,
        (shape((cells, height, width), BF16), column, column),
        atm_state,
        touched=12 << 20,
    )
    left, right = swap(first, last)
    ocean_first, ocean_last = call(
        edges_kernel,
        (shape((layers, ocean_width), F32),) * 2,
        ocean_rows,
        touched=2 << 20,
    )
    ocean_left, ocean_right = swap(ocean_first, ocean_last)
    row = shape((cells, width), F32)
    mixed, mixed_first, mixed_last, upper, lower, upper_mix, lower_mix = call(
        first_step_kernel,
        (shape((cells, height, width), BF16), column, column, row, row, row, row),
        turned, left, right, courant, atm_vertical,
        touched=16 << 20,
    )
    mixed_left, mixed_right = swap(mixed_first, mixed_last)
    new_ocean = call(
        ocean_kernel,
        shape(ocean_rows.shape, F32),
        ocean_rows, ocean_left, ocean_right, ocean_sea, flux_in, ocean_vertical,
        touched=8 << 20,
    )

    small = shape((8, width), F32)
    held = [pltpu.VMEM(remap_weight.shape, BF16), pltpu.SemaphoreType.DMA((PARTS,))]
    temp, upper_forced, lower_forced, forced_first, forced_last, slots = call(
        pull_kernel,
        (row, row, row, small, small, shape((8, devices), F32)),
        gathered, remap_owner, remap_block, remap_weight, atm_sea, upper, lower,
        spaces=[VM, VM, VM, pl.ANY, VM, VM, VM],
        scratch=[*held, pltpu.VMEM((devices * 8, 128), F32), pltpu.VMEM((blocks, 128), F32)],
        touched=12 << 20,
    )
    forced_left, forced_right = swap(forced_first, forced_last)
    outgoing = call(
        push_kernel,
        shape((devices * 8, 128), BF16),
        place, remap_weight, atm_sea, temp, upper, lower,
        upper_forced, lower_forced, upper_mix, lower_mix,
        forced_left, forced_right, mixed_left, mixed_right, courant, atm_vertical,
        spaces=[VM, pl.ANY] + [VM] * 14,
        scratch=[*held, pltpu.VMEM((blocks * 8, 128), F32), pltpu.VMEM((pairs * 8, 128), F32)],
        touched=12 << 20,
    )
    incoming = lax.all_to_all(
        outgoing.reshape(devices, 8, 128), BOTH, split_axis=0, concat_axis=0, tiled=True
    )
    state = call(
        second_step_kernel,
        shape(atm_state.shape, BF16),
        mixed, mixed_left, mixed_right, courant, atm_vertical, atm_sea, temp,
        upper_forced, lower_forced, forced_left, forced_right,
        scratch=[
            pltpu.VMEM((cells + 2, height, width), BF16),
            pltpu.VMEM((cells, height, width), BF16),
        ],
        touched=24 << 20,
    )
    ocean_flux = call(
        land_kernel,
        shape((2, ocean_cells, ocean_width), F32),
        incoming.reshape(devices * 8, 128), slots, ocean_sea,
        scratch=[pltpu.VMEM((devices * 8, 128), F32)],
        touched=1 << 20,
    )
    return state, new_ocean.reshape(ocean_state.shape), ocean_flux


def solution(mesh):
    return jax.shard_map(
        per_device,
        mesh=mesh,
        in_specs=(
            P(None, BOTH, None), P(BOTH, None), P(), P(), P(None, BOTH, None), P(BOTH, None),
            P(None, BOTH, None), P(), P(BOTH, None), P(BOTH, None), P(BOTH, None, None, None),
        ),
        out_specs=(P(None, BOTH, None), P(None, BOTH, None), P(None, BOTH, None)),
        check_vma=False,
    )
```

```python
import functools

import jax
import jax.numpy as jnp
from jax import lax
from jax.experimental import pallas as pl
from jax.experimental.pallas import tpu as pltpu
from jax.sharding import PartitionSpec as P

ATM_DIFFUSION = 0.1
OCEAN_DIFFUSION = 0.15
EXCHANGE_RATE = 0.3
FLUX_GAIN = 0.5

F32 = jnp.float32
BF16 = jnp.bfloat16
VM = pltpu.VMEM
BOTH = ("comp", "tile")
HEAD = 24


def call(kernel, outs, *args, scratch=(), specs=None, out_specs=None, limit=50, touched=0, grid=()):
    specs, out_specs = specs or {}, out_specs or {}
    single = not isinstance(outs, tuple)
    placed = [
        out_specs.get(i, pl.BlockSpec(memory_space=VM)) for i in range(1 if single else len(outs))
    ]
    return pl.pallas_call(
        kernel,
        out_shape=outs,
        grid=grid,
        in_specs=[specs.get(i, pl.BlockSpec(memory_space=VM)) for i in range(len(args))],
        out_specs=placed[0] if single else tuple(placed),
        scratch_shapes=list(scratch),
        compiler_params=pltpu.CompilerParams(vmem_limit_bytes=limit << 20),
        cost_estimate=pl.CostEstimate(flops=0, bytes_accessed=touched, transcendentals=0),
    )(*args)


SCALAR = pl.BlockSpec(memory_space=pltpu.SMEM)
ANY = pl.BlockSpec(memory_space=pltpu.HBM)


def start_all(copies):
    for c in copies:
        c.start()
    return copies


def wait_all(copies):
    for c in copies:
        c.wait()


def shape(dims, dtype):
    return jax.ShapeDtypeStruct(dims, dtype)


def iota(dims, axis):
    return lax.broadcasted_iota(jnp.int32, dims, axis)


def columns(ref):
    count, rows = ref.shape
    wide = [jnp.broadcast_to(ref[k : k + 1, :], (128, rows)) for k in range(count)]
    return jnp.concatenate([jnp.transpose(w) for w in wide], axis=0)


def is_odd():
    return jnp.bitwise_and(lax.axis_index("tile"), 1).astype(jnp.int32).reshape(1)


def plan_kernel(
    owner_hbm, block_hbm, ocean_hbm, head_ref, place_ref, slot_rows, owner_ref, block_ref, surface_ref, sems
):
    copies = start_all([
        pltpu.make_async_copy(owner_hbm, owner_ref, sems.at[0]),
        pltpu.make_async_copy(block_hbm, block_ref, sems.at[1]),
        pltpu.make_async_copy(ocean_hbm.at[0], surface_ref, sems.at[2]),
    ])
    devices = head_ref.shape[0]
    slot_rows[...] = jnp.zeros_like(slot_rows)
    wait_all(copies)
    owner, block = columns(owner_ref), columns(block_ref)
    pairs = owner.shape[0]
    hits = (owner == iota((pairs, devices), 1)).astype(F32)
    earlier = (iota((pairs, pairs), 1) < iota((pairs, pairs), 0)).astype(F32)
    before = jnp.dot(earlier.astype(BF16), hits.astype(BF16), preferred_element_type=F32)
    slot = jnp.sum(before * hits, axis=1, keepdims=True)
    marked = jnp.where(
        slot == iota((pairs, 128), 1).astype(F32), (block + 1).astype(F32), 0.0
    )
    wanted = jnp.dot(
        jnp.transpose(hits).astype(BF16), marked.astype(BF16), preferred_element_type=F32
    )
    spread = jnp.transpose(owner.astype(F32) * 8.0 + slot)
    place_ref[...] = spread[:8].astype(jnp.int32)
    slot_rows[pl.ds(0, devices, stride=8), :] = wanted
    surface = surface_ref[...].astype(BF16)
    head_ref[:, 0:16, :] = jnp.broadcast_to(surface[None], (devices, 16, 128))
    head_ref[:, 16:24, :] = slot_rows[...].reshape(devices, 8, 128).astype(BF16)


def turn_kernel(odd_ref, state_ref, ocean_hbm, turned_ref, send_ref, ocean_send_ref, sems):
    i, odd = pl.program_id(0), odd_ref[0]
    rows, cells = state_ref.shape[0], state_ref.shape[1]
    copies = [
        pltpu.make_async_copy(ocean_hbm.at[:, x], ocean_send_ref.at[to], sems.at[n])
        for n, (x, to) in enumerate(((0, 1 - odd), (ocean_hbm.shape[1] - 1, odd)))
    ]
    pl.when(i == 0)(lambda: (start_all(copies), None)[1])
    step = 32
    for n in range(rows // step):
        turned_ref[:, n * step : (n + 1) * step, :] = jnp.swapaxes(
            state_ref[n * step : (n + 1) * step], 0, 1
        )
    at = pl.ds(pl.multiple_of(i * rows, rows), rows)
    send_ref[1 - odd, :, at, :] = turned_ref[0:2]
    send_ref[odd, :, at, :] = turned_ref[cells - 2 : cells]
    pl.when(i == pl.num_programs(0) - 1)(lambda: wait_all(copies))


def sides(odd_ref, within, across):
    odd = odd_ref[0] == 1
    return jnp.where(odd, within, across), jnp.where(odd, across, within)


def lateral_matrix(size):
    row, col = iota((size, size), 0), iota((size, size), 1)
    near = jnp.where(jnp.abs(row - col) == 1, 1.0, 0.0)
    edge = jnp.where((row == 0) | (row == size - 1), -3.0, -4.0)
    return (near + jnp.where(row == col, edge, 0.0)).astype(BF16)


def without_forced(vertical):
    height = vertical.shape[0]
    col = iota(vertical.shape, 1)
    keep = (col != height // 2 - 1) & (col != height - 1)
    return jnp.where(keep, vertical.astype(F32), 0.0).astype(BF16)


def stencil(west, center, east, lateral, courant):
    w, c, e = west.astype(F32), center.astype(F32), east.astype(F32)
    side = jnp.dot(center, lateral, preferred_element_type=F32)
    return c + courant * (w - c) + ATM_DIFFUSION * (w + e + side)


GROUP = 8


def groups(hbm, held, sems, out=False):
    copies = []
    for g in range(held.shape[0] // GROUP):
        at = pl.ds(g * GROUP, GROUP)
        ends = (held.at[at], hbm.at[at]) if out else (hbm.at[at], held.at[at])
        copies.append(pltpu.make_async_copy(*ends, sems.at[g]))
    return copies


def first_step_kernel(
    turned_hbm, courant_ref, vertical_ref, mixed_hbm, upper_ref, lower_ref, upper_mix_ref, lower_mix_ref,
    turned, mixed_out, in_sems, out_sems,
):
    coming = start_all(groups(turned_hbm, turned, in_sems))
    going = groups(mixed_hbm, mixed_out, out_sems, out=True)
    cells, height = turned.shape[0], turned.shape[1]
    top, low = height // 2 - 1, height - 1
    lateral = lateral_matrix(turned.shape[2])
    vertical = without_forced(vertical_ref[...])
    courant = courant_ref[...]

    def body(x):
        updated = stencil(turned[x - 1], turned[x], turned[x + 1], lateral, courant)
        upper_ref[x : x + 1, :] = updated[top : top + 1]
        lower_ref[x : x + 1, :] = updated[low : low + 1]
        mixed = jnp.dot(vertical, updated.astype(BF16), preferred_element_type=F32)
        upper_mix_ref[x : x + 1, :] = mixed[top : top + 1]
        lower_mix_ref[x : x + 1, :] = mixed[low : low + 1]
        mixed_out[x] = mixed.astype(BF16)

    for x in (0, cells - 1):
        mixed_out[x] = jnp.zeros_like(mixed_out[x])
        for ref in (upper_ref, lower_ref, upper_mix_ref, lower_mix_ref):
            ref[x : x + 1, :] = jnp.zeros_like(ref[x : x + 1, :])
    coming[0].wait()
    for g in range(cells // GROUP):
        if g + 1 < len(coming):
            coming[g + 1].wait()
        for x in range(max(1, g * GROUP), min(cells - 1, (g + 1) * GROUP)):
            body(x)
        going[g].start()
    wait_all(going)


def first_edges_kernel(
    odd_ref, within_ref, across_ref, own_ref, courant_ref, vertical_ref, _, __,
    mixed_ref, upper_ref, lower_ref, upper_mix_ref, lower_mix_ref,
):
    height = own_ref.shape[2]
    top, low = height // 2 - 1, height - 1
    lateral = lateral_matrix(own_ref.shape[3])
    vertical = without_forced(vertical_ref[...])
    courant = courant_ref[...]
    left, right = sides(odd_ref, within_ref[...], across_ref[...])
    first, last = sides(odd_ref, own_ref[0], own_ref[1])
    for ref in (upper_ref, lower_ref, upper_mix_ref, lower_mix_ref):
        ref[...] = jnp.zeros_like(ref)
    before = [left[0], left[1], first[0], first[1]]
    after = [last[0], last[1], right[0], right[1]]
    for i, columns_of in enumerate((before[:3], before[1:], after[:3], after[1:])):
        updated = stencil(*columns_of, lateral, courant)
        upper_ref[i : i + 1, :] = updated[top : top + 1]
        lower_ref[i : i + 1, :] = updated[low : low + 1]
        mixed = jnp.dot(vertical, updated.astype(BF16), preferred_element_type=F32)
        upper_mix_ref[i : i + 1, :] = mixed[top : top + 1]
        lower_mix_ref[i : i + 1, :] = mixed[low : low + 1]
        mixed_ref[i] = mixed.astype(BF16)


def with_edges(main, edges):
    cells = main.shape[0]
    at = iota(main.shape, 0)
    return jnp.where(at == 0, edges[1:2], jnp.where(at == cells - 1, edges[2:3], main))


def ocean_kernel(
    odd_ref, ocean_ref, within_ref, across_ref, sea_ref, flux_ref, vertical_ref, out_ref
):
    cells, width = sea_ref.shape
    height = ocean_ref.shape[0] // cells
    vertical = vertical_ref[...]
    high = vertical.astype(BF16)
    low = (vertical - high.astype(F32)).astype(BF16)
    both = jnp.concatenate([high, low], axis=0)
    left, right = sides(odd_ref, within_ref[...], across_ref[...])
    lane = iota((height, width), 1)
    row = iota((height, width), 0)

    def column(x):
        if x < 0:
            return left
        if x >= cells:
            return right
        return ocean_ref[pl.ds(x, height, stride=cells), :]

    parts = []
    for x in range(cells):
        west, center, east = column(x - 1), column(x), column(x + 1)
        north = jnp.where(lane == width - 1, center, pltpu.roll(center, width - 1, 1))
        south = jnp.where(lane == 0, center, pltpu.roll(center, 1, 1))
        wet = sea_ref[x : x + 1, :].astype(F32)
        near = east + west + (north + south) - 4.0 * center
        heat = FLUX_GAIN * wet * flux_ref[0, x : x + 1, :]
        fresh = FLUX_GAIN * wet * flux_ref[1, x : x + 1, :]
        added = jnp.where(row == 0, heat, jnp.where(row == height // 2, fresh, 0.0))
        updated = (center + OCEAN_DIFFUSION * near) * wet + added
        upper = updated.astype(BF16)
        rest = (updated - upper.astype(F32)).astype(BF16)
        parts.append((upper, rest))
        if x % 2 == 0:
            continue
        upper, rest = (jnp.concatenate(p, axis=1) for p in zip(*parts))
        parts = []
        mixed = jnp.dot(both, upper, preferred_element_type=F32)
        mixed = mixed[:height] + mixed[height:]
        mixed += jnp.dot(high, rest, preferred_element_type=F32)
        out_ref[pl.ds(x - 1, height, stride=cells), :] = mixed[:, :width]
        out_ref[pl.ds(x, height, stride=cells), :] = mixed[:, width:]


PARTS = 8


def weight_copies(weight_hbm, held, sems):
    step = weight_hbm.shape[0] // PARTS
    return start_all([
        pltpu.make_async_copy(
            weight_hbm.at[pl.ds(i * step, step)], held.at[pl.ds(i * step, step)], sems.at[i]
        )
        for i in range(PARTS)
    ])


def pull_kernel(
    odd_ref, head_ref, owner_ref, block_ref, weight_hbm, sea_ref,
    upper_ref, lower_ref, upper_edge_ref, lower_edge_ref,
    temp_ref, heat_ref, moist_ref, upper_forced_ref, lower_forced_ref, send_ref, slots_ref,
    slot_rows, by_block, held, sems,
):
    copies = weight_copies(weight_hbm, held, sems)
    devices = head_ref.shape[0]
    surface = head_ref[:, 0:16, :].reshape(devices * 16, 128)
    slot_rows[...] = head_ref[:, 16:24, :].astype(F32).reshape(devices * 8, 128)
    slots_ref[...] = jnp.transpose(slot_rows[pl.ds(0, devices, stride=8), :])[:8]
    sources, blocks = owner_ref.shape
    goal = (columns(owner_ref) * 16 + columns(block_ref))[:, :1]
    pick = (goal == iota((blocks * sources, devices * 16), 1)).astype(F32).astype(BF16)
    fetched = jnp.dot(pick, surface, preferred_element_type=F32)
    wanted = jnp.concatenate(
        [jnp.transpose(fetched[k * blocks : (k + 1) * blocks]) for k in range(sources)], axis=0
    ).astype(BF16)
    lane = iota((128, blocks), 1)

    def add(j, total):
        rows = jnp.concatenate([held[j, k] for k in range(sources)], axis=1)
        product = jnp.dot(rows, wanted, preferred_element_type=F32)
        return jnp.where(lane == j, product, total)

    total = jnp.zeros((128, blocks), F32)
    step = blocks // PARTS
    for i, c in enumerate(copies):
        c.wait()
        for j in range(i * step, (i + 1) * step):
            total = add(j, total)
    by_block[...] = jnp.transpose(total)
    half = blocks // 2
    temp = jnp.concatenate(
        [by_block[pl.ds(h, half, stride=2), :] for h in range(2)], axis=1
    )
    temp_ref[...] = temp
    exchange = EXCHANGE_RATE * sea_ref[...].astype(F32)
    upper = with_edges(upper_ref[...], upper_edge_ref[...])
    lower = with_edges(lower_ref[...], lower_edge_ref[...])
    heat, moist = exchange * (temp - upper), exchange * (0.5 * temp - lower)
    heat_ref[...] = heat
    moist_ref[...] = moist
    upper = (upper + heat).astype(BF16).astype(F32)
    lower = (lower + moist).astype(BF16).astype(F32)
    upper_forced_ref[...] = upper
    lower_forced_ref[...] = lower
    two = iota((8, upper.shape[1]), 0) == 0
    first = jnp.where(two, upper[0:1], lower[0:1])
    last = jnp.where(two, upper[half - 1 : half], lower[half - 1 : half])
    send_ref[0], send_ref[1] = sides(odd_ref, first, last)


def push_kernel(
    odd_ref, place_ref, weight_hbm, sea_ref, temp_ref, heat_ref, moist_ref,
    upper_forced_ref, lower_forced_ref, upper_mix_ref, lower_mix_ref,
    upper_mix_edge_ref, lower_mix_edge_ref, within_ref, across_ref,
    courant_ref, vertical_ref, out_ref,
    flux_rows, shares, held, sems,
):
    copies = weight_copies(weight_hbm, held, sems)
    height = vertical_ref.shape[0]
    top, low = height // 2 - 1, height - 1
    cells, width = sea_ref.shape
    sub, lane = iota((cells, width), 0), iota((cells, width), 1)

    left_forced, right_forced = sides(odd_ref, within_ref[...], across_ref[...])

    def row_of(r, mix, upper, lower):
        a = vertical_ref[pl.ds(r - 7, 8), :].astype(F32)[7:8]
        kept = mix.astype(BF16).astype(F32)
        return (kept + a[:, top : top + 1] * upper + a[:, low : low + 1] * lower).astype(BF16).astype(F32)

    def updated(r, mix_ref, edge_ref):
        edges = edge_ref[...]
        center = row_of(
            r, with_edges(mix_ref[...], edges), upper_forced_ref[...], lower_forced_ref[...]
        )
        before = row_of(r, edges[0:1], left_forced[0:1], left_forced[1:2])
        after = row_of(r, edges[3:4], right_forced[0:1], right_forced[1:2])
        west = jnp.where(sub == 0, before, pltpu.roll(center, 1, 0))
        east = jnp.where(sub == cells - 1, after, pltpu.roll(center, cells - 1, 0))
        north = jnp.where(lane == width - 1, center, pltpu.roll(center, width - 1, 1))
        south = jnp.where(lane == 0, center, pltpu.roll(center, 1, 1))
        near = east + west + (north + south) - 4.0 * center
        courant = courant_ref[pl.ds(r - 7, 8), :][7:8]
        return center - courant * (center - west) + ATM_DIFFUSION * near

    exchange = EXCHANGE_RATE * sea_ref[...].astype(F32)
    temp = temp_ref[...]
    heat = 0.5 * heat_ref[...] + 0.5 * (
        exchange * (temp - updated(top, upper_mix_ref, upper_mix_edge_ref))
    )
    moist = 0.5 * moist_ref[...] + 0.5 * (
        exchange * (0.5 * temp - updated(low, lower_mix_ref, lower_mix_edge_ref))
    )
    flux_rows[...] = jnp.zeros_like(flux_rows)
    for v, flux in enumerate((heat, moist)):
        for h in range(2):
            flux_rows[pl.ds(h * 8 + v, cells, stride=16), :] = flux[:, h * 128 : (h + 1) * 128]
    blocks, sources = held.shape[0], held.shape[1]
    step = blocks // PARTS
    for i, c in enumerate(copies):
        c.wait()
        for j in range(i * step, (i + 1) * step):
            rows = flux_rows[j * 8 : (j + 1) * 8, :].astype(BF16)
            for k in range(sources):
                got = jnp.dot(rows, held[j, k], preferred_element_type=F32)
                at = (k * blocks + j) * 8
                shares[at : at + 8, :] = got

    pairs = blocks * sources
    place = place_ref[0:1, :]
    rows = iota((out_ref.shape[0], pairs), 0)
    total = jnp.zeros(out_ref.shape, F32)
    for v in range(2):
        pick = (rows == place + 4 * v).astype(F32).astype(BF16)
        share = shares[pl.ds(v, pairs, stride=8), :].astype(BF16)
        total += jnp.dot(pick, share, preferred_element_type=F32)
    out_ref[...] = total.astype(BF16)


def second_step_kernel(
    odd_ref, mixed_hbm, edge_ref, courant_ref, vertical_ref, sea_ref, temp_ref,
    upper_forced_ref, lower_forced_ref, within_ref, across_ref,
    out_hbm, mixed_ref, state, result, out_ref, in_sems, out_sems,
):
    coming = start_all(groups(mixed_hbm, mixed_ref, in_sems))
    cells, height = mixed_ref.shape[0], mixed_ref.shape[1]
    top, low = height // 2 - 1, height - 1
    lateral = lateral_matrix(mixed_ref.shape[2])
    vertical = vertical_ref[...]
    upper_column = vertical[:, top : top + 1].astype(F32)
    lower_column = vertical[:, low : low + 1].astype(F32)
    courant = courant_ref[...]

    def complete(mixed, upper, lower):
        return (mixed.astype(F32) + upper_column * upper + lower_column * lower).astype(BF16)

    left, right = sides(odd_ref, within_ref[...], across_ref[...])
    state[0] = complete(edge_ref[0], left[0:1], left[1:2])
    state[1] = complete(edge_ref[1], upper_forced_ref[0:1, :], lower_forced_ref[0:1, :])
    state[cells] = complete(
        edge_ref[2], upper_forced_ref[cells - 1 : cells, :], lower_forced_ref[cells - 1 : cells, :]
    )
    state[cells + 1] = complete(edge_ref[3], right[0:1], right[1:2])

    for g, c in enumerate(coming):
        c.wait()
        for x in range(max(1, g * GROUP), min(cells - 1, (g + 1) * GROUP)):
            state[x + 1] = complete(
                mixed_ref[x], upper_forced_ref[x : x + 1, :], lower_forced_ref[x : x + 1, :]
            )

    last = iota((8, mixed_ref.shape[2]), 0) == 7

    @pl.loop(0, cells, unroll=GROUP)
    def _(x):
        updated = stencil(state[x], state[x + 1], state[x + 2], lateral, courant)
        exchange = EXCHANGE_RATE * sea_ref[pl.ds(x, 1), :].astype(F32)
        temp = temp_ref[pl.ds(x, 1), :]
        upper = updated[top - 7 : top + 1]
        lower = updated[low - 7 : low + 1]
        upper = jnp.where(last, upper + exchange * (temp - upper), upper)
        lower = jnp.where(last, lower + exchange * (0.5 * temp - lower), lower)
        forced = jnp.concatenate(
            [updated[: top - 7], upper, updated[top + 1 : low - 7], lower], axis=0
        ).astype(BF16)
        result[x] = jnp.dot(vertical, forced, preferred_element_type=F32).astype(BF16)

    step = 32
    going = []
    for i in range(height // step):
        at = pl.ds(i * step, step)
        out_ref[at] = jnp.swapaxes(result[:, i * step : (i + 1) * step, :], 0, 1)
        going.append(pltpu.make_async_copy(out_ref.at[at], out_hbm.at[at], out_sems.at[i]))
        going[-1].start()
    wait_all(going)


def land_kernel(incoming_ref, slots_ref, sea_ref, out_ref, wide):
    devices = slots_ref.shape[1]
    cells = sea_ref.shape[0]
    wide[...] = incoming_ref[...].astype(F32)
    wet = sea_ref[...].astype(F32)
    here = (iota((cells, devices), 0) + 1).astype(F32)
    picks = [(slots_ref[s : s + 1, :] == here).astype(F32).astype(BF16) for s in range(4)]
    for v in range(2):
        total = jnp.zeros((cells, 128), F32)
        for s in range(4):
            part = wide[pl.ds(v * 4 + s, devices, stride=8), :].astype(BF16)
            total += jnp.dot(picks[s], part, preferred_element_type=F32)
        out_ref[v] = total * wet


def swap(within, across):
    peers = lax.axis_size(BOTH)
    pair = [(i, i ^ 1) for i in range(peers)]
    other = [(i, ((i + 1) ^ 1) - 1) for i in range(peers)]
    other = [(i, j % peers) for i, j in other]
    return lax.ppermute(within, BOTH, pair), lax.ppermute(across, BOTH, other)


def per_device(
    atm_state, atm_sea, zonal_courant, atm_vertical, ocean_state, ocean_sea,
    flux_in, ocean_vertical, remap_owner, remap_block, remap_weight,
):
    devices = lax.axis_size(BOTH)
    height, cells, width = atm_state.shape
    blocks, sources = remap_owner.shape
    pairs = blocks * sources
    courant = zonal_courant.reshape(height, 1)
    layers, ocean_cells, ocean_width = ocean_state.shape
    ocean_rows = ocean_state.reshape(layers * ocean_cells, ocean_width)
    owner, block = remap_owner.T, remap_block.T
    odd = is_odd()
    dma = pltpu.SemaphoreType.DMA
    held = [pltpu.VMEM(remap_weight.shape, BF16), dma((PARTS,))]
    whole = pltpu.VMEM((cells, height, width), BF16)
    levels = 64

    head, place = call(
        plan_kernel,
        (shape((devices, HEAD, 128), BF16), shape((8, pairs), jnp.int32)),
        owner, block, ocean_state,
        specs={0: ANY, 1: ANY, 2: ANY},
        scratch=[
            pltpu.VMEM((devices * 8, 128), F32),
            pltpu.VMEM(owner.shape, jnp.int32),
            pltpu.VMEM(owner.shape, jnp.int32),
            pltpu.VMEM((ocean_cells, ocean_width), F32),
            dma((3,)),
        ],
        limit=58,
        touched=1 << 20,
    )
    gathered = lax.all_to_all(head, BOTH, split_axis=0, concat_axis=0, tiled=True)

    turned, send, ocean_send = call(
        turn_kernel,
        (
            shape((cells, height, width), BF16),
            shape((2, 2, height, width), BF16),
            shape((2, layers, ocean_width), F32),
        ),
        odd, atm_state, ocean_state,
        specs={0: SCALAR, 1: pl.BlockSpec((levels, cells, width), lambda i: (i, 0, 0)), 2: ANY},
        out_specs={
            0: pl.BlockSpec((cells, levels, width), lambda i: (0, i, 0)),
            1: pl.BlockSpec((2, 2, height, width), lambda i: (0, 0, 0, 0)),
            2: pl.BlockSpec((2, layers, ocean_width), lambda i: (0, 0, 0)),
        },
        scratch=[dma((2,))],
        grid=(height // levels,),
        limit=54,
        touched=12 << 20,
    )
    near = swap(send[0], send[1])
    ocean_near = swap(ocean_send[0], ocean_send[1])
    row, small = shape((cells, width), F32), shape((8, width), F32)
    mixed, upper, lower, upper_mix, lower_mix = call(
        first_step_kernel,
        (shape((cells, height, width), BF16), row, row, row, row),
        turned, courant, atm_vertical,
        specs={0: ANY},
        out_specs={0: ANY},
        scratch=[whole, whole, dma((cells // GROUP,)), dma((cells // GROUP,))],
        touched=16 << 20,
    )
    mixed_edge, upper_edge, lower_edge, upper_mix_edge, lower_mix_edge = call(
        first_edges_kernel,
        (shape((4, height, width), BF16), small, small, small, small),
        odd, *near, send, courant, atm_vertical, *ocean_near,
        specs={0: SCALAR},
        touched=2 << 20,
    )

    temp, heat, moist, upper_forced, lower_forced, forced_send, slots = call(
        pull_kernel,
        (row, row, row, row, row, shape((2, 8, width), F32), shape((8, devices), F32)),
        odd, gathered, owner, block, remap_weight, atm_sea, upper, lower, upper_edge, lower_edge,
        specs={0: SCALAR, 4: ANY},
        scratch=[pltpu.VMEM((devices * 8, 128), F32), pltpu.VMEM((blocks, 128), F32), *held],
        touched=12 << 20,
    )
    forced_near = swap(forced_send[0], forced_send[1])
    outgoing = call(
        push_kernel,
        shape((devices * 8, 128), BF16),
        odd, place, remap_weight, atm_sea, temp, heat, moist,
        upper_forced, lower_forced, upper_mix, lower_mix, upper_mix_edge, lower_mix_edge,
        *forced_near, courant, atm_vertical,
        specs={0: SCALAR, 2: ANY},
        scratch=[pltpu.VMEM((blocks * 8, 128), F32), pltpu.VMEM((pairs * 8, 128), F32), *held],
        touched=12 << 20,
    )
    incoming = lax.all_to_all(
        outgoing.reshape(devices, 8, 128), BOTH, split_axis=0, concat_axis=0, tiled=True
    )
    state = call(
        second_step_kernel,
        shape(atm_state.shape, BF16),
        odd, mixed, mixed_edge, courant, atm_vertical, atm_sea, temp,
        upper_forced, lower_forced, *forced_near,
        specs={0: SCALAR, 1: ANY},
        out_specs={0: ANY},
        scratch=[
            whole,
            pltpu.VMEM((cells + 2, height, width), BF16),
            whole,
            pltpu.VMEM(atm_state.shape, BF16),
            dma((cells // GROUP,)),
            dma((height // 32,)),
        ],
        touched=24 << 20,
    )
    new_ocean = call(
        ocean_kernel,
        shape(ocean_rows.shape, F32),
        odd, ocean_rows, *ocean_near, ocean_sea, flux_in, ocean_vertical,
        specs={0: SCALAR},
        touched=8 << 20,
    )
    ocean_flux = call(
        land_kernel,
        shape((2, ocean_cells, ocean_width), F32),
        incoming.reshape(devices * 8, 128), slots, ocean_sea,
        scratch=[pltpu.VMEM((devices * 8, 128), F32)],
        touched=1 << 20,
    )
    return state, new_ocean.reshape(ocean_state.shape), ocean_flux


def solution(mesh):
    return jax.shard_map(
        per_device,
        mesh=mesh,
        in_specs=(
            P(None, BOTH, None), P(BOTH, None), P(), P(), P(None, BOTH, None), P(BOTH, None),
            P(None, BOTH, None), P(), P(BOTH, None), P(BOTH, None), P(BOTH, None, None, None),
        ),
        out_specs=(P(None, BOTH, None), P(None, BOTH, None), P(None, BOTH, None)),
        check_vma=False,
    )
```

```python
import functools

import jax
import jax.numpy as jnp
from jax import lax
from jax.experimental import pallas as pl
from jax.experimental.pallas import tpu as pltpu
from jax.sharding import PartitionSpec as P

ATM_DIFFUSION = 0.1
OCEAN_DIFFUSION = 0.15
EXCHANGE_RATE = 0.3
FLUX_GAIN = 0.5

F32 = jnp.float32
BF16 = jnp.bfloat16
VM = pltpu.VMEM
BOTH = ("comp", "tile")
HEAD = 24


def call(kernel, outs, *args, scratch=(), specs=None, out_specs=None, limit=50, touched=0, grid=()):
    specs, out_specs = specs or {}, out_specs or {}
    single = not isinstance(outs, tuple)
    placed = [
        out_specs.get(i, pl.BlockSpec(memory_space=VM)) for i in range(1 if single else len(outs))
    ]
    return pl.pallas_call(
        kernel,
        out_shape=outs,
        grid=grid,
        in_specs=[specs.get(i, pl.BlockSpec(memory_space=VM)) for i in range(len(args))],
        out_specs=placed[0] if single else tuple(placed),
        scratch_shapes=list(scratch),
        compiler_params=pltpu.CompilerParams(vmem_limit_bytes=limit << 20),
        cost_estimate=pl.CostEstimate(flops=0, bytes_accessed=touched, transcendentals=0),
    )(*args)


SCALAR = pl.BlockSpec(memory_space=pltpu.SMEM)
ANY = pl.BlockSpec(memory_space=pltpu.HBM)


def start_all(copies):
    for c in copies:
        c.start()
    return copies


def wait_all(copies):
    for c in copies:
        c.wait()


def shape(dims, dtype):
    return jax.ShapeDtypeStruct(dims, dtype)


def iota(dims, axis):
    return lax.broadcasted_iota(jnp.int32, dims, axis)


def columns(ref):
    count, rows = ref.shape
    wide = [jnp.broadcast_to(ref[k : k + 1, :], (128, rows)) for k in range(count)]
    return jnp.concatenate([jnp.transpose(w) for w in wide], axis=0)


def is_odd():
    return jnp.bitwise_and(lax.axis_index("tile"), 1).astype(jnp.int32).reshape(1)


def plan_kernel(
    owner_hbm, block_hbm, ocean_hbm, head_ref, place_ref, slot_rows, places, owner_ref, block_ref, surface_ref, sems
):
    copies = start_all([
        pltpu.make_async_copy(owner_hbm, owner_ref, sems.at[0]),
        pltpu.make_async_copy(block_hbm, block_ref, sems.at[1]),
        pltpu.make_async_copy(ocean_hbm.at[0], surface_ref, sems.at[2]),
    ])
    devices = head_ref.shape[0]
    slot_rows[...] = jnp.zeros_like(slot_rows)
    wait_all(copies)
    owner, block = columns(owner_ref), columns(block_ref)
    pairs = owner.shape[0]
    hits = (owner == iota((pairs, devices), 1)).astype(F32)
    earlier = (iota((pairs, pairs), 1) < iota((pairs, pairs), 0)).astype(F32)
    before = jnp.dot(earlier.astype(BF16), hits.astype(BF16), preferred_element_type=F32)
    slot = jnp.sum(before * hits, axis=1, keepdims=True)
    marked = jnp.where(
        slot == iota((pairs, 128), 1).astype(F32), (block + 1).astype(F32), 0.0
    )
    wanted = jnp.dot(
        jnp.transpose(hits).astype(BF16), marked.astype(BF16), preferred_element_type=F32
    )
    places[...] = owner.astype(F32) * 8.0 + slot
    spread = jnp.transpose(
        jnp.concatenate([places[pl.ds(h, pairs // 2, stride=2), :] for h in range(2)], axis=0)
    )
    place_ref[...] = spread[:8].astype(jnp.int32)
    slot_rows[pl.ds(0, devices, stride=8), :] = wanted
    surface = surface_ref[...].astype(BF16)
    head_ref[:, 0:16, :] = jnp.broadcast_to(surface[None], (devices, 16, 128))
    head_ref[:, 16:24, :] = slot_rows[...].reshape(devices, 8, 128).astype(BF16)


def edges_kernel(
    odd_ref, state_ref, ocean_hbm, weight_hbm, owner_ref, block_ref, sea_ref,
    state_a_ref, state_b_ref, weight_a_hbm, weight_b_hbm, pack_a_ref, pack_b_ref,
    ocean_first, ocean_last, sems,
):
    i, odd = pl.program_id(0), odd_ref[0]
    blocks = weight_hbm.shape[0]
    at_a = (1 - odd) * (blocks - 2)
    copies = [
        pltpu.make_async_copy(weight_hbm.at[pl.ds(at_a, 2)], weight_a_hbm, sems.at[0]),
        pltpu.make_async_copy(weight_hbm.at[pl.ds(blocks - 2 - at_a, 2)], weight_b_hbm, sems.at[1]),
        pltpu.make_async_copy(ocean_hbm.at[:, 0], ocean_first, sems.at[2]),
        pltpu.make_async_copy(ocean_hbm.at[:, ocean_hbm.shape[1] - 1], ocean_last, sems.at[3]),
    ]
    pl.when(i == 0)(lambda: (start_all(copies), None)[1])
    rows, cells = state_ref.shape[0], state_ref.shape[1]
    first = jnp.swapaxes(state_ref[:, 0:8, :], 0, 1)[0:2]
    last = jnp.swapaxes(state_ref[:, cells - 8 : cells, :], 0, 1)[6:8]
    at = pl.ds(pl.multiple_of(i * rows, rows), rows)
    state_a_ref[:, at, :], state_b_ref[:, at, :] = sides(odd_ref, first, last)

    @pl.when(i == pl.num_programs(0) - 1)
    def _():
        layers = ocean_first.shape[0]
        goal = (owner_ref[...] * 16 + block_ref[...]).astype(F32)
        sea = sea_ref[...].astype(F32)
        width = sea.shape[1] // 2
        wait_all(copies)
        ends = [ocean_first[...], ocean_last[...]], [sea[0:1], sea[cells - 1 : cells]]
        for ref, ocean, line in zip(
            (pack_a_ref, pack_b_ref), sides(odd_ref, *ends[0]), sides(odd_ref, *ends[1])
        ):
            ref[0:layers, :] = ocean
            ref[layers:, :] = jnp.zeros_like(ref[layers:, :])
            for h in range(2):
                ref[layers + h : layers + h + 1, :] = line[:, h * width : (h + 1) * width]
            ref[layers + 8 : layers + 8 + goal.shape[0], 0 : goal.shape[1]] = goal


def sides(odd_ref, within, across):
    odd = odd_ref[0] == 1
    return jnp.where(odd, within, across), jnp.where(odd, across, within)


def lateral_matrix(size):
    row, col = iota((size, size), 0), iota((size, size), 1)
    near = jnp.where(jnp.abs(row - col) == 1, 1.0, 0.0)
    edge = jnp.where((row == 0) | (row == size - 1), -3.0, -4.0)
    return (near + jnp.where(row == col, edge, 0.0)).astype(BF16)


def without_forced(vertical):
    height = vertical.shape[0]
    col = iota(vertical.shape, 1)
    keep = (col != height // 2 - 1) & (col != height - 1)
    return jnp.where(keep, vertical.astype(F32), 0.0).astype(BF16)


def stencil(west, center, east, lateral, courant):
    w, c, e = west.astype(F32), center.astype(F32), east.astype(F32)
    side = jnp.dot(center, lateral, preferred_element_type=F32)
    return c + courant * (w - c) + ATM_DIFFUSION * (w + e + side)


GROUP = 8
LEVEL_PARTS = 4


def groups(hbm, held, sems, out=False):
    copies = []
    for g in range(held.shape[0] // GROUP):
        at = pl.ds(g * GROUP, GROUP)
        ends = (held.at[at], hbm.at[at]) if out else (hbm.at[at], held.at[at])
        copies.append(pltpu.make_async_copy(*ends, sems.at[g]))
    return copies


def keep_rows(ref, x, updated, mixed):
    height = updated.shape[0]
    for n, (field, r) in enumerate(
        ((updated, height // 2), (updated, height), (mixed, height // 2), (mixed, height))
    ):
        ref[n, x : x + 1, :] = field[r - 1 : r]


def first_step_kernel(
    state_hbm, courant_ref, vertical_ref, mixed_hbm, rows_ref, state, turned, mixed_out, in_sems, out_sems,
):
    levels = state.shape[0] // LEVEL_PARTS
    coming = start_all([
        pltpu.make_async_copy(
            state_hbm.at[pl.ds(n * levels, levels)], state.at[pl.ds(n * levels, levels)], in_sems.at[n]
        )
        for n in range(LEVEL_PARTS)
    ])
    going = groups(mixed_hbm, mixed_out, out_sems, out=True)
    cells, height = turned.shape[0], turned.shape[1]
    lateral = lateral_matrix(turned.shape[2])
    vertical = without_forced(vertical_ref[...])
    courant = courant_ref[...]

    def body(x):
        updated = stencil(turned[x - 1], turned[x], turned[x + 1], lateral, courant)
        mixed = jnp.dot(vertical, updated.astype(BF16), preferred_element_type=F32)
        keep_rows(rows_ref, x, updated, mixed)
        mixed_out[x] = mixed.astype(BF16)

    for x in (0, cells - 1):
        mixed_out[x] = jnp.zeros_like(mixed_out[x])
        rows_ref[:, x : x + 1, :] = jnp.zeros_like(rows_ref[:, x : x + 1, :])
    step = 32
    for n, c in enumerate(coming):
        c.wait()
        for at in range(n * levels, (n + 1) * levels, step):
            turned[:, at : at + step, :] = jnp.swapaxes(state[at : at + step], 0, 1)
    for g in range(cells // GROUP):
        for x in range(max(1, g * GROUP), min(cells - 1, (g + 1) * GROUP)):
            body(x)
        going[g].start()
    wait_all(going)


def first_edges_kernel(
    odd_ref, within_ref, across_ref, own_a_ref, own_b_ref, courant_ref, vertical_ref, _, __,
    mixed_hbm, rows_ref, mixed_out, sem,
):
    height = own_a_ref.shape[1]
    lateral = lateral_matrix(own_a_ref.shape[2])
    vertical = without_forced(vertical_ref[...])
    courant = courant_ref[...]
    left, right = sides(odd_ref, within_ref[...], across_ref[...])
    first, last = sides(odd_ref, own_a_ref[...], own_b_ref[...])
    rows_ref[...] = jnp.zeros_like(rows_ref)
    before = [left[0], left[1], first[0], first[1]]
    after = [last[0], last[1], right[0], right[1]]
    for i, columns_of in enumerate((before[:3], before[1:], after[:3], after[1:])):
        updated = stencil(*columns_of, lateral, courant)
        mixed = jnp.dot(vertical, updated.astype(BF16), preferred_element_type=F32)
        keep_rows(rows_ref, i, updated, mixed)
        mixed_out[i] = mixed.astype(BF16)
    copy = pltpu.make_async_copy(mixed_out, mixed_hbm, sem)
    copy.start()
    copy.wait()


def with_edges(main, edges):
    cells = main.shape[0]
    at = iota(main.shape, 0)
    return jnp.where(at == 0, edges[1:2], jnp.where(at == cells - 1, edges[2:3], main))


def ocean_kernel(
    odd_ref, ocean_hbm, within_ref, across_ref, sea_ref, flux_ref, vertical_ref, out_hbm,
    ocean_ref, out_ref, sem,
):
    copy = pltpu.make_async_copy(ocean_hbm, ocean_ref, sem)
    copy.start()
    cells, width = sea_ref.shape
    height = ocean_ref.shape[0] // cells
    vertical = vertical_ref[...]
    high = vertical.astype(BF16)
    low = (vertical - high.astype(F32)).astype(BF16)
    both = jnp.concatenate([high, low], axis=0)
    left, right = sides(odd_ref, within_ref[0:height, :], across_ref[0:height, :])
    lane = iota((height, width), 1)
    row = iota((height, width), 0)

    copy.wait()

    def column(x):
        if x < 0:
            return left
        if x >= cells:
            return right
        return ocean_ref[pl.ds(x, height, stride=cells), :]

    parts = []
    for x in range(cells):
        west, center, east = column(x - 1), column(x), column(x + 1)
        north = jnp.where(lane == width - 1, center, pltpu.roll(center, width - 1, 1))
        south = jnp.where(lane == 0, center, pltpu.roll(center, 1, 1))
        wet = sea_ref[x : x + 1, :].astype(F32)
        near = east + west + (north + south) - 4.0 * center
        heat = FLUX_GAIN * wet * flux_ref[0, x : x + 1, :]
        fresh = FLUX_GAIN * wet * flux_ref[1, x : x + 1, :]
        added = jnp.where(row == 0, heat, jnp.where(row == height // 2, fresh, 0.0))
        updated = (center + OCEAN_DIFFUSION * near) * wet + added
        upper = updated.astype(BF16)
        rest = (updated - upper.astype(F32)).astype(BF16)
        parts.append((upper, rest))
        if x % 2 == 0:
            continue
        upper, rest = (jnp.concatenate(p, axis=1) for p in zip(*parts))
        parts = []
        mixed = jnp.dot(both, upper, preferred_element_type=F32)
        mixed = mixed[:height] + mixed[height:]
        mixed += jnp.dot(high, rest, preferred_element_type=F32)
        out_ref[pl.ds(x - 1, height, stride=cells), :] = mixed[:, :width]
        out_ref[pl.ds(x, height, stride=cells), :] = mixed[:, width:]
    copy = pltpu.make_async_copy(out_ref, out_hbm, sem)
    copy.start()
    copy.wait()


PARTS = 8


def weight_copies(weight_hbm, held, sems):
    step = weight_hbm.shape[0] // PARTS
    return start_all([
        pltpu.make_async_copy(
            weight_hbm.at[pl.ds(i * step, step)], held.at[pl.ds(i * step, step)], sems.at[i]
        )
        for i in range(PARTS)
    ])


def couple_kernel(
    odd_ref, head_ref, own_pack_ref, within_pack_ref, across_pack_ref,
    weight_hbm, within_weight_ref, across_weight_ref, sea_ref, place_ref,
    rows_ref, edges_ref, courant_ref, vertical_ref, coupled_ref, slots_ref, out_ref,
    slot_rows, by_block, flux_rows, shares, held, sems,
):
    copies = weight_copies(weight_hbm, held, sems)
    devices = head_ref.shape[0]
    blocks, sources = held.shape[0], held.shape[1]
    surface = head_ref[:, 0:16, :].reshape(devices * 16, 128)
    slot_rows[...] = head_ref[:, 16:24, :].astype(F32).reshape(devices * 8, 128)
    slots_ref[...] = jnp.transpose(slot_rows[pl.ds(0, devices, stride=8), :])[:8]

    layers = own_pack_ref.shape[0] - 16
    left_pack, right_pack = sides(
        odd_ref, within_pack_ref[layers:, :], across_pack_ref[layers:, :]
    )
    lane = iota((8, 128), 1)
    goals = jnp.where(
        lane < blocks,
        own_pack_ref[layers + 8 :, :],
        jnp.where(
            lane < blocks + 2,
            pltpu.roll(left_pack[8:], 2, 1),
            jnp.where(lane < blocks + 4, pltpu.roll(right_pack[8:], blocks + 2, 1), -1.0),
        ),
    )
    count = blocks + 8
    goal = jnp.concatenate(
        [
            jnp.transpose(jnp.broadcast_to(goals[k : k + 1], (128, 128)))[:count, :1]
            for k in range(sources)
        ],
        axis=0,
    ).astype(jnp.int32)
    pick = (goal == iota((sources * count, devices * 16), 1)).astype(F32).astype(BF16)
    fetched = jnp.dot(pick, surface, preferred_element_type=F32)
    empty = jnp.zeros((128 - count, 128), F32)
    wanted = jnp.concatenate(
        [
            jnp.transpose(jnp.concatenate([fetched[k * count : (k + 1) * count], empty], axis=0))
            for k in range(sources)
        ],
        axis=0,
    ).astype(BF16)
    lane = iota((128, 128), 1)

    def add(j, weights, total):
        rows = jnp.concatenate(weights, axis=1)
        return jnp.where(lane == j, jnp.dot(rows, wanted, preferred_element_type=F32), total)

    total = jnp.zeros((128, 128), F32)
    before, after = sides(odd_ref, within_weight_ref[...], across_weight_ref[...])
    for n, weights in enumerate((before[0], before[1], after[0], after[1])):
        total = add(blocks + n, [weights[k] for k in range(sources)], total)
    step = blocks // PARTS
    for i, c in enumerate(copies):
        c.wait()
        for j in range(i * step, (i + 1) * step):
            total = add(j, [held[j, k] for k in range(sources)], total)
    by_block[...] = jnp.transpose(total)

    half = blocks // 2
    temp = jnp.concatenate([by_block[pl.ds(h, half, stride=2), :] for h in range(2)], axis=1)
    coupled_ref[0:half, :] = temp
    exchange = EXCHANGE_RATE * sea_ref[...].astype(F32)
    upper = with_edges(rows_ref[0], edges_ref[0])
    lower = with_edges(rows_ref[1], edges_ref[1])
    heat, moist = exchange * (temp - upper), exchange * (0.5 * temp - lower)
    upper = (upper + heat).astype(BF16).astype(F32)
    lower = (lower + moist).astype(BF16).astype(F32)
    coupled_ref[half : 2 * half, :] = upper
    coupled_ref[2 * half : 3 * half, :] = lower
    halo = []
    for n, (edge, pack) in enumerate(((0, left_pack), (3, right_pack))):
        at = blocks + 2 * n
        warm = jnp.concatenate([by_block[at : at + 1, :], by_block[at + 1 : at + 2, :]], axis=1)
        rate = EXCHANGE_RATE * jnp.concatenate([pack[0:1], pack[1:2]], axis=1)
        u, w = edges_ref[0, edge : edge + 1, :], edges_ref[1, edge : edge + 1, :]
        halo.append((u + rate * (warm - u)).astype(BF16).astype(F32))
        halo.append((w + rate * (0.5 * warm - w)).astype(BF16).astype(F32))
    coupled_ref[3 * half :, :] = jnp.zeros_like(coupled_ref[3 * half :, :])
    for n, line in enumerate(halo):
        coupled_ref[3 * half + n : 3 * half + n + 1, :] = line

    height = vertical_ref.shape[0]
    top, low = height // 2 - 1, height - 1
    cells, width = sea_ref.shape
    sub, lane = iota((cells, width), 0), iota((cells, width), 1)

    def row_of(r, mix, upper, lower):
        a = vertical_ref[pl.ds(r - 7, 8), :].astype(F32)[7:8]
        kept = mix.astype(BF16).astype(F32)
        return (kept + a[:, top : top + 1] * upper + a[:, low : low + 1] * lower).astype(BF16).astype(F32)

    def updated(r, n):
        edges = edges_ref[n]
        center = row_of(r, with_edges(rows_ref[n], edges), upper, lower)
        left = row_of(r, edges[0:1], halo[0], halo[1])
        right = row_of(r, edges[3:4], halo[2], halo[3])
        west = jnp.where(sub == 0, left, pltpu.roll(center, 1, 0))
        east = jnp.where(sub == cells - 1, right, pltpu.roll(center, cells - 1, 0))
        north = jnp.where(lane == width - 1, center, pltpu.roll(center, width - 1, 1))
        south = jnp.where(lane == 0, center, pltpu.roll(center, 1, 1))
        near = east + west + (north + south) - 4.0 * center
        courant = courant_ref[pl.ds(r - 7, 8), :][7:8]
        return center - courant * (center - west) + ATM_DIFFUSION * near

    heat = 0.5 * heat + 0.5 * (exchange * (temp - updated(top, 2)))
    moist = 0.5 * moist + 0.5 * (
        exchange * (0.5 * temp - updated(low, 3))
    )
    flux_rows[...] = jnp.zeros_like(flux_rows)
    for v, flux in enumerate((heat, moist)):
        for h in range(2):
            flux_rows[pl.ds(h * 10 + v, cells, stride=16), :] = flux[:, h * 128 : (h + 1) * 128]
    for x in range(half):
        rows = jnp.concatenate(
            [flux_rows[(2 * x + h) * 8 : (2 * x + h + 1) * 8, :] for h in range(2)], axis=1
        ).astype(BF16)
        weights = jnp.concatenate(
            [
                jnp.concatenate([held[2 * x + h, k] for k in range(sources)], axis=1)
                for h in range(2)
            ],
            axis=0,
        )
        got = jnp.dot(rows, weights, preferred_element_type=F32)
        for k in range(sources):
            at = (k * half + x) * 8
            shares[at : at + 8, :] = got[:, k * 128 : (k + 1) * 128]

    pairs = blocks * sources
    place = place_ref[0:1, :]
    rows = iota((out_ref.shape[0], pairs), 0)
    total = jnp.zeros(out_ref.shape, F32)
    for v in range(2):
        pick = (rows == place + 4 * v).astype(F32).astype(BF16)
        share = jnp.concatenate(
            [shares[pl.ds(2 * h + v, pairs // 2, stride=8), :] for h in range(2)], axis=0
        ).astype(BF16)
        total += jnp.dot(pick, share, preferred_element_type=F32)
    out_ref[...] = total.astype(BF16)


def second_step_kernel(
    mixed_hbm, edge_hbm, courant_ref, vertical_ref, sea_ref, coupled_ref,
    out_hbm, mixed_ref, edge_ref, state, result, out_ref, in_sems, edge_sem, out_sems,
):
    edge_copy = pltpu.make_async_copy(edge_hbm, edge_ref, edge_sem)
    edge_copy.start()
    coming = start_all(groups(mixed_hbm, mixed_ref, in_sems))
    cells, height = mixed_ref.shape[0], mixed_ref.shape[1]
    top, low = height // 2 - 1, height - 1
    lateral = lateral_matrix(mixed_ref.shape[2])
    vertical = vertical_ref[...]
    upper_column = vertical[:, top : top + 1].astype(F32)
    lower_column = vertical[:, low : low + 1].astype(F32)
    courant = courant_ref[...]

    def complete(mixed, upper, lower):
        return (mixed.astype(F32) + upper_column * upper + lower_column * lower).astype(BF16)

    halo_ref = coupled_ref.at[3 * cells :]
    upper_forced_ref = coupled_ref.at[cells : 2 * cells]
    lower_forced_ref = coupled_ref.at[2 * cells : 3 * cells]
    edge_copy.wait()
    state[0] = complete(edge_ref[0], halo_ref[0:1, :], halo_ref[1:2, :])
    state[1] = complete(edge_ref[1], upper_forced_ref[0:1, :], lower_forced_ref[0:1, :])
    state[cells] = complete(
        edge_ref[2], upper_forced_ref[cells - 1 : cells, :], lower_forced_ref[cells - 1 : cells, :]
    )
    state[cells + 1] = complete(edge_ref[3], halo_ref[2:3, :], halo_ref[3:4, :])

    for g, c in enumerate(coming):
        c.wait()
        for x in range(max(1, g * GROUP), min(cells - 1, (g + 1) * GROUP)):
            state[x + 1] = complete(
                mixed_ref[x], upper_forced_ref[x : x + 1, :], lower_forced_ref[x : x + 1, :]
            )

    last = iota((8, mixed_ref.shape[2]), 0) == 7

    @pl.loop(0, cells, unroll=GROUP)
    def _(x):
        updated = stencil(state[x], state[x + 1], state[x + 2], lateral, courant)
        exchange = EXCHANGE_RATE * sea_ref[pl.ds(x, 1), :].astype(F32)
        temp = coupled_ref[pl.ds(x, 1), :]
        upper = updated[top - 7 : top + 1]
        lower = updated[low - 7 : low + 1]
        upper = jnp.where(last, upper + exchange * (temp - upper), upper)
        lower = jnp.where(last, lower + exchange * (0.5 * temp - lower), lower)
        forced = jnp.concatenate(
            [updated[: top - 7], upper, updated[top + 1 : low - 7], lower], axis=0
        ).astype(BF16)
        result[x] = jnp.dot(vertical, forced, preferred_element_type=F32).astype(BF16)

    step = 32
    going = []
    for i in range(height // step):
        at = pl.ds(i * step, step)
        out_ref[at] = jnp.swapaxes(result[:, i * step : (i + 1) * step, :], 0, 1)
        going.append(pltpu.make_async_copy(out_ref.at[at], out_hbm.at[at], out_sems.at[i]))
        going[-1].start()
    wait_all(going)


def land_kernel(incoming_ref, slots_ref, sea_ref, out_ref, wide):
    devices = slots_ref.shape[1]
    cells = sea_ref.shape[0]
    wide[...] = incoming_ref[...].astype(F32)
    wet = sea_ref[...].astype(F32)
    here = (iota((cells, devices), 0) + 1).astype(F32)
    picks = [(slots_ref[s : s + 1, :] == here).astype(F32).astype(BF16) for s in range(4)]
    for v in range(2):
        total = jnp.zeros((cells, 128), F32)
        for s in range(4):
            part = wide[pl.ds(v * 4 + s, devices, stride=8), :].astype(BF16)
            total += jnp.dot(picks[s], part, preferred_element_type=F32)
        out_ref[v] = total * wet


def swap(within, across):
    peers = lax.axis_size(BOTH)
    pair = [(i, i ^ 1) for i in range(peers)]
    other = [(i, ((i + 1) ^ 1) - 1) for i in range(peers)]
    other = [(i, j % peers) for i, j in other]
    return lax.ppermute(within, BOTH, pair), lax.ppermute(across, BOTH, other)


def per_device(
    atm_state, atm_sea, zonal_courant, atm_vertical, ocean_state, ocean_sea,
    flux_in, ocean_vertical, remap_owner, remap_block, remap_weight,
):
    devices = lax.axis_size(BOTH)
    height, cells, width = atm_state.shape
    blocks, sources = remap_owner.shape
    pairs = blocks * sources
    courant = zonal_courant.reshape(height, 1)
    layers, ocean_cells, ocean_width = ocean_state.shape
    ocean_rows = ocean_state.reshape(layers * ocean_cells, ocean_width)
    owner, block = remap_owner.T, remap_block.T
    odd = is_odd()
    dma = pltpu.SemaphoreType.DMA
    held = [pltpu.VMEM(remap_weight.shape, BF16), dma((PARTS,))]
    whole = pltpu.VMEM((cells, height, width), BF16)
    levels = 64

    head, place = call(
        plan_kernel,
        (shape((devices, HEAD, 128), BF16), shape((8, pairs), jnp.int32)),
        owner, block, ocean_state,
        specs={0: ANY, 1: ANY, 2: ANY},
        scratch=[
            pltpu.VMEM((devices * 8, 128), F32),
            pltpu.VMEM((pairs, 128), F32),
            pltpu.VMEM(owner.shape, jnp.int32),
            pltpu.VMEM(owner.shape, jnp.int32),
            pltpu.VMEM((ocean_cells, ocean_width), F32),
            dma((3,)),
        ],
        limit=58,
        touched=1 << 20,
    )
    gathered = lax.all_to_all(head, BOTH, split_axis=0, concat_axis=0, tiled=True)

    pair_of_columns = shape((2, height, width), BF16)
    pair_of_blocks = shape((2, *remap_weight.shape[1:]), BF16)
    pack = shape((layers + 16, ocean_width), F32)
    state_a, state_b, weight_a, weight_b, pack_a, pack_b = call(
        edges_kernel,
        (pair_of_columns, pair_of_columns, pair_of_blocks, pair_of_blocks, pack, pack),
        odd, atm_state, ocean_state, remap_weight, owner, block, atm_sea,
        specs={
            0: SCALAR,
            1: pl.BlockSpec((levels, cells, width), lambda i: (i, 0, 0)),
            2: ANY,
            3: ANY,
        },
        out_specs={2: ANY, 3: ANY},
        scratch=[pltpu.VMEM((layers, ocean_width), F32)] * 2 + [dma((4,))],
        grid=(height // levels,),
        limit=54,
        touched=6 << 20,
    )
    state_near = swap(state_a, state_b)
    pack_near = swap(pack_a, pack_b)
    weight_near = swap(weight_a, weight_b)
    mixed, rows = call(
        first_step_kernel,
        (shape((cells, height, width), BF16), shape((4, cells, width), F32)),
        atm_state, courant, atm_vertical,
        specs={0: ANY},
        out_specs={0: ANY},
        scratch=[
            pltpu.VMEM(atm_state.shape, BF16), whole, whole,
            dma((LEVEL_PARTS,)), dma((cells // GROUP,)),
        ],
        touched=16 << 20,
    )
    mixed_edge, edge_rows = call(
        first_edges_kernel,
        (shape((4, height, width), BF16), shape((4, 8, width), F32)),
        odd, *state_near, state_a, state_b, courant, atm_vertical, *pack_near,
        specs={0: SCALAR},
        out_specs={0: ANY},
        scratch=[pltpu.VMEM((4, height, width), BF16), dma],
        limit=50,
        touched=2 << 20,
    )

    coupled, slots, outgoing = call(
        couple_kernel,
        (
            shape((3 * cells + 8, width), F32),
            shape((8, devices), F32),
            shape((devices * 8, 128), BF16),
        ),
        odd, gathered, pack_a, *pack_near, remap_weight, *weight_near, atm_sea, place,
        rows, edge_rows, courant, atm_vertical,
        specs={0: SCALAR, 5: ANY},
        scratch=[
            pltpu.VMEM((devices * 8, 128), F32),
            pltpu.VMEM((128, 128), F32),
            pltpu.VMEM((blocks * 8, 128), F32),
            pltpu.VMEM((pairs * 4, 128), F32),
            *held,
        ],
        limit=50,
        touched=16 << 20,
    )
    incoming = lax.all_to_all(
        outgoing.reshape(devices, 8, 128), BOTH, split_axis=0, concat_axis=0, tiled=True
    )
    state = call(
        second_step_kernel,
        shape(atm_state.shape, BF16),
        mixed, mixed_edge, courant, atm_vertical, atm_sea, coupled,
        specs={0: ANY, 1: ANY},
        out_specs={0: ANY},
        scratch=[
            whole,
            pltpu.VMEM((4, height, width), BF16),
            pltpu.VMEM((cells + 2, height, width), BF16),
            whole,
            pltpu.VMEM(atm_state.shape, BF16),
            dma((cells // GROUP,)),
            dma,
            dma((height // 32,)),
        ],
        touched=24 << 20,
    )
    new_ocean = call(
        ocean_kernel,
        shape(ocean_rows.shape, F32),
        odd, ocean_rows, *pack_near, ocean_sea, flux_in, ocean_vertical,
        specs={0: SCALAR, 1: ANY},
        out_specs={0: ANY},
        scratch=[pltpu.VMEM(ocean_rows.shape, F32), pltpu.VMEM(ocean_rows.shape, F32), dma],
        limit=53,
        touched=8 << 20,
    )
    ocean_flux = call(
        land_kernel,
        shape((2, ocean_cells, ocean_width), F32),
        incoming.reshape(devices * 8, 128), slots, ocean_sea,
        scratch=[pltpu.VMEM((devices * 8, 128), F32)],
        touched=1 << 20,
    )
    return state, new_ocean.reshape(ocean_state.shape), ocean_flux


def solution(mesh):
    return jax.shard_map(
        per_device,
        mesh=mesh,
        in_specs=(
            P(None, BOTH, None), P(BOTH, None), P(), P(), P(None, BOTH, None), P(BOTH, None),
            P(None, BOTH, None), P(), P(BOTH, None), P(BOTH, None), P(BOTH, None, None, None),
        ),
        out_specs=(P(None, BOTH, None), P(None, BOTH, None), P(None, BOTH, None)),
        check_vma=False,
    )
```

```python
import functools

import jax
import jax.numpy as jnp
from jax import lax
from jax.experimental import pallas as pl
from jax.experimental.pallas import tpu as pltpu
from jax.sharding import PartitionSpec as P

ATM_DIFFUSION = 0.1
OCEAN_DIFFUSION = 0.15
EXCHANGE_RATE = 0.3
FLUX_GAIN = 0.5

F32 = jnp.float32
BF16 = jnp.bfloat16
VM = pltpu.VMEM
BOTH = ("comp", "tile")
HEAD = 24


def call(kernel, outs, *args, scratch=(), specs=None, out_specs=None, limit=50, touched=0, grid=()):
    specs, out_specs = specs or {}, out_specs or {}
    single = not isinstance(outs, tuple)
    placed = [
        out_specs.get(i, pl.BlockSpec(memory_space=VM)) for i in range(1 if single else len(outs))
    ]
    return pl.pallas_call(
        kernel,
        out_shape=outs,
        grid=grid,
        in_specs=[specs.get(i, pl.BlockSpec(memory_space=VM)) for i in range(len(args))],
        out_specs=placed[0] if single else tuple(placed),
        scratch_shapes=list(scratch),
        compiler_params=pltpu.CompilerParams(vmem_limit_bytes=limit << 20),
        cost_estimate=pl.CostEstimate(flops=0, bytes_accessed=touched, transcendentals=0),
    )(*args)


SCALAR = pl.BlockSpec(memory_space=pltpu.SMEM)
ANY = pl.BlockSpec(memory_space=pltpu.HBM)


def start_all(copies):
    for c in copies:
        c.start()
    return copies


def wait_all(copies):
    for c in copies:
        c.wait()


def shape(dims, dtype):
    return jax.ShapeDtypeStruct(dims, dtype)


def iota(dims, axis):
    return lax.broadcasted_iota(jnp.int32, dims, axis)


def columns(ref):
    count, rows = ref.shape
    wide = [jnp.broadcast_to(ref[k : k + 1, :], (128, rows)) for k in range(count)]
    return jnp.concatenate([jnp.transpose(w) for w in wide], axis=0)


def is_odd():
    return jnp.bitwise_and(lax.axis_index("tile"), 1).astype(jnp.int32).reshape(1)


def plan_kernel(
    owner_hbm, block_hbm, ocean_hbm, head_ref, place_ref, slot_rows, places, owner_ref, block_ref, surface_ref, sems
):
    copies = start_all([
        pltpu.make_async_copy(owner_hbm, owner_ref, sems.at[0]),
        pltpu.make_async_copy(block_hbm, block_ref, sems.at[1]),
        pltpu.make_async_copy(ocean_hbm.at[0], surface_ref, sems.at[2]),
    ])
    devices = head_ref.shape[0]
    slot_rows[...] = jnp.zeros_like(slot_rows)
    wait_all(copies)
    owner, block = columns(owner_ref), columns(block_ref)
    pairs = owner.shape[0]
    hits = (owner == iota((pairs, devices), 1)).astype(F32)
    earlier = (iota((pairs, pairs), 1) < iota((pairs, pairs), 0)).astype(F32)
    before = jnp.dot(earlier.astype(BF16), hits.astype(BF16), preferred_element_type=F32)
    slot = jnp.sum(before * hits, axis=1, keepdims=True)
    marked = jnp.where(
        slot == iota((pairs, 128), 1).astype(F32), (block + 1).astype(F32), 0.0
    )
    wanted = jnp.dot(
        jnp.transpose(hits).astype(BF16), marked.astype(BF16), preferred_element_type=F32
    )
    places[...] = owner.astype(F32) * 8.0 + slot
    spread = jnp.transpose(
        jnp.concatenate([places[pl.ds(h, pairs // 2, stride=2), :] for h in range(2)], axis=0)
    )
    place_ref[...] = spread[:8].astype(jnp.int32)
    slot_rows[pl.ds(0, devices, stride=8), :] = wanted
    surface = surface_ref[...].astype(BF16)
    head_ref[:, 0:16, :] = jnp.broadcast_to(surface[None], (devices, 16, 128))
    head_ref[:, 16:24, :] = slot_rows[...].reshape(devices, 8, 128).astype(BF16)


PACK = 192


def edges_kernel(
    odd_ref, state_ref, ocean_hbm, weight_hbm, owner_ref, block_ref, sea_ref,
    state_a_ref, state_b_ref, load_a_ref, load_b_ref, goal_ref,
    ocean_first, ocean_last, sems,
):
    i, odd = pl.program_id(0), odd_ref[0]
    tiles = 2 * owner_ref.shape[0]
    at_a = (1 - odd) * (weight_hbm.shape[0] - tiles)
    at_b = odd * (weight_hbm.shape[0] - tiles)
    copies = [
        pltpu.make_async_copy(weight_hbm.at[pl.ds(at_a, tiles)], load_a_ref.at[0:tiles], sems.at[0]),
        pltpu.make_async_copy(weight_hbm.at[pl.ds(at_b, tiles)], load_b_ref.at[0:tiles], sems.at[1]),
        pltpu.make_async_copy(ocean_hbm.at[:, 0], ocean_first, sems.at[2]),
        pltpu.make_async_copy(ocean_hbm.at[:, ocean_hbm.shape[1] - 1], ocean_last, sems.at[3]),
    ]
    pl.when(i == 0)(lambda: (start_all(copies), None)[1])
    rows, cells = state_ref.shape[0], state_ref.shape[1]
    first = jnp.swapaxes(state_ref[:, 0:8, :], 0, 1)[0:2]
    last = jnp.swapaxes(state_ref[:, cells - 8 : cells, :], 0, 1)[6:8]
    at = pl.ds(pl.multiple_of(i * rows, rows), rows)
    state_a_ref[:, at, :], state_b_ref[:, at, :] = sides(odd_ref, first, last)

    @pl.when(i == pl.num_programs(0) - 1)
    def _():
        layers = ocean_first.shape[0]
        goal = (owner_ref[...] * 16 + block_ref[...]).astype(F32)
        goal_ref[...] = jnp.zeros_like(goal_ref)
        goal_ref[0 : goal.shape[0], 0 : goal.shape[1]] = goal
        sea = sea_ref[...].astype(F32)
        width = sea.shape[1] // 2
        row = iota((8, width), 0)
        wait_all(copies)
        oceans = sides(odd_ref, ocean_first[...], ocean_last[...])
        lines = sides(odd_ref, sea[0:1], sea[cells - 1 : cells])
        for ref, ocean, line in zip((load_a_ref, load_b_ref), oceans, lines):
            halves = jnp.where(row == 0, line[:, :width], jnp.where(row == 1, line[:, width:], 0.0))
            empty = jnp.zeros((PACK - layers - 16, width), F32)
            pack = jnp.concatenate([ocean, halves, goal_ref[...], empty], axis=0)
            high = pack.astype(BF16)
            low = (pack - high.astype(F32)).astype(BF16)
            ref[tiles:] = jnp.concatenate([high, low], axis=0).reshape(
                2 * PACK // width, width, width
            )


def unpack(load):
    both = load.reshape(2 * PACK, load.shape[2]).astype(F32)
    return both[:PACK] + both[PACK:]


def sides(odd_ref, within, across):
    odd = odd_ref[0] == 1
    return jnp.where(odd, within, across), jnp.where(odd, across, within)


def lateral_matrix(size):
    row, col = iota((size, size), 0), iota((size, size), 1)
    near = jnp.where(jnp.abs(row - col) == 1, 1.0, 0.0)
    edge = jnp.where((row == 0) | (row == size - 1), -3.0, -4.0)
    return (near + jnp.where(row == col, edge, 0.0)).astype(BF16)


def without_forced(vertical):
    height = vertical.shape[0]
    col = iota(vertical.shape, 1)
    keep = (col != height // 2 - 1) & (col != height - 1)
    return jnp.where(keep, vertical.astype(F32), 0.0).astype(BF16)


def stencil(west, center, east, lateral, courant):
    w, c, e = west.astype(F32), center.astype(F32), east.astype(F32)
    side = jnp.dot(center, lateral, preferred_element_type=F32)
    return c + courant * (w - c) + ATM_DIFFUSION * (w + e + side)


GROUP = 8
LEVEL_PARTS = 4


def groups(hbm, held, sems, out=False):
    copies = []
    for g in range(held.shape[0] // GROUP):
        at = pl.ds(g * GROUP, GROUP)
        ends = (held.at[at], hbm.at[at]) if out else (hbm.at[at], held.at[at])
        copies.append(pltpu.make_async_copy(*ends, sems.at[g]))
    return copies


def keep_rows(ref, x, updated, mixed):
    height = updated.shape[0]
    for n, (field, r) in enumerate(
        ((updated, height // 2), (updated, height), (mixed, height // 2), (mixed, height))
    ):
        ref[n, x : x + 1, :] = field[r - 1 : r]


def first_step_kernel(
    state_hbm, courant_ref, vertical_ref, mixed_hbm, rows_ref, state, turned, mixed_out, in_sems, out_sems,
):
    levels = state.shape[0] // LEVEL_PARTS
    coming = start_all([
        pltpu.make_async_copy(
            state_hbm.at[pl.ds(n * levels, levels)], state.at[pl.ds(n * levels, levels)], in_sems.at[n]
        )
        for n in range(LEVEL_PARTS)
    ])
    going = groups(mixed_hbm, mixed_out, out_sems, out=True)
    cells, height = turned.shape[0], turned.shape[1]
    lateral = lateral_matrix(turned.shape[2])
    vertical = without_forced(vertical_ref[...])
    courant = courant_ref[...]

    def body(x):
        updated = stencil(turned[x - 1], turned[x], turned[x + 1], lateral, courant)
        mixed = jnp.dot(vertical, updated.astype(BF16), preferred_element_type=F32)
        keep_rows(rows_ref, x, updated, mixed)
        mixed_out[x] = mixed.astype(BF16)

    for x in (0, cells - 1):
        mixed_out[x] = jnp.zeros_like(mixed_out[x])
        rows_ref[:, x : x + 1, :] = jnp.zeros_like(rows_ref[:, x : x + 1, :])
    step = 32
    for n, c in enumerate(coming):
        c.wait()
        for at in range(n * levels, (n + 1) * levels, step):
            turned[:, at : at + step, :] = jnp.swapaxes(state[at : at + step], 0, 1)
    for g in range(cells // GROUP):
        for x in range(max(1, g * GROUP), min(cells - 1, (g + 1) * GROUP)):
            body(x)
        going[g].start()
    wait_all(going)


def first_edges_kernel(
    odd_ref, within_ref, across_ref, own_a_ref, own_b_ref, courant_ref, vertical_ref,
    mixed_hbm, rows_ref, mixed_out, sem,
):
    height = own_a_ref.shape[1]
    lateral = lateral_matrix(own_a_ref.shape[2])
    vertical = without_forced(vertical_ref[...])
    courant = courant_ref[...]
    left, right = sides(odd_ref, within_ref[...], across_ref[...])
    first, last = sides(odd_ref, own_a_ref[...], own_b_ref[...])
    rows_ref[...] = jnp.zeros_like(rows_ref)
    before = [left[0], left[1], first[0], first[1]]
    after = [last[0], last[1], right[0], right[1]]
    for i, columns_of in enumerate((before[:3], before[1:], after[:3], after[1:])):
        updated = stencil(*columns_of, lateral, courant)
        mixed = jnp.dot(vertical, updated.astype(BF16), preferred_element_type=F32)
        keep_rows(rows_ref, i, updated, mixed)
        mixed_out[i] = mixed.astype(BF16)
    copy = pltpu.make_async_copy(mixed_out, mixed_hbm, sem)
    copy.start()
    copy.wait()


def with_edges(main, edges):
    cells = main.shape[0]
    at = iota(main.shape, 0)
    return jnp.where(at == 0, edges[1:2], jnp.where(at == cells - 1, edges[2:3], main))


def ocean_step(ocean_ref, left, right, sea_ref, flux_ref, vertical_ref, out_ref):
    cells, width = sea_ref.shape
    height = ocean_ref.shape[0] // cells
    vertical = vertical_ref[...]
    high = vertical.astype(BF16)
    low = (vertical - high.astype(F32)).astype(BF16)
    both = jnp.concatenate([high, low], axis=0)
    lane = iota((height, width), 1)
    row = iota((height, width), 0)

    def column(x):
        if x < 0:
            return left
        if x >= cells:
            return right
        return ocean_ref[pl.ds(x, height, stride=cells), :]

    parts = []
    for x in range(cells):
        west, center, east = column(x - 1), column(x), column(x + 1)
        north = jnp.where(lane == width - 1, center, pltpu.roll(center, width - 1, 1))
        south = jnp.where(lane == 0, center, pltpu.roll(center, 1, 1))
        wet = sea_ref[x : x + 1, :].astype(F32)
        near = east + west + (north + south) - 4.0 * center
        heat = FLUX_GAIN * wet * flux_ref[0, x : x + 1, :]
        fresh = FLUX_GAIN * wet * flux_ref[1, x : x + 1, :]
        added = jnp.where(row == 0, heat, jnp.where(row == height // 2, fresh, 0.0))
        updated = (center + OCEAN_DIFFUSION * near) * wet + added
        upper = updated.astype(BF16)
        rest = (updated - upper.astype(F32)).astype(BF16)
        parts.append((upper, rest))
        if x % 2 == 0:
            continue
        upper, rest = (jnp.concatenate(p, axis=1) for p in zip(*parts))
        parts = []
        mixed = jnp.dot(both, upper, preferred_element_type=F32)
        mixed = mixed[:height] + mixed[height:]
        mixed += jnp.dot(high, rest, preferred_element_type=F32)
        out_ref[pl.ds(x - 1, height, stride=cells), :] = mixed[:, :width]
        out_ref[pl.ds(x, height, stride=cells), :] = mixed[:, width:]


PARTS = 8


def weight_copies(weight_hbm, held, sems):
    step = weight_hbm.shape[0] // PARTS
    return start_all([
        pltpu.make_async_copy(
            weight_hbm.at[pl.ds(i * step, step)], held.at[pl.ds(i * step, step)], sems.at[i]
        )
        for i in range(PARTS)
    ])


def couple_kernel(
    layers,
    odd_ref, head_ref, goal_ref, within_ref, across_ref, weight_hbm, sea_ref, place_ref,
    rows_ref, edges_ref, courant_ref, vertical_ref, coupled_ref, slots_ref, out_ref,
    slot_rows, by_block, flux_rows, shares, held, sems,
):
    copies = weight_copies(weight_hbm, held, sems)
    devices = head_ref.shape[0]
    blocks, sources = held.shape[0], held.shape[1]
    surface = head_ref[:, 0:16, :].reshape(devices * 16, 128)
    slot_rows[...] = head_ref[:, 16:24, :].astype(F32).reshape(devices * 8, 128)
    slots_ref[...] = jnp.transpose(slot_rows[pl.ds(0, devices, stride=8), :])[:8]

    tiles = 2 * sources
    left_pack, right_pack = (
        p[layers : layers + 16]
        for p in sides(odd_ref, unpack(within_ref[tiles:]), unpack(across_ref[tiles:]))
    )
    lane = iota((8, 128), 1)
    goals = jnp.where(
        lane < blocks,
        goal_ref[...],
        jnp.where(
            lane < blocks + 2,
            pltpu.roll(left_pack[8:], 2, 1),
            jnp.where(lane < blocks + 4, pltpu.roll(right_pack[8:], blocks + 2, 1), -1.0),
        ),
    )
    count = blocks + 8
    goal = jnp.concatenate(
        [
            jnp.transpose(jnp.broadcast_to(goals[k : k + 1], (128, 128)))[:count, :1]
            for k in range(sources)
        ],
        axis=0,
    ).astype(jnp.int32)
    pick = (goal == iota((sources * count, devices * 16), 1)).astype(F32).astype(BF16)
    fetched = jnp.dot(pick, surface, preferred_element_type=F32)
    empty = jnp.zeros((128 - count, 128), F32)
    wanted = jnp.concatenate(
        [
            jnp.transpose(jnp.concatenate([fetched[k * count : (k + 1) * count], empty], axis=0))
            for k in range(sources)
        ],
        axis=0,
    ).astype(BF16)
    lane = iota((128, 128), 1)

    def add(j, weights, total):
        rows = jnp.concatenate(weights, axis=1)
        return jnp.where(lane == j, jnp.dot(rows, wanted, preferred_element_type=F32), total)

    total = jnp.zeros((128, 128), F32)
    for n, weights in enumerate(sides(odd_ref, within_ref[0:tiles], across_ref[0:tiles])):
        for b in range(2):
            total = add(
                blocks + 2 * n + b, [weights[b * sources + k] for k in range(sources)], total
            )
    step = blocks // PARTS
    for i, c in enumerate(copies):
        c.wait()
        for j in range(i * step, (i + 1) * step):
            total = add(j, [held[j, k] for k in range(sources)], total)
    by_block[...] = jnp.transpose(total)

    half = blocks // 2
    temp = jnp.concatenate([by_block[pl.ds(h, half, stride=2), :] for h in range(2)], axis=1)
    coupled_ref[0:half, :] = temp
    exchange = EXCHANGE_RATE * sea_ref[...].astype(F32)
    upper = with_edges(rows_ref[0], edges_ref[0])
    lower = with_edges(rows_ref[1], edges_ref[1])
    heat, moist = exchange * (temp - upper), exchange * (0.5 * temp - lower)
    upper = (upper + heat).astype(BF16).astype(F32)
    lower = (lower + moist).astype(BF16).astype(F32)
    coupled_ref[half : 2 * half, :] = upper
    coupled_ref[2 * half : 3 * half, :] = lower
    halo = []
    for n, (edge, pack) in enumerate(((0, left_pack), (3, right_pack))):
        at = blocks + 2 * n
        warm = jnp.concatenate([by_block[at : at + 1, :], by_block[at + 1 : at + 2, :]], axis=1)
        rate = EXCHANGE_RATE * jnp.concatenate([pack[0:1], pack[1:2]], axis=1)
        u, w = edges_ref[0, edge : edge + 1, :], edges_ref[1, edge : edge + 1, :]
        halo.append((u + rate * (warm - u)).astype(BF16).astype(F32))
        halo.append((w + rate * (0.5 * warm - w)).astype(BF16).astype(F32))
    coupled_ref[3 * half :, :] = jnp.zeros_like(coupled_ref[3 * half :, :])
    for n, line in enumerate(halo):
        coupled_ref[3 * half + n : 3 * half + n + 1, :] = line

    height = vertical_ref.shape[0]
    top, low = height // 2 - 1, height - 1
    cells, width = sea_ref.shape
    sub, lane = iota((cells, width), 0), iota((cells, width), 1)

    def row_of(r, mix, upper, lower):
        a = vertical_ref[pl.ds(r - 7, 8), :].astype(F32)[7:8]
        kept = mix.astype(BF16).astype(F32)
        return (kept + a[:, top : top + 1] * upper + a[:, low : low + 1] * lower).astype(BF16).astype(F32)

    def updated(r, n):
        edges = edges_ref[n]
        center = row_of(r, with_edges(rows_ref[n], edges), upper, lower)
        left = row_of(r, edges[0:1], halo[0], halo[1])
        right = row_of(r, edges[3:4], halo[2], halo[3])
        west = jnp.where(sub == 0, left, pltpu.roll(center, 1, 0))
        east = jnp.where(sub == cells - 1, right, pltpu.roll(center, cells - 1, 0))
        north = jnp.where(lane == width - 1, center, pltpu.roll(center, width - 1, 1))
        south = jnp.where(lane == 0, center, pltpu.roll(center, 1, 1))
        near = east + west + (north + south) - 4.0 * center
        courant = courant_ref[pl.ds(r - 7, 8), :][7:8]
        return center - courant * (center - west) + ATM_DIFFUSION * near

    heat = 0.5 * heat + 0.5 * (exchange * (temp - updated(top, 2)))
    moist = 0.5 * moist + 0.5 * (
        exchange * (0.5 * temp - updated(low, 3))
    )
    flux_rows[...] = jnp.zeros_like(flux_rows)
    for v, flux in enumerate((heat, moist)):
        for h in range(2):
            flux_rows[pl.ds(h * 10 + v, cells, stride=16), :] = flux[:, h * 128 : (h + 1) * 128]
    for x in range(half):
        rows = jnp.concatenate(
            [flux_rows[(2 * x + h) * 8 : (2 * x + h + 1) * 8, :] for h in range(2)], axis=1
        ).astype(BF16)
        weights = jnp.concatenate(
            [
                jnp.concatenate([held[2 * x + h, k] for k in range(sources)], axis=1)
                for h in range(2)
            ],
            axis=0,
        )
        got = jnp.dot(rows, weights, preferred_element_type=F32)
        for k in range(sources):
            at = (k * half + x) * 8
            shares[at : at + 8, :] = got[:, k * 128 : (k + 1) * 128]

    pairs = blocks * sources
    place = place_ref[0:1, :]
    rows = iota((out_ref.shape[0], pairs), 0)
    total = jnp.zeros(out_ref.shape, F32)
    for v in range(2):
        pick = (rows == place + 4 * v).astype(F32).astype(BF16)
        share = jnp.concatenate(
            [shares[pl.ds(2 * h + v, pairs // 2, stride=8), :] for h in range(2)], axis=0
        ).astype(BF16)
        total += jnp.dot(pick, share, preferred_element_type=F32)
    out_ref[...] = total.astype(BF16)


def second_step_kernel(
    tiles, odd_ref, mixed_hbm, edge_hbm, courant_ref, vertical_ref, sea_ref, coupled_ref,
    ocean_hbm, within_ref, across_ref, ocean_sea_ref, flux_ref, ocean_vertical_ref,
    out_hbm, new_ocean_hbm,
    mixed_ref, edge_ref, state, result, out_ref, ocean_ref, new_ocean_ref,
    in_sems, edge_sem, ocean_sems, out_sems,
):
    edge_copy = pltpu.make_async_copy(edge_hbm, edge_ref, edge_sem)
    edge_copy.start()
    coming = start_all(groups(mixed_hbm, mixed_ref, in_sems))
    ocean_coming = pltpu.make_async_copy(ocean_hbm, ocean_ref, ocean_sems.at[0])
    ocean_coming.start()
    cells, height = mixed_ref.shape[0], mixed_ref.shape[1]
    top, low = height // 2 - 1, height - 1
    lateral = lateral_matrix(mixed_ref.shape[2])
    vertical = vertical_ref[...]
    upper_column = vertical[:, top : top + 1].astype(F32)
    lower_column = vertical[:, low : low + 1].astype(F32)
    courant = courant_ref[...]
    halo = 3 * cells

    def complete(to, mixed, upper_at, lower_at):
        upper = coupled_ref[upper_at : upper_at + 1, :]
        lower = coupled_ref[lower_at : lower_at + 1, :]
        done = mixed.astype(F32) + upper_column * upper + lower_column * lower
        state[to] = done.astype(BF16)

    last = iota((8, mixed_ref.shape[2]), 0) == 7

    def advance(x):
        updated = stencil(state[x], state[x + 1], state[x + 2], lateral, courant)
        exchange = EXCHANGE_RATE * sea_ref[x : x + 1, :].astype(F32)
        temp = coupled_ref[x : x + 1, :]
        upper = updated[top - 7 : top + 1]
        lower = updated[low - 7 : low + 1]
        upper = jnp.where(last, upper + exchange * (temp - upper), upper)
        lower = jnp.where(last, lower + exchange * (0.5 * temp - lower), lower)
        forced = jnp.concatenate(
            [updated[: top - 7], upper, updated[top + 1 : low - 7], lower], axis=0
        ).astype(BF16)
        result[x] = jnp.dot(vertical, forced, preferred_element_type=F32).astype(BF16)

    edge_copy.wait()
    coming[0].wait()
    complete(0, edge_ref[0], halo, halo + 1)
    complete(1, edge_ref[1], cells, 2 * cells)
    going = []
    step, half = 32, cells // 2
    for x in range(cells):
        ahead = x + 1
        if ahead % GROUP == 0 and ahead < cells:
            coming[ahead // GROUP].wait()
        if ahead < cells - 1:
            complete(ahead + 1, mixed_ref[ahead], cells + ahead, 2 * cells + ahead)
        elif ahead == cells - 1:
            complete(cells, edge_ref[2], 2 * cells - 1, 3 * cells - 1)
        else:
            complete(cells + 1, edge_ref[3], halo + 2, halo + 3)
        advance(x)
        if (x + 1) % half:
            continue
        across = slice(x + 1 - half, x + 1)
        for i in range(height // step):
            at = slice(i * step, (i + 1) * step)
            out_ref[at, across, :] = jnp.swapaxes(result[across, at, :], 0, 1)
        ends = out_ref.at[:, across], out_hbm.at[:, across]
        going.append(pltpu.make_async_copy(*ends, out_sems.at[(x + 1) // half - 1]))
        going[-1].start()
        if x + 1 == cells:
            break
        ocean_coming.wait()
        layers = ocean_ref.shape[0] // ocean_sea_ref.shape[0]
        left, right = (
            p[:layers]
            for p in sides(odd_ref, unpack(within_ref[tiles:]), unpack(across_ref[tiles:]))
        )
        ocean_step(
            ocean_ref, left, right, ocean_sea_ref, flux_ref, ocean_vertical_ref, new_ocean_ref
        )
        going.append(pltpu.make_async_copy(new_ocean_ref, new_ocean_hbm, ocean_sems.at[1]))
        going[-1].start()
    wait_all(going)


def land_kernel(incoming_ref, slots_ref, sea_ref, out_ref, wide):
    devices = slots_ref.shape[1]
    cells = sea_ref.shape[0]
    wide[...] = incoming_ref[...].astype(F32)
    wet = sea_ref[...].astype(F32)
    here = (iota((cells, devices), 0) + 1).astype(F32)
    picks = [(slots_ref[s : s + 1, :] == here).astype(F32).astype(BF16) for s in range(4)]
    for v in range(2):
        total = jnp.zeros((cells, 128), F32)
        for s in range(4):
            part = wide[pl.ds(v * 4 + s, devices, stride=8), :].astype(BF16)
            total += jnp.dot(picks[s], part, preferred_element_type=F32)
        out_ref[v] = total * wet


def swap(within, across):
    peers = lax.axis_size(BOTH)
    pair = [(i, i ^ 1) for i in range(peers)]
    other = [(i, ((i + 1) ^ 1) - 1) for i in range(peers)]
    other = [(i, j % peers) for i, j in other]
    return lax.ppermute(within, BOTH, pair), lax.ppermute(across, BOTH, other)


def per_device(
    atm_state, atm_sea, zonal_courant, atm_vertical, ocean_state, ocean_sea,
    flux_in, ocean_vertical, remap_owner, remap_block, remap_weight,
):
    devices = lax.axis_size(BOTH)
    height, cells, width = atm_state.shape
    blocks, sources = remap_owner.shape
    pairs = blocks * sources
    courant = zonal_courant.reshape(height, 1)
    layers, ocean_cells, ocean_width = ocean_state.shape
    ocean_rows = ocean_state.reshape(layers * ocean_cells, ocean_width)
    owner, block = remap_owner.T, remap_block.T
    odd = is_odd()
    dma = pltpu.SemaphoreType.DMA
    held = [pltpu.VMEM(remap_weight.shape, BF16), dma((PARTS,))]
    whole = pltpu.VMEM((cells, height, width), BF16)
    levels = 64

    head, place = call(
        plan_kernel,
        (shape((devices, HEAD, 128), BF16), shape((8, pairs), jnp.int32)),
        owner, block, ocean_state,
        specs={0: ANY, 1: ANY, 2: ANY},
        scratch=[
            pltpu.VMEM((devices * 8, 128), F32),
            pltpu.VMEM((pairs, 128), F32),
            pltpu.VMEM(owner.shape, jnp.int32),
            pltpu.VMEM(owner.shape, jnp.int32),
            pltpu.VMEM((ocean_cells, ocean_width), F32),
            dma((3,)),
        ],
        limit=58,
        touched=1 << 20,
    )
    gathered = lax.all_to_all(head, BOTH, split_axis=0, concat_axis=0, tiled=True)

    tiles = 2 * sources
    columns_sent = shape((2, height, width), BF16)
    load = shape((tiles + 2 * PACK // 128, 128, 128), BF16)
    state_a, state_b, load_a, load_b, goal = call(
        edges_kernel,
        (columns_sent, columns_sent, load, load, shape((8, 128), F32)),
        odd, atm_state, ocean_state, remap_weight.reshape(pairs, 128, 128), owner, block, atm_sea,
        specs={
            0: SCALAR,
            1: pl.BlockSpec((levels, cells, width), lambda i: (i, 0, 0)),
            2: ANY,
            3: ANY,
        },
        scratch=[pltpu.VMEM((layers, ocean_width), F32)] * 2 + [dma((4,))],
        grid=(height // levels,),
        limit=54,
        touched=6 << 20,
    )
    state_near = swap(state_a, state_b)
    load_near = swap(load_a, load_b)
    mixed, rows = call(
        first_step_kernel,
        (shape((cells, height, width), BF16), shape((4, cells, width), F32)),
        atm_state, courant, atm_vertical,
        specs={0: ANY},
        out_specs={0: ANY},
        scratch=[
            pltpu.VMEM(atm_state.shape, BF16), whole, whole,
            dma((LEVEL_PARTS,)), dma((cells // GROUP,)),
        ],
        touched=16 << 20,
    )
    mixed_edge, edge_rows = call(
        first_edges_kernel,
        (shape((4, height, width), BF16), shape((4, 8, width), F32)),
        odd, *state_near, state_a, state_b, courant, atm_vertical,
        specs={0: SCALAR},
        out_specs={0: ANY},
        scratch=[pltpu.VMEM((4, height, width), BF16), dma],
        limit=50,
        touched=2 << 20,
    )

    coupled, slots, outgoing = call(
        functools.partial(couple_kernel, layers),
        (
            shape((3 * cells + 8, width), F32),
            shape((8, devices), F32),
            shape((devices * 8, 128), BF16),
        ),
        odd, gathered, goal, *load_near, remap_weight, atm_sea, place,
        rows, edge_rows, courant, atm_vertical,
        specs={0: SCALAR, 5: ANY},
        scratch=[
            pltpu.VMEM((devices * 8, 128), F32),
            pltpu.VMEM((128, 128), F32),
            pltpu.VMEM((blocks * 8, 128), F32),
            pltpu.VMEM((pairs * 4, 128), F32),
            *held,
        ],
        limit=50,
        touched=16 << 20,
    )
    incoming = lax.all_to_all(
        outgoing.reshape(devices, 8, 128), BOTH, split_axis=0, concat_axis=0, tiled=True
    )
    state, new_ocean = call(
        functools.partial(second_step_kernel, tiles),
        (shape(atm_state.shape, BF16), shape(ocean_rows.shape, F32)),
        odd, mixed, mixed_edge, courant, atm_vertical, atm_sea, coupled,
        ocean_rows, *load_near, ocean_sea, flux_in, ocean_vertical,
        specs={0: SCALAR, 1: ANY, 2: ANY, 7: ANY},
        out_specs={0: ANY, 1: ANY},
        scratch=[
            whole,
            pltpu.VMEM((4, height, width), BF16),
            pltpu.VMEM((cells + 2, height, width), BF16),
            whole,
            pltpu.VMEM(atm_state.shape, BF16),
            pltpu.VMEM(ocean_rows.shape, F32),
            pltpu.VMEM(ocean_rows.shape, F32),
            dma((cells // GROUP,)),
            dma,
            dma((2,)),
            dma((2,)),
        ],
        limit=52,
        touched=24 << 20,
    )
    ocean_flux = call(
        land_kernel,
        shape((2, ocean_cells, ocean_width), F32),
        incoming.reshape(devices * 8, 128), slots, ocean_sea,
        scratch=[pltpu.VMEM((devices * 8, 128), F32)],
        touched=1 << 20,
    )
    return state, new_ocean.reshape(ocean_state.shape), ocean_flux


def solution(mesh):
    return jax.shard_map(
        per_device,
        mesh=mesh,
        in_specs=(
            P(None, BOTH, None), P(BOTH, None), P(), P(), P(None, BOTH, None), P(BOTH, None),
            P(None, BOTH, None), P(), P(BOTH, None), P(BOTH, None), P(BOTH, None, None, None),
        ),
        out_specs=(P(None, BOTH, None), P(None, BOTH, None), P(None, BOTH, None)),
        check_vma=False,
    )
```

```python
import functools

import jax
import jax.numpy as jnp
from jax import lax
from jax.experimental import pallas as pl
from jax.experimental.pallas import tpu as pltpu
from jax.sharding import PartitionSpec as P

ATM_DIFFUSION = 0.1
OCEAN_DIFFUSION = 0.15
EXCHANGE_RATE = 0.3
FLUX_GAIN = 0.5

F32 = jnp.float32
BF16 = jnp.bfloat16
VM = pltpu.VMEM
BOTH = ("comp", "tile")
HEAD = 24


def call(kernel, outs, *args, scratch=(), specs=None, out_specs=None, limit=50, touched=0, grid=(), aliases=None):
    specs, out_specs = specs or {}, out_specs or {}
    single = not isinstance(outs, tuple)
    placed = [
        out_specs.get(i, pl.BlockSpec(memory_space=VM)) for i in range(1 if single else len(outs))
    ]
    return pl.pallas_call(
        kernel,
        out_shape=outs,
        grid=grid,
        in_specs=[specs.get(i, pl.BlockSpec(memory_space=VM)) for i in range(len(args))],
        out_specs=placed[0] if single else tuple(placed),
        scratch_shapes=list(scratch),
        input_output_aliases=aliases or {},
        compiler_params=pltpu.CompilerParams(vmem_limit_bytes=limit << 20),
        cost_estimate=pl.CostEstimate(flops=0, bytes_accessed=touched, transcendentals=0),
    )(*args)


SCALAR = pl.BlockSpec(memory_space=pltpu.SMEM)
ANY = pl.BlockSpec(memory_space=pltpu.HBM)


def start_all(copies):
    for c in copies:
        c.start()
    return copies


def wait_all(copies):
    for c in copies:
        c.wait()


def shape(dims, dtype):
    return jax.ShapeDtypeStruct(dims, dtype)


def iota(dims, axis):
    return lax.broadcasted_iota(jnp.int32, dims, axis)


def columns(ref):
    count, rows = ref.shape
    wide = [jnp.broadcast_to(ref[k : k + 1, :], (128, rows)) for k in range(count)]
    return jnp.concatenate([jnp.transpose(w) for w in wide], axis=0)


def is_odd():
    return jnp.bitwise_and(lax.axis_index("tile"), 1).astype(jnp.int32).reshape(1)


def plan_kernel(
    owner_hbm, block_hbm, ocean_hbm, head_ref, place_ref, slot_rows, places, owner_ref, block_ref, surface_ref, sems
):
    copies = start_all([
        pltpu.make_async_copy(owner_hbm, owner_ref, sems.at[0]),
        pltpu.make_async_copy(block_hbm, block_ref, sems.at[1]),
        pltpu.make_async_copy(ocean_hbm.at[0], surface_ref, sems.at[2]),
    ])
    devices = head_ref.shape[0]
    slot_rows[...] = jnp.zeros_like(slot_rows)
    wait_all(copies)
    owner, block = columns(owner_ref), columns(block_ref)
    pairs = owner.shape[0]
    hits = (owner == iota((pairs, devices), 1)).astype(F32)
    earlier = (iota((pairs, pairs), 1) < iota((pairs, pairs), 0)).astype(F32)
    before = jnp.dot(earlier.astype(BF16), hits.astype(BF16), preferred_element_type=F32)
    slot = jnp.sum(before * hits, axis=1, keepdims=True)
    marked = jnp.where(
        slot == iota((pairs, 128), 1).astype(F32), (block + 1).astype(F32), 0.0
    )
    wanted = jnp.dot(
        jnp.transpose(hits).astype(BF16), marked.astype(BF16), preferred_element_type=F32
    )
    places[...] = owner.astype(F32) * 8.0 + slot
    spread = jnp.transpose(
        jnp.concatenate([places[pl.ds(h, pairs // 2, stride=2), :] for h in range(2)], axis=0)
    )
    place_ref[...] = spread[:8].astype(jnp.int32)
    slot_rows[pl.ds(0, devices, stride=8), :] = wanted
    surface = surface_ref[...].astype(BF16)
    head_ref[:, 0:16, :] = jnp.broadcast_to(surface[None], (devices, 16, 128))
    head_ref[:, 16:24, :] = slot_rows[...].reshape(devices, 8, 128).astype(BF16)


PACK = 192


def edges_kernel(
    odd_ref, state_ref, ocean_hbm, weight_hbm, owner_ref, block_ref, sea_ref,
    state_a_ref, state_b_ref, load_a_ref, load_b_ref, goal_ref,
    ocean_first, ocean_last, sems,
):
    i, odd = pl.program_id(0), odd_ref[0]
    tiles = 2 * owner_ref.shape[0]
    at_a = (1 - odd) * (weight_hbm.shape[0] - tiles)
    at_b = odd * (weight_hbm.shape[0] - tiles)
    copies = [
        pltpu.make_async_copy(weight_hbm.at[pl.ds(at_a, tiles)], load_a_ref.at[0:tiles], sems.at[0]),
        pltpu.make_async_copy(weight_hbm.at[pl.ds(at_b, tiles)], load_b_ref.at[0:tiles], sems.at[1]),
        pltpu.make_async_copy(ocean_hbm.at[:, 0], ocean_first, sems.at[2]),
        pltpu.make_async_copy(ocean_hbm.at[:, ocean_hbm.shape[1] - 1], ocean_last, sems.at[3]),
    ]
    pl.when(i == 0)(lambda: (start_all(copies), None)[1])
    rows, cells = state_ref.shape[0], state_ref.shape[1]
    first = jnp.swapaxes(state_ref[:, 0:8, :], 0, 1)[0:2]
    last = jnp.swapaxes(state_ref[:, cells - 8 : cells, :], 0, 1)[6:8]
    at = pl.ds(pl.multiple_of(i * rows, rows), rows)
    state_a_ref[:, at, :], state_b_ref[:, at, :] = sides(odd_ref, first, last)

    @pl.when(i == pl.num_programs(0) - 1)
    def _():
        layers = ocean_first.shape[0]
        goal = (owner_ref[...] * 16 + block_ref[...]).astype(F32)
        goal_ref[...] = jnp.zeros_like(goal_ref)
        goal_ref[0 : goal.shape[0], 0 : goal.shape[1]] = goal
        sea = sea_ref[...].astype(F32)
        width = sea.shape[1] // 2
        row = iota((8, width), 0)
        wait_all(copies)
        oceans = sides(odd_ref, ocean_first[...], ocean_last[...])
        lines = sides(odd_ref, sea[0:1], sea[cells - 1 : cells])
        for ref, ocean, line in zip((load_a_ref, load_b_ref), oceans, lines):
            halves = jnp.where(row == 0, line[:, :width], jnp.where(row == 1, line[:, width:], 0.0))
            empty = jnp.zeros((PACK - layers - 16, width), F32)
            pack = jnp.concatenate([ocean, halves, goal_ref[...], empty], axis=0)
            high = pack.astype(BF16)
            low = (pack - high.astype(F32)).astype(BF16)
            ref[tiles:] = jnp.concatenate([high, low], axis=0).reshape(
                2 * PACK // width, width, width
            )


def unpack(load):
    both = load.reshape(2 * PACK, load.shape[2]).astype(F32)
    return both[:PACK] + both[PACK:]


def sides(odd_ref, within, across):
    odd = odd_ref[0] == 1
    return jnp.where(odd, within, across), jnp.where(odd, across, within)


def lateral_matrix(size):
    row, col = iota((size, size), 0), iota((size, size), 1)
    near = jnp.where(jnp.abs(row - col) == 1, 1.0, 0.0)
    edge = jnp.where((row == 0) | (row == size - 1), -3.0, -4.0)
    return (near + jnp.where(row == col, edge, 0.0)).astype(BF16)


def without_forced(vertical):
    height = vertical.shape[0]
    col = iota(vertical.shape, 1)
    keep = (col != height // 2 - 1) & (col != height - 1)
    return jnp.where(keep, vertical.astype(F32), 0.0).astype(BF16)


def stencil(west, center, east, lateral, courant):
    w, c, e = west.astype(F32), center.astype(F32), east.astype(F32)
    side = jnp.dot(center, lateral, preferred_element_type=F32)
    return c + courant * (w - c) + ATM_DIFFUSION * (w + e + side)


GROUP = 8
LEVEL_PARTS = 4


def groups(hbm, held, sems, out=False):
    copies = []
    for g in range(held.shape[0] // GROUP):
        at = pl.ds(g * GROUP, GROUP)
        ends = (held.at[at], hbm.at[at]) if out else (hbm.at[at], held.at[at])
        copies.append(pltpu.make_async_copy(*ends, sems.at[g]))
    return copies


def keep_rows(ref, x, updated, mixed):
    height = updated.shape[0]
    for n, (field, r) in enumerate(
        ((updated, height // 2), (updated, height), (mixed, height // 2), (mixed, height))
    ):
        ref[n, x : x + 1, :] = field[r - 1 : r]


def first_step_kernel(
    state_hbm, courant_ref, vertical_ref, ocean_hbm, ocean_sea_ref, flux_ref, ocean_vertical_ref,
    mixed_hbm, rows_ref, new_ocean_hbm, ocean_ref, new_ocean_ref, ocean_sems, state, turned, mixed_out, in_sems, out_sems,
):
    levels = state.shape[0] // LEVEL_PARTS
    coming = start_all([
        pltpu.make_async_copy(
            state_hbm.at[pl.ds(n * levels, levels)], state.at[pl.ds(n * levels, levels)], in_sems.at[n]
        )
        for n in range(LEVEL_PARTS)
    ])
    ocean_coming = pltpu.make_async_copy(ocean_hbm, ocean_ref, ocean_sems.at[0])
    ocean_coming.start()
    going = groups(mixed_hbm, mixed_out, out_sems, out=True)
    cells, height = turned.shape[0], turned.shape[1]
    lateral = lateral_matrix(turned.shape[2])
    vertical = without_forced(vertical_ref[...])
    courant = courant_ref[...]

    def body(x):
        updated = stencil(turned[x - 1], turned[x], turned[x + 1], lateral, courant)
        mixed = jnp.dot(vertical, updated.astype(BF16), preferred_element_type=F32)
        keep_rows(rows_ref, x, updated, mixed)
        mixed_out[x] = mixed.astype(BF16)

    for x in (0, cells - 1):
        mixed_out[x] = jnp.zeros_like(mixed_out[x])
        rows_ref[:, x : x + 1, :] = jnp.zeros_like(rows_ref[:, x : x + 1, :])
    step = 32
    for n, c in enumerate(coming):
        c.wait()
        for at in range(n * levels, (n + 1) * levels, step):
            turned[:, at : at + step, :] = jnp.swapaxes(state[at : at + step], 0, 1)
    for g in range(cells // GROUP):
        for x in range(max(1, g * GROUP), min(cells - 1, (g + 1) * GROUP)):
            body(x)
        going[g].start()
        if (g + 1) * GROUP != cells // 2:
            continue
        ocean_coming.wait()
        ocean_cells = ocean_sea_ref.shape[0]
        layers = ocean_ref.shape[0] // ocean_cells

        def column(x):
            return pl.ds(x, layers, stride=ocean_cells), slice(None)

        def store(x, value):
            new_ocean_ref[column(x)] = value

        for x in (0, ocean_cells - 1):
            store(x, jnp.zeros((layers, ocean_ref.shape[1]), F32))
        ocean_step(
            [(x, x + 1) for x in range(1, ocean_cells - 1, 2)],
            lambda x: ocean_ref[column(x)],
            ocean_sea_ref, flux_ref, ocean_vertical_ref, store,
        )
        going.append(pltpu.make_async_copy(new_ocean_ref, new_ocean_hbm, ocean_sems.at[1]))
        going[-1].start()
    wait_all(going)


def edge_columns(left, right, first, last, courant, vertical, keep, mixed_out):
    lateral = lateral_matrix(first.shape[2])
    vertical = without_forced(vertical)
    before = [left[0], left[1], first[0], first[1]]
    after = [last[0], last[1], right[0], right[1]]
    keep[...] = jnp.zeros_like(keep)
    for i, columns_of in enumerate((before[:3], before[1:], after[:3], after[1:])):
        updated = stencil(*columns_of, lateral, courant)
        mixed = jnp.dot(vertical, updated.astype(BF16), preferred_element_type=F32)
        keep_rows(keep, i, updated, mixed)
        mixed_out[i] = mixed.astype(BF16)


def with_edges(main, edges):
    cells = main.shape[0]
    at = iota(main.shape, 0)
    return jnp.where(at == 0, edges[1:2], jnp.where(at == cells - 1, edges[2:3], main))


def ocean_step(pairs, column, sea_ref, flux_ref, vertical_ref, store):
    width = sea_ref.shape[1]
    height = vertical_ref.shape[0]
    vertical = vertical_ref[...]
    high = vertical.astype(BF16)
    low = (vertical - high.astype(F32)).astype(BF16)
    both = jnp.concatenate([high, low], axis=0)
    lane = iota((height, width), 1)
    row = iota((height, width), 0)

    def forced(x):
        west, center, east = column(x - 1), column(x), column(x + 1)
        north = jnp.where(lane == width - 1, center, pltpu.roll(center, width - 1, 1))
        south = jnp.where(lane == 0, center, pltpu.roll(center, 1, 1))
        wet = sea_ref[x : x + 1, :].astype(F32)
        near = east + west + (north + south) - 4.0 * center
        heat = FLUX_GAIN * wet * flux_ref[0, x : x + 1, :]
        fresh = FLUX_GAIN * wet * flux_ref[1, x : x + 1, :]
        added = jnp.where(row == 0, heat, jnp.where(row == height // 2, fresh, 0.0))
        return (center + OCEAN_DIFFUSION * near) * wet + added

    for pair in pairs:
        updated = jnp.concatenate([forced(x) for x in pair], axis=1)
        upper = updated.astype(BF16)
        rest = (updated - upper.astype(F32)).astype(BF16)
        mixed = jnp.dot(both, upper, preferred_element_type=F32)
        mixed = mixed[:height] + mixed[height:]
        mixed += jnp.dot(high, rest, preferred_element_type=F32)
        for n, x in enumerate(pair):
            store(x, mixed[:, n * width : (n + 1) * width])


PARTS = 8


def weight_copies(weight_hbm, held, sems):
    step = weight_hbm.shape[0] // PARTS
    return start_all([
        pltpu.make_async_copy(
            weight_hbm.at[pl.ds(i * step, step)], held.at[pl.ds(i * step, step)], sems.at[i]
        )
        for i in range(PARTS)
    ])


def couple_kernel(
    layers,
    odd_ref, head_ref, goal_ref, within_ref, across_ref, weight_hbm, sea_ref, place_ref,
    rows_ref, near_within_ref, near_across_ref, own_a_ref, own_b_ref, courant_ref, vertical_ref,
    coupled_ref, slots_ref, out_ref, mixed_hbm,
    slot_rows, by_block, flux_rows, shares, edges_ref, mixed_out, mixed_sem, held, sems,
):
    copies = weight_copies(weight_hbm, held, sems)
    edge_columns(
        *sides(odd_ref, near_within_ref[...], near_across_ref[...]),
        *sides(odd_ref, own_a_ref[...], own_b_ref[...]),
        courant_ref[...], vertical_ref[...], edges_ref, mixed_out,
    )
    mixed_going = pltpu.make_async_copy(mixed_out, mixed_hbm, mixed_sem)
    mixed_going.start()
    devices = head_ref.shape[0]
    blocks, sources = held.shape[0], held.shape[1]
    surface = head_ref[:, 0:16, :].reshape(devices * 16, 128)
    slot_rows[...] = head_ref[:, 16:24, :].astype(F32).reshape(devices * 8, 128)
    slots_ref[...] = jnp.transpose(slot_rows[pl.ds(0, devices, stride=8), :])[:8]

    tiles = 2 * sources
    left_pack, right_pack = (
        p[layers : layers + 16]
        for p in sides(odd_ref, unpack(within_ref[tiles:]), unpack(across_ref[tiles:]))
    )
    lane = iota((8, 128), 1)
    goals = jnp.where(
        lane < blocks,
        goal_ref[...],
        jnp.where(
            lane < blocks + 2,
            pltpu.roll(left_pack[8:], 2, 1),
            jnp.where(lane < blocks + 4, pltpu.roll(right_pack[8:], blocks + 2, 1), -1.0),
        ),
    )
    count = blocks + 8
    goal = jnp.concatenate(
        [
            jnp.transpose(jnp.broadcast_to(goals[k : k + 1], (128, 128)))[:count, :1]
            for k in range(sources)
        ],
        axis=0,
    ).astype(jnp.int32)
    pick = (goal == iota((sources * count, devices * 16), 1)).astype(F32).astype(BF16)
    fetched = jnp.dot(pick, surface, preferred_element_type=F32)
    empty = jnp.zeros((128 - count, 128), F32)
    wanted = jnp.concatenate(
        [
            jnp.transpose(jnp.concatenate([fetched[k * count : (k + 1) * count], empty], axis=0))
            for k in range(sources)
        ],
        axis=0,
    ).astype(BF16)
    lane = iota((128, 128), 1)

    def add(j, weights, total):
        rows = jnp.concatenate(weights, axis=1)
        return jnp.where(lane == j, jnp.dot(rows, wanted, preferred_element_type=F32), total)

    total = jnp.zeros((128, 128), F32)
    for n, weights in enumerate(sides(odd_ref, within_ref[0:tiles], across_ref[0:tiles])):
        for b in range(2):
            total = add(
                blocks + 2 * n + b, [weights[b * sources + k] for k in range(sources)], total
            )
    step = blocks // PARTS
    for i, c in enumerate(copies):
        c.wait()
        for j in range(i * step, (i + 1) * step):
            total = add(j, [held[j, k] for k in range(sources)], total)
    by_block[...] = jnp.transpose(total)

    half = blocks // 2
    temp = jnp.concatenate([by_block[pl.ds(h, half, stride=2), :] for h in range(2)], axis=1)
    coupled_ref[0:half, :] = temp
    exchange = EXCHANGE_RATE * sea_ref[...].astype(F32)
    upper = with_edges(rows_ref[0], edges_ref[0])
    lower = with_edges(rows_ref[1], edges_ref[1])
    heat, moist = exchange * (temp - upper), exchange * (0.5 * temp - lower)
    upper = (upper + heat).astype(BF16).astype(F32)
    lower = (lower + moist).astype(BF16).astype(F32)
    coupled_ref[half : 2 * half, :] = upper
    coupled_ref[2 * half : 3 * half, :] = lower
    halo = []
    for n, (edge, pack) in enumerate(((0, left_pack), (3, right_pack))):
        at = blocks + 2 * n
        warm = jnp.concatenate([by_block[at : at + 1, :], by_block[at + 1 : at + 2, :]], axis=1)
        rate = EXCHANGE_RATE * jnp.concatenate([pack[0:1], pack[1:2]], axis=1)
        u, w = edges_ref[0, edge : edge + 1, :], edges_ref[1, edge : edge + 1, :]
        halo.append((u + rate * (warm - u)).astype(BF16).astype(F32))
        halo.append((w + rate * (0.5 * warm - w)).astype(BF16).astype(F32))
    coupled_ref[3 * half :, :] = jnp.zeros_like(coupled_ref[3 * half :, :])
    for n, line in enumerate(halo):
        coupled_ref[3 * half + n : 3 * half + n + 1, :] = line

    height = vertical_ref.shape[0]
    top, low = height // 2 - 1, height - 1
    cells, width = sea_ref.shape
    sub, lane = iota((cells, width), 0), iota((cells, width), 1)

    def row_of(r, mix, upper, lower):
        a = vertical_ref[pl.ds(r - 7, 8), :].astype(F32)[7:8]
        kept = mix.astype(BF16).astype(F32)
        return (kept + a[:, top : top + 1] * upper + a[:, low : low + 1] * lower).astype(BF16).astype(F32)

    def updated(r, n):
        edges = edges_ref[n]
        center = row_of(r, with_edges(rows_ref[n], edges), upper, lower)
        left = row_of(r, edges[0:1], halo[0], halo[1])
        right = row_of(r, edges[3:4], halo[2], halo[3])
        west = jnp.where(sub == 0, left, pltpu.roll(center, 1, 0))
        east = jnp.where(sub == cells - 1, right, pltpu.roll(center, cells - 1, 0))
        north = jnp.where(lane == width - 1, center, pltpu.roll(center, width - 1, 1))
        south = jnp.where(lane == 0, center, pltpu.roll(center, 1, 1))
        near = east + west + (north + south) - 4.0 * center
        courant = courant_ref[pl.ds(r - 7, 8), :][7:8]
        return center - courant * (center - west) + ATM_DIFFUSION * near

    heat = 0.5 * heat + 0.5 * (exchange * (temp - updated(top, 2)))
    moist = 0.5 * moist + 0.5 * (
        exchange * (0.5 * temp - updated(low, 3))
    )
    flux_rows[...] = jnp.zeros_like(flux_rows)
    for v, flux in enumerate((heat, moist)):
        for h in range(2):
            flux_rows[pl.ds(h * 10 + v, cells, stride=16), :] = flux[:, h * 128 : (h + 1) * 128]
    for x in range(half):
        rows = jnp.concatenate(
            [flux_rows[(2 * x + h) * 8 : (2 * x + h + 1) * 8, :] for h in range(2)], axis=1
        ).astype(BF16)
        weights = jnp.concatenate(
            [
                jnp.concatenate([held[2 * x + h, k] for k in range(sources)], axis=1)
                for h in range(2)
            ],
            axis=0,
        )
        got = jnp.dot(rows, weights, preferred_element_type=F32)
        for k in range(sources):
            at = (k * half + x) * 8
            shares[at : at + 8, :] = got[:, k * 128 : (k + 1) * 128]

    pairs = blocks * sources
    place = place_ref[0:1, :]
    rows = iota((out_ref.shape[0], pairs), 0)
    total = jnp.zeros(out_ref.shape, F32)
    for v in range(2):
        pick = (rows == place + 4 * v).astype(F32).astype(BF16)
        share = jnp.concatenate(
            [shares[pl.ds(2 * h + v, pairs // 2, stride=8), :] for h in range(2)], axis=0
        ).astype(BF16)
        total += jnp.dot(pick, share, preferred_element_type=F32)
    out_ref[...] = total.astype(BF16)
    mixed_going.wait()


def second_step_kernel(
    tiles, odd_ref, mixed_hbm, edge_hbm, courant_ref, vertical_ref, sea_ref, coupled_ref,
    ocean_hbm, _, within_ref, across_ref, ocean_sea_ref, flux_ref, ocean_vertical_ref,
    out_hbm, new_ocean_hbm,
    mixed_ref, edge_ref, state, result, out_ref, ocean_ref, new_ocean_ref,
    in_sems, edge_sem, ocean_sems, out_sems,
):
    edge_copy = pltpu.make_async_copy(edge_hbm, edge_ref, edge_sem)
    edge_copy.start()
    coming = start_all(groups(mixed_hbm, mixed_ref, in_sems))
    ocean_cells = ocean_sea_ref.shape[0]
    near_ends = (0, 1, ocean_cells - 2, ocean_cells - 1)
    ocean_coming = start_all([
        pltpu.make_async_copy(ocean_hbm.at[:, x], ocean_ref.at[n], ocean_sems.at[n])
        for n, x in enumerate(near_ends)
    ])
    cells, height = mixed_ref.shape[0], mixed_ref.shape[1]
    top, low = height // 2 - 1, height - 1
    lateral = lateral_matrix(mixed_ref.shape[2])
    vertical = vertical_ref[...]
    upper_column = vertical[:, top : top + 1].astype(F32)
    lower_column = vertical[:, low : low + 1].astype(F32)
    courant = courant_ref[...]
    halo = 3 * cells

    def complete(to, mixed, upper_at, lower_at):
        upper = coupled_ref[upper_at : upper_at + 1, :]
        lower = coupled_ref[lower_at : lower_at + 1, :]
        done = mixed.astype(F32) + upper_column * upper + lower_column * lower
        state[to] = done.astype(BF16)

    last = iota((8, mixed_ref.shape[2]), 0) == 7

    def advance(x):
        updated = stencil(state[x], state[x + 1], state[x + 2], lateral, courant)
        exchange = EXCHANGE_RATE * sea_ref[x : x + 1, :].astype(F32)
        temp = coupled_ref[x : x + 1, :]
        upper = updated[top - 7 : top + 1]
        lower = updated[low - 7 : low + 1]
        upper = jnp.where(last, upper + exchange * (temp - upper), upper)
        lower = jnp.where(last, lower + exchange * (0.5 * temp - lower), lower)
        forced = jnp.concatenate(
            [updated[: top - 7], upper, updated[top + 1 : low - 7], lower], axis=0
        ).astype(BF16)
        result[x] = jnp.dot(vertical, forced, preferred_element_type=F32).astype(BF16)

    edge_copy.wait()
    coming[0].wait()
    complete(0, edge_ref[0], halo, halo + 1)
    complete(1, edge_ref[1], cells, 2 * cells)
    going = []
    step, half = 32, cells // 2
    for x in range(cells):
        ahead = x + 1
        if ahead % GROUP == 0 and ahead < cells:
            coming[ahead // GROUP].wait()
        if ahead < cells - 1:
            complete(ahead + 1, mixed_ref[ahead], cells + ahead, 2 * cells + ahead)
        elif ahead == cells - 1:
            complete(cells, edge_ref[2], 2 * cells - 1, 3 * cells - 1)
        else:
            complete(cells + 1, edge_ref[3], halo + 2, halo + 3)
        advance(x)
        if (x + 1) % half:
            continue
        across = slice(x + 1 - half, x + 1)
        for i in range(height // step):
            at = slice(i * step, (i + 1) * step)
            out_ref[at, across, :] = jnp.swapaxes(result[across, at, :], 0, 1)
        ends = out_ref.at[:, across], out_hbm.at[:, across]
        going.append(pltpu.make_async_copy(*ends, out_sems.at[(x + 1) // half - 1]))
        going[-1].start()
        if x + 1 == cells:
            break
        wait_all(ocean_coming)
        layers = ocean_ref.shape[1]
        left, right = (
            p[:layers]
            for p in sides(odd_ref, unpack(within_ref[tiles:]), unpack(across_ref[tiles:]))
        )
        known = {-1: left, ocean_cells: right}
        known.update((at, ocean_ref[n]) for n, at in enumerate(near_ends))

        def store(x, value):
            new_ocean_ref[min(x, 1)] = value

        ocean_step(
            [(0, ocean_cells - 1)], known.get, ocean_sea_ref, flux_ref, ocean_vertical_ref, store
        )
        for n, at in enumerate((0, ocean_cells - 1)):
            ends = new_ocean_ref.at[n], new_ocean_hbm.at[:, at]
            going.append(pltpu.make_async_copy(*ends, ocean_sems.at[4 + n]))
            going[-1].start()
    wait_all(going)


def land_kernel(incoming_ref, slots_ref, sea_ref, out_ref, wide):
    devices = slots_ref.shape[1]
    cells = sea_ref.shape[0]
    wide[...] = incoming_ref[...].astype(F32)
    wet = sea_ref[...].astype(F32)
    here = (iota((cells, devices), 0) + 1).astype(F32)
    picks = [(slots_ref[s : s + 1, :] == here).astype(F32).astype(BF16) for s in range(4)]
    for v in range(2):
        total = jnp.zeros((cells, 128), F32)
        for s in range(4):
            part = wide[pl.ds(v * 4 + s, devices, stride=8), :].astype(BF16)
            total += jnp.dot(picks[s], part, preferred_element_type=F32)
        out_ref[v] = total * wet


def swap(within, across):
    peers = lax.axis_size(BOTH)
    pair = [(i, i ^ 1) for i in range(peers)]
    other = [(i, ((i + 1) ^ 1) - 1) for i in range(peers)]
    other = [(i, j % peers) for i, j in other]
    return lax.ppermute(within, BOTH, pair), lax.ppermute(across, BOTH, other)


def per_device(
    atm_state, atm_sea, zonal_courant, atm_vertical, ocean_state, ocean_sea,
    flux_in, ocean_vertical, remap_owner, remap_block, remap_weight,
):
    devices = lax.axis_size(BOTH)
    height, cells, width = atm_state.shape
    blocks, sources = remap_owner.shape
    pairs = blocks * sources
    courant = zonal_courant.reshape(height, 1)
    layers, ocean_cells, ocean_width = ocean_state.shape
    ocean_rows = ocean_state.reshape(layers * ocean_cells, ocean_width)
    owner, block = remap_owner.T, remap_block.T
    odd = is_odd()
    dma = pltpu.SemaphoreType.DMA
    held = [pltpu.VMEM(remap_weight.shape, BF16), dma((PARTS,))]
    whole = pltpu.VMEM((cells, height, width), BF16)
    levels = 64

    head, place = call(
        plan_kernel,
        (shape((devices, HEAD, 128), BF16), shape((8, pairs), jnp.int32)),
        owner, block, ocean_state,
        specs={0: ANY, 1: ANY, 2: ANY},
        scratch=[
            pltpu.VMEM((devices * 8, 128), F32),
            pltpu.VMEM((pairs, 128), F32),
            pltpu.VMEM(owner.shape, jnp.int32),
            pltpu.VMEM(owner.shape, jnp.int32),
            pltpu.VMEM((ocean_cells, ocean_width), F32),
            dma((3,)),
        ],
        limit=58,
        touched=1 << 20,
    )
    gathered = lax.all_to_all(head, BOTH, split_axis=0, concat_axis=0, tiled=True)

    tiles = 2 * sources
    columns_sent = shape((2, height, width), BF16)
    load = shape((tiles + 2 * PACK // 128, 128, 128), BF16)
    state_a, state_b, load_a, load_b, goal = call(
        edges_kernel,
        (columns_sent, columns_sent, load, load, shape((8, 128), F32)),
        odd, atm_state, ocean_state, remap_weight.reshape(pairs, 128, 128), owner, block, atm_sea,
        specs={
            0: SCALAR,
            1: pl.BlockSpec((levels, cells, width), lambda i: (i, 0, 0)),
            2: ANY,
            3: ANY,
        },
        scratch=[pltpu.VMEM((layers, ocean_width), F32)] * 2 + [dma((4,))],
        grid=(height // levels,),
        limit=54,
        touched=6 << 20,
    )
    state_near = swap(state_a, state_b)
    load_near = swap(load_a, load_b)
    mixed, rows, ocean_inside = call(
        first_step_kernel,
        (
            shape((cells, height, width), BF16),
            shape((4, cells, width), F32),
            shape(ocean_rows.shape, F32),
        ),
        atm_state, courant, atm_vertical, ocean_rows, ocean_sea, flux_in, ocean_vertical,
        specs={0: ANY, 3: ANY},
        out_specs={0: ANY, 2: ANY},
        scratch=[
            pltpu.VMEM(ocean_rows.shape, F32),
            pltpu.VMEM(ocean_rows.shape, F32),
            dma((2,)),
            pltpu.VMEM(atm_state.shape, BF16), whole, whole,
            dma((LEVEL_PARTS,)), dma((cells // GROUP,)),
        ],
        limit=53,
        touched=16 << 20,
    )
    coupled, slots, outgoing, mixed_edge = call(
        functools.partial(couple_kernel, layers),
        (
            shape((3 * cells + 8, width), F32),
            shape((8, devices), F32),
            shape((devices * 8, 128), BF16),
            shape((4, height, width), BF16),
        ),
        odd, gathered, goal, *load_near, remap_weight, atm_sea, place,
        rows, *state_near, state_a, state_b, courant, atm_vertical,
        specs={0: SCALAR, 5: ANY},
        out_specs={3: ANY},
        scratch=[
            pltpu.VMEM((devices * 8, 128), F32),
            pltpu.VMEM((128, 128), F32),
            pltpu.VMEM((blocks * 8, 128), F32),
            pltpu.VMEM((pairs * 4, 128), F32),
            pltpu.VMEM((4, 8, width), F32),
            pltpu.VMEM((4, height, width), BF16),
            dma,
            *held,
        ],
        limit=50,
        touched=16 << 20,
    )
    incoming = lax.all_to_all(
        outgoing.reshape(devices, 8, 128), BOTH, split_axis=0, concat_axis=0, tiled=True
    )
    state, new_ocean = call(
        functools.partial(second_step_kernel, tiles),
        (shape(atm_state.shape, BF16), shape(ocean_state.shape, F32)),
        odd, mixed, mixed_edge, courant, atm_vertical, atm_sea, coupled,
        ocean_state, ocean_inside.reshape(ocean_state.shape), *load_near, ocean_sea, flux_in, ocean_vertical,
        specs={0: SCALAR, 1: ANY, 2: ANY, 7: ANY, 8: ANY},
        out_specs={0: ANY, 1: ANY},
        aliases={8: 1},
        scratch=[
            whole,
            pltpu.VMEM((4, height, width), BF16),
            pltpu.VMEM((cells + 2, height, width), BF16),
            whole,
            pltpu.VMEM(atm_state.shape, BF16),
            pltpu.VMEM((4, layers, ocean_width), F32),
            pltpu.VMEM((2, layers, ocean_width), F32),
            dma((cells // GROUP,)),
            dma,
            dma((6,)),
            dma((2,)),
        ],
        limit=53,
        touched=24 << 20,
    )
    ocean_flux = call(
        land_kernel,
        shape((2, ocean_cells, ocean_width), F32),
        incoming.reshape(devices * 8, 128), slots, ocean_sea,
        scratch=[pltpu.VMEM((devices * 8, 128), F32)],
        touched=1 << 20,
    )
    return state, new_ocean, ocean_flux


def solution(mesh):
    return jax.shard_map(
        per_device,
        mesh=mesh,
        in_specs=(
            P(None, BOTH, None), P(BOTH, None), P(), P(), P(None, BOTH, None), P(BOTH, None),
            P(None, BOTH, None), P(), P(BOTH, None), P(BOTH, None), P(BOTH, None, None, None),
        ),
        out_specs=(P(None, BOTH, None), P(None, BOTH, None), P(None, BOTH, None)),
        check_vma=False,
    )
```

```python
import functools

import jax
import jax.numpy as jnp
from jax import lax
from jax.experimental import pallas as pl
from jax.experimental.pallas import tpu as pltpu
from jax.sharding import PartitionSpec as P

ATM_DIFFUSION = 0.1
OCEAN_DIFFUSION = 0.15
EXCHANGE_RATE = 0.3
FLUX_GAIN = 0.5

F32 = jnp.float32
BF16 = jnp.bfloat16
VM = pltpu.VMEM
BOTH = ("comp", "tile")
HEAD = 24


def call(kernel, outs, *args, scratch=(), specs=None, out_specs=None, limit=50, touched=0, grid=(), aliases=None):
    specs, out_specs = specs or {}, out_specs or {}
    single = not isinstance(outs, tuple)
    placed = [
        out_specs.get(i, pl.BlockSpec(memory_space=VM)) for i in range(1 if single else len(outs))
    ]
    return pl.pallas_call(
        kernel,
        out_shape=outs,
        grid=grid,
        in_specs=[specs.get(i, pl.BlockSpec(memory_space=VM)) for i in range(len(args))],
        out_specs=placed[0] if single else tuple(placed),
        scratch_shapes=list(scratch),
        input_output_aliases=aliases or {},
        compiler_params=pltpu.CompilerParams(vmem_limit_bytes=limit << 20),
        cost_estimate=pl.CostEstimate(flops=0, bytes_accessed=touched, transcendentals=0),
    )(*args)


SCALAR = pl.BlockSpec(memory_space=pltpu.SMEM)
ANY = pl.BlockSpec(memory_space=pltpu.HBM)


def start_all(copies):
    for c in copies:
        c.start()
    return copies


def wait_all(copies):
    for c in copies:
        c.wait()


def shape(dims, dtype):
    return jax.ShapeDtypeStruct(dims, dtype)


def iota(dims, axis):
    return lax.broadcasted_iota(jnp.int32, dims, axis)


def columns(ref):
    count, rows = ref.shape
    wide = [jnp.broadcast_to(ref[k : k + 1, :], (128, rows)) for k in range(count)]
    return jnp.concatenate([jnp.transpose(w) for w in wide], axis=0)


def is_odd():
    return jnp.bitwise_and(lax.axis_index("tile"), 1).astype(jnp.int32).reshape(1)


def plan_kernel(
    owner_hbm, block_hbm, ocean_hbm, head_ref, place_ref, slot_rows, places, owner_ref, block_ref, surface_ref, sems
):
    copies = start_all([
        pltpu.make_async_copy(owner_hbm, owner_ref, sems.at[0]),
        pltpu.make_async_copy(block_hbm, block_ref, sems.at[1]),
        pltpu.make_async_copy(ocean_hbm.at[0], surface_ref, sems.at[2]),
    ])
    devices = head_ref.shape[0]
    slot_rows[...] = jnp.zeros_like(slot_rows)
    wait_all(copies)
    owner, block = columns(owner_ref), columns(block_ref)
    pairs = owner.shape[0]
    hits = (owner == iota((pairs, devices), 1)).astype(F32)
    earlier = (iota((pairs, pairs), 1) < iota((pairs, pairs), 0)).astype(F32)
    before = jnp.dot(earlier.astype(BF16), hits.astype(BF16), preferred_element_type=F32)
    slot = jnp.sum(before * hits, axis=1, keepdims=True)
    marked = jnp.where(
        slot == iota((pairs, 128), 1).astype(F32), (block + 1).astype(F32), 0.0
    )
    wanted = jnp.dot(
        jnp.transpose(hits).astype(BF16), marked.astype(BF16), preferred_element_type=F32
    )
    places[...] = owner.astype(F32) * 8.0 + slot
    spread = jnp.transpose(
        jnp.concatenate([places[pl.ds(h, pairs // 2, stride=2), :] for h in range(2)], axis=0)
    )
    place_ref[...] = spread[:8].astype(jnp.int32)
    slot_rows[pl.ds(0, devices, stride=8), :] = wanted
    surface = surface_ref[...].astype(BF16)
    head_ref[:, 0:16, :] = jnp.broadcast_to(surface[None], (devices, 16, 128))
    head_ref[:, 16:24, :] = slot_rows[...].reshape(devices, 8, 128).astype(BF16)


EDGE_PARTS = 8
PACK = 192


def edges_kernel(
    odd_ref, state_hbm, ocean_hbm, weight_hbm, owner_ref, block_ref, sea_ref,
    state_a_ref, state_b_ref, load_a_ref, load_b_ref, goal_ref,
    state_ref, ocean_first, ocean_last, state_sems, sems,
):
    odd = odd_ref[0]
    levels = state_ref.shape[0] // EDGE_PARTS
    coming = start_all([
        pltpu.make_async_copy(
            state_hbm.at[pl.ds(n * levels, levels)],
            state_ref.at[pl.ds(n * levels, levels)],
            state_sems.at[n],
        )
        for n in range(EDGE_PARTS)
    ])
    tiles = 2 * owner_ref.shape[0]
    at_a = (1 - odd) * (weight_hbm.shape[0] - tiles)
    at_b = odd * (weight_hbm.shape[0] - tiles)
    copies = [
        pltpu.make_async_copy(weight_hbm.at[pl.ds(at_a, tiles)], load_a_ref.at[0:tiles], sems.at[0]),
        pltpu.make_async_copy(weight_hbm.at[pl.ds(at_b, tiles)], load_b_ref.at[0:tiles], sems.at[1]),
        pltpu.make_async_copy(ocean_hbm.at[:, 0], ocean_first, sems.at[2]),
        pltpu.make_async_copy(ocean_hbm.at[:, ocean_hbm.shape[1] - 1], ocean_last, sems.at[3]),
    ]
    start_all(copies)
    cells = state_ref.shape[1]
    layers = ocean_first.shape[0]
    goal = (owner_ref[...] * 16 + block_ref[...]).astype(F32)
    goal_ref[...] = jnp.zeros_like(goal_ref)
    goal_ref[0 : goal.shape[0], 0 : goal.shape[1]] = goal
    sea = sea_ref[...].astype(F32)
    width = sea.shape[1] // 2
    row = iota((8, width), 0)
    for n, c in enumerate(coming):
        c.wait()
        at = slice(n * levels, (n + 1) * levels)
        first = jnp.swapaxes(state_ref[at, 0:8, :], 0, 1)[0:2]
        last = jnp.swapaxes(state_ref[at, cells - 8 : cells, :], 0, 1)[6:8]
        state_a_ref[:, at, :], state_b_ref[:, at, :] = sides(odd_ref, first, last)
    wait_all(copies)
    oceans = sides(odd_ref, ocean_first[...], ocean_last[...])
    lines = sides(odd_ref, sea[0:1], sea[cells - 1 : cells])
    for ref, ocean, line in zip((load_a_ref, load_b_ref), oceans, lines):
        halves = jnp.where(row == 0, line[:, :width], jnp.where(row == 1, line[:, width:], 0.0))
        empty = jnp.zeros((PACK - layers - 16, width), F32)
        pack = jnp.concatenate([ocean, halves, goal_ref[...], empty], axis=0)
        high = pack.astype(BF16)
        low = (pack - high.astype(F32)).astype(BF16)
        ref[tiles:] = jnp.concatenate([high, low], axis=0).reshape(
            2 * PACK // width, width, width
        )


def unpack(load):
    both = load.reshape(2 * PACK, load.shape[2]).astype(F32)
    return both[:PACK] + both[PACK:]


def sides(odd_ref, within, across):
    odd = odd_ref[0] == 1
    return jnp.where(odd, within, across), jnp.where(odd, across, within)


def lateral_matrix(size):
    row, col = iota((size, size), 0), iota((size, size), 1)
    near = jnp.where(jnp.abs(row - col) == 1, 1.0, 0.0)
    edge = jnp.where((row == 0) | (row == size - 1), -3.0, -4.0)
    return (near + jnp.where(row == col, edge, 0.0)).astype(BF16)


def without_forced(vertical):
    height = vertical.shape[0]
    col = iota(vertical.shape, 1)
    keep = (col != height // 2 - 1) & (col != height - 1)
    return jnp.where(keep, vertical.astype(F32), 0.0).astype(BF16)


def stencil(west, center, east, lateral, courant):
    w, c, e = west.astype(F32), center.astype(F32), east.astype(F32)
    side = jnp.dot(center, lateral, preferred_element_type=F32)
    return c + courant * (w - c) + ATM_DIFFUSION * (w + e + side)


GROUP = 8
LEVEL_PARTS = 4


def groups(hbm, held, sems, out=False):
    copies = []
    for g in range(held.shape[0] // GROUP):
        at = pl.ds(g * GROUP, GROUP)
        ends = (held.at[at], hbm.at[at]) if out else (hbm.at[at], held.at[at])
        copies.append(pltpu.make_async_copy(*ends, sems.at[g]))
    return copies


def keep_rows(ref, x, updated, mixed):
    height = updated.shape[0]
    for n, (field, r) in enumerate(
        ((updated, height // 2), (updated, height), (mixed, height // 2), (mixed, height))
    ):
        ref[n, x : x + 1, :] = field[r - 1 : r]


def first_step_kernel(
    state_hbm, courant_ref, vertical_ref, ocean_hbm, ocean_sea_ref, flux_ref, ocean_vertical_ref,
    mixed_hbm, rows_ref, new_ocean_hbm, ocean_ref, new_ocean_ref, ocean_sems, state, turned, mixed_out, in_sems, out_sems,
):
    levels = state.shape[0] // LEVEL_PARTS
    coming = start_all([
        pltpu.make_async_copy(
            state_hbm.at[pl.ds(n * levels, levels)], state.at[pl.ds(n * levels, levels)], in_sems.at[n]
        )
        for n in range(LEVEL_PARTS)
    ])
    ocean_coming = pltpu.make_async_copy(ocean_hbm, ocean_ref, ocean_sems.at[0])
    ocean_coming.start()
    going = groups(mixed_hbm, mixed_out, out_sems, out=True)
    cells, height = turned.shape[0], turned.shape[1]
    lateral = lateral_matrix(turned.shape[2])
    vertical = without_forced(vertical_ref[...])
    courant = courant_ref[...]

    def body(x):
        updated = stencil(turned[x - 1], turned[x], turned[x + 1], lateral, courant)
        mixed = jnp.dot(vertical, updated.astype(BF16), preferred_element_type=F32)
        keep_rows(rows_ref, x, updated, mixed)
        mixed_out[x] = mixed.astype(BF16)

    for x in (0, cells - 1):
        mixed_out[x] = jnp.zeros_like(mixed_out[x])
        rows_ref[:, x : x + 1, :] = jnp.zeros_like(rows_ref[:, x : x + 1, :])
    step = 32
    for n, c in enumerate(coming):
        c.wait()
        for at in range(n * levels, (n + 1) * levels, step):
            turned[:, at : at + step, :] = jnp.swapaxes(state[at : at + step], 0, 1)
    for g in range(cells // GROUP):
        for x in range(max(1, g * GROUP), min(cells - 1, (g + 1) * GROUP)):
            body(x)
        going[g].start()
        if (g + 1) * GROUP != cells // 2:
            continue
        ocean_coming.wait()
        ocean_cells = ocean_sea_ref.shape[0]
        layers = ocean_ref.shape[0] // ocean_cells

        def column(x):
            return pl.ds(x, layers, stride=ocean_cells), slice(None)

        def store(x, value):
            new_ocean_ref[column(x)] = value

        for x in (0, ocean_cells - 1):
            store(x, jnp.zeros((layers, ocean_ref.shape[1]), F32))
        ocean_step(
            [(x, x + 1) for x in range(1, ocean_cells - 1, 2)],
            lambda x: ocean_ref[column(x)],
            ocean_sea_ref, flux_ref, ocean_vertical_ref, store,
        )
        going.append(pltpu.make_async_copy(new_ocean_ref, new_ocean_hbm, ocean_sems.at[1]))
        going[-1].start()
    wait_all(going)


def edge_columns(left, right, first, last, courant, vertical, keep, mixed_out):
    lateral = lateral_matrix(first.shape[2])
    vertical = without_forced(vertical)
    before = [left[0], left[1], first[0], first[1]]
    after = [last[0], last[1], right[0], right[1]]
    keep[...] = jnp.zeros_like(keep)
    for i, columns_of in enumerate((before[:3], before[1:], after[:3], after[1:])):
        updated = stencil(*columns_of, lateral, courant)
        mixed = jnp.dot(vertical, updated.astype(BF16), preferred_element_type=F32)
        keep_rows(keep, i, updated, mixed)
        mixed_out[i] = mixed.astype(BF16)


def with_edges(main, edges):
    cells = main.shape[0]
    at = iota(main.shape, 0)
    return jnp.where(at == 0, edges[1:2], jnp.where(at == cells - 1, edges[2:3], main))


def ocean_step(pairs, column, sea_ref, flux_ref, vertical_ref, store):
    width = sea_ref.shape[1]
    height = vertical_ref.shape[0]
    vertical = vertical_ref[...]
    high = vertical.astype(BF16)
    low = (vertical - high.astype(F32)).astype(BF16)
    both = jnp.concatenate([high, low], axis=0)
    lane = iota((height, width), 1)
    row = iota((height, width), 0)

    def forced(x):
        west, center, east = column(x - 1), column(x), column(x + 1)
        north = jnp.where(lane == width - 1, center, pltpu.roll(center, width - 1, 1))
        south = jnp.where(lane == 0, center, pltpu.roll(center, 1, 1))
        wet = sea_ref[x : x + 1, :].astype(F32)
        near = east + west + (north + south) - 4.0 * center
        heat = FLUX_GAIN * wet * flux_ref[0, x : x + 1, :]
        fresh = FLUX_GAIN * wet * flux_ref[1, x : x + 1, :]
        added = jnp.where(row == 0, heat, jnp.where(row == height // 2, fresh, 0.0))
        return (center + OCEAN_DIFFUSION * near) * wet + added

    for pair in pairs:
        updated = jnp.concatenate([forced(x) for x in pair], axis=1)
        upper = updated.astype(BF16)
        rest = (updated - upper.astype(F32)).astype(BF16)
        mixed = jnp.dot(both, upper, preferred_element_type=F32)
        mixed = mixed[:height] + mixed[height:]
        mixed += jnp.dot(high, rest, preferred_element_type=F32)
        for n, x in enumerate(pair):
            store(x, mixed[:, n * width : (n + 1) * width])


PARTS = 8


def weight_copies(weight_hbm, held, sems):
    step = weight_hbm.shape[0] // PARTS
    return start_all([
        pltpu.make_async_copy(
            weight_hbm.at[pl.ds(i * step, step)], held.at[pl.ds(i * step, step)], sems.at[i]
        )
        for i in range(PARTS)
    ])


def couple_kernel(
    layers,
    odd_ref, head_ref, goal_ref, within_ref, across_ref, weight_hbm, sea_ref, place_ref,
    rows_ref, near_within_ref, near_across_ref, own_a_ref, own_b_ref, courant_ref, vertical_ref, _,
    coupled_ref, slots_ref, out_ref, mixed_hbm, ocean_hbm,
    slot_rows, by_block, flux_rows, shares, edges_ref, mixed_out, ocean_out, out_sems, held, sems,
):
    copies = weight_copies(weight_hbm, held, sems)
    edge_columns(
        *sides(odd_ref, near_within_ref[...], near_across_ref[...]),
        *sides(odd_ref, own_a_ref[...], own_b_ref[...]),
        courant_ref[...], vertical_ref[...], edges_ref, mixed_out,
    )
    going = [pltpu.make_async_copy(
        mixed_out, mixed_hbm.at[pl.ds(sea_ref.shape[0], 4)], out_sems.at[0]
    )]
    going[0].start()
    devices = head_ref.shape[0]
    blocks, sources = held.shape[0], held.shape[1]
    surface = head_ref[:, 0:16, :].reshape(devices * 16, 128)
    slot_rows[...] = head_ref[:, 16:24, :].astype(F32).reshape(devices * 8, 128)
    slots_ref[...] = jnp.transpose(slot_rows[pl.ds(0, devices, stride=8), :])[:8]

    tiles = 2 * sources
    packs = sides(odd_ref, unpack(within_ref[tiles:]), unpack(across_ref[tiles:]))
    for n in range(2):
        ocean_out[n] = packs[n][:layers]
    going.append(pltpu.make_async_copy(ocean_out, ocean_hbm, out_sems.at[1]))
    going[1].start()
    left_pack, right_pack = (p[layers : layers + 16] for p in packs)
    lane = iota((8, 128), 1)
    goals = jnp.where(
        lane < blocks,
        goal_ref[...],
        jnp.where(
            lane < blocks + 2,
            pltpu.roll(left_pack[8:], 2, 1),
            jnp.where(lane < blocks + 4, pltpu.roll(right_pack[8:], blocks + 2, 1), -1.0),
        ),
    )
    count = blocks + 8
    goal = jnp.concatenate(
        [
            jnp.transpose(jnp.broadcast_to(goals[k : k + 1], (128, 128)))[:count, :1]
            for k in range(sources)
        ],
        axis=0,
    ).astype(jnp.int32)
    pick = (goal == iota((sources * count, devices * 16), 1)).astype(F32).astype(BF16)
    fetched = jnp.dot(pick, surface, preferred_element_type=F32)
    empty = jnp.zeros((128 - count, 128), F32)
    wanted = jnp.concatenate(
        [
            jnp.transpose(jnp.concatenate([fetched[k * count : (k + 1) * count], empty], axis=0))
            for k in range(sources)
        ],
        axis=0,
    ).astype(BF16)
    lane = iota((128, 128), 1)

    def add(j, weights, total):
        rows = jnp.concatenate(weights, axis=1)
        return jnp.where(lane == j, jnp.dot(rows, wanted, preferred_element_type=F32), total)

    total = jnp.zeros((128, 128), F32)
    for n, weights in enumerate(sides(odd_ref, within_ref[0:tiles], across_ref[0:tiles])):
        for b in range(2):
            total = add(
                blocks + 2 * n + b, [weights[b * sources + k] for k in range(sources)], total
            )
    step = blocks // PARTS
    for i, c in enumerate(copies):
        c.wait()
        for j in range(i * step, (i + 1) * step):
            total = add(j, [held[j, k] for k in range(sources)], total)
    by_block[...] = jnp.transpose(total)

    half = blocks // 2
    temp = jnp.concatenate([by_block[pl.ds(h, half, stride=2), :] for h in range(2)], axis=1)
    coupled_ref[0:half, :] = temp
    exchange = EXCHANGE_RATE * sea_ref[...].astype(F32)
    upper = with_edges(rows_ref[0], edges_ref[0])
    lower = with_edges(rows_ref[1], edges_ref[1])
    heat, moist = exchange * (temp - upper), exchange * (0.5 * temp - lower)
    upper = (upper + heat).astype(BF16).astype(F32)
    lower = (lower + moist).astype(BF16).astype(F32)
    coupled_ref[half : 2 * half, :] = upper
    coupled_ref[2 * half : 3 * half, :] = lower
    halo = []
    for n, (edge, pack) in enumerate(((0, left_pack), (3, right_pack))):
        at = blocks + 2 * n
        warm = jnp.concatenate([by_block[at : at + 1, :], by_block[at + 1 : at + 2, :]], axis=1)
        rate = EXCHANGE_RATE * jnp.concatenate([pack[0:1], pack[1:2]], axis=1)
        u, w = edges_ref[0, edge : edge + 1, :], edges_ref[1, edge : edge + 1, :]
        halo.append((u + rate * (warm - u)).astype(BF16).astype(F32))
        halo.append((w + rate * (0.5 * warm - w)).astype(BF16).astype(F32))
    coupled_ref[3 * half :, :] = jnp.zeros_like(coupled_ref[3 * half :, :])
    for n, line in enumerate(halo):
        coupled_ref[3 * half + n : 3 * half + n + 1, :] = line

    height = vertical_ref.shape[0]
    top, low = height // 2 - 1, height - 1
    cells, width = sea_ref.shape
    sub, lane = iota((cells, width), 0), iota((cells, width), 1)

    def row_of(r, mix, upper, lower):
        a = vertical_ref[pl.ds(r - 7, 8), :].astype(F32)[7:8]
        kept = mix.astype(BF16).astype(F32)
        return (kept + a[:, top : top + 1] * upper + a[:, low : low + 1] * lower).astype(BF16).astype(F32)

    def updated(r, n):
        edges = edges_ref[n]
        center = row_of(r, with_edges(rows_ref[n], edges), upper, lower)
        left = row_of(r, edges[0:1], halo[0], halo[1])
        right = row_of(r, edges[3:4], halo[2], halo[3])
        west = jnp.where(sub == 0, left, pltpu.roll(center, 1, 0))
        east = jnp.where(sub == cells - 1, right, pltpu.roll(center, cells - 1, 0))
        north = jnp.where(lane == width - 1, center, pltpu.roll(center, width - 1, 1))
        south = jnp.where(lane == 0, center, pltpu.roll(center, 1, 1))
        near = east + west + (north + south) - 4.0 * center
        courant = courant_ref[pl.ds(r - 7, 8), :][7:8]
        return center - courant * (center - west) + ATM_DIFFUSION * near

    heat = 0.5 * heat + 0.5 * (exchange * (temp - updated(top, 2)))
    moist = 0.5 * moist + 0.5 * (
        exchange * (0.5 * temp - updated(low, 3))
    )
    flux_rows[...] = jnp.zeros_like(flux_rows)
    for v, flux in enumerate((heat, moist)):
        for h in range(2):
            flux_rows[pl.ds(h * 10 + v, cells, stride=16), :] = flux[:, h * 128 : (h + 1) * 128]
    for x in range(half):
        rows = jnp.concatenate(
            [flux_rows[(2 * x + h) * 8 : (2 * x + h + 1) * 8, :] for h in range(2)], axis=1
        ).astype(BF16)
        weights = jnp.concatenate(
            [
                jnp.concatenate([held[2 * x + h, k] for k in range(sources)], axis=1)
                for h in range(2)
            ],
            axis=0,
        )
        got = jnp.dot(rows, weights, preferred_element_type=F32)
        for k in range(sources):
            at = (k * half + x) * 8
            shares[at : at + 8, :] = got[:, k * 128 : (k + 1) * 128]

    pairs = blocks * sources
    place = place_ref[0:1, :]
    rows = iota((out_ref.shape[0], pairs), 0)
    total = jnp.zeros(out_ref.shape, F32)
    for v in range(2):
        pick = (rows == place + 4 * v).astype(F32).astype(BF16)
        share = jnp.concatenate(
            [shares[pl.ds(2 * h + v, pairs // 2, stride=8), :] for h in range(2)], axis=0
        ).astype(BF16)
        total += jnp.dot(pick, share, preferred_element_type=F32)
    out_ref[...] = total.astype(BF16)
    wait_all(going)


def second_step_kernel(
    mixed_hbm, courant_ref, vertical_ref, sea_ref, coupled_ref,
    ocean_hbm, _, ocean_halo_hbm, ocean_sea_ref, flux_ref, ocean_vertical_ref,
    out_hbm, new_ocean_hbm,
    mixed_ref, edge_ref, state, result, out_ref, ocean_ref, ocean_halo_ref, new_ocean_ref,
    in_sems, edge_sem, ocean_sems, out_sems,
):
    edge_copy = pltpu.make_async_copy(
        mixed_hbm.at[pl.ds(mixed_ref.shape[0], 4)], edge_ref, edge_sem
    )
    edge_copy.start()
    coming = start_all(groups(mixed_hbm, mixed_ref, in_sems))
    ocean_cells = ocean_sea_ref.shape[0]
    near_ends = (0, 1, ocean_cells - 2, ocean_cells - 1)
    ocean_coming = start_all([
        pltpu.make_async_copy(ocean_hbm.at[:, x], ocean_ref.at[n], ocean_sems.at[n])
        for n, x in enumerate(near_ends)
    ] + [pltpu.make_async_copy(ocean_halo_hbm, ocean_halo_ref, ocean_sems.at[6])])
    cells, height = mixed_ref.shape[0], mixed_ref.shape[1]
    top, low = height // 2 - 1, height - 1
    lateral = lateral_matrix(mixed_ref.shape[2])
    vertical = vertical_ref[...]
    upper_column = vertical[:, top : top + 1].astype(F32)
    lower_column = vertical[:, low : low + 1].astype(F32)
    courant = courant_ref[...]
    halo = 3 * cells

    def complete(to, mixed, upper_at, lower_at):
        upper = coupled_ref[upper_at : upper_at + 1, :]
        lower = coupled_ref[lower_at : lower_at + 1, :]
        done = mixed.astype(F32) + upper_column * upper + lower_column * lower
        state[to] = done.astype(BF16)

    last = iota((8, mixed_ref.shape[2]), 0) == 7

    def advance(x):
        updated = stencil(state[x], state[x + 1], state[x + 2], lateral, courant)
        exchange = EXCHANGE_RATE * sea_ref[x : x + 1, :].astype(F32)
        temp = coupled_ref[x : x + 1, :]
        upper = updated[top - 7 : top + 1]
        lower = updated[low - 7 : low + 1]
        upper = jnp.where(last, upper + exchange * (temp - upper), upper)
        lower = jnp.where(last, lower + exchange * (0.5 * temp - lower), lower)
        forced = jnp.concatenate(
            [updated[: top - 7], upper, updated[top + 1 : low - 7], lower], axis=0
        ).astype(BF16)
        result[x] = jnp.dot(vertical, forced, preferred_element_type=F32).astype(BF16)

    edge_copy.wait()
    coming[0].wait()
    complete(0, edge_ref[0], halo, halo + 1)
    complete(1, edge_ref[1], cells, 2 * cells)
    going = []
    step, half = 32, cells // 2
    for x in range(cells):
        ahead = x + 1
        if ahead % GROUP == 0 and ahead < cells:
            coming[ahead // GROUP].wait()
        if ahead < cells - 1:
            complete(ahead + 1, mixed_ref[ahead], cells + ahead, 2 * cells + ahead)
        elif ahead == cells - 1:
            complete(cells, edge_ref[2], 2 * cells - 1, 3 * cells - 1)
        else:
            complete(cells + 1, edge_ref[3], halo + 2, halo + 3)
        advance(x)
        if (x + 1) % half:
            continue
        across = slice(x + 1 - half, x + 1)
        for i in range(height // step):
            at = slice(i * step, (i + 1) * step)
            out_ref[at, across, :] = jnp.swapaxes(result[across, at, :], 0, 1)
        ends = out_ref.at[:, across], out_hbm.at[:, across]
        going.append(pltpu.make_async_copy(*ends, out_sems.at[(x + 1) // half - 1]))
        going[-1].start()
        if x + 1 == cells:
            break
        wait_all(ocean_coming)
        known = {-1: ocean_halo_ref[0], ocean_cells: ocean_halo_ref[1]}
        known.update((at, ocean_ref[n]) for n, at in enumerate(near_ends))

        def store(x, value):
            new_ocean_ref[min(x, 1)] = value

        ocean_step(
            [(0, ocean_cells - 1)], known.get, ocean_sea_ref, flux_ref, ocean_vertical_ref, store
        )
        for n, at in enumerate((0, ocean_cells - 1)):
            ends = new_ocean_ref.at[n], new_ocean_hbm.at[:, at]
            going.append(pltpu.make_async_copy(*ends, ocean_sems.at[4 + n]))
            going[-1].start()
    wait_all(going)


def land_kernel(incoming_ref, slots_ref, sea_ref, out_ref, wide):
    devices = slots_ref.shape[1]
    cells = sea_ref.shape[0]
    wide[...] = incoming_ref[...].astype(F32)
    wet = sea_ref[...].astype(F32)
    here = (iota((cells, devices), 0) + 1).astype(F32)
    picks = [(slots_ref[s : s + 1, :] == here).astype(F32).astype(BF16) for s in range(4)]
    for v in range(2):
        total = jnp.zeros((cells, 128), F32)
        for s in range(4):
            part = wide[pl.ds(v * 4 + s, devices, stride=8), :].astype(BF16)
            total += jnp.dot(picks[s], part, preferred_element_type=F32)
        out_ref[v] = total * wet


def swap(within, across):
    peers = lax.axis_size(BOTH)
    pair = [(i, i ^ 1) for i in range(peers)]
    other = [(i, ((i + 1) ^ 1) - 1) for i in range(peers)]
    other = [(i, j % peers) for i, j in other]
    return lax.ppermute(within, BOTH, pair), lax.ppermute(across, BOTH, other)


def per_device(
    atm_state, atm_sea, zonal_courant, atm_vertical, ocean_state, ocean_sea,
    flux_in, ocean_vertical, remap_owner, remap_block, remap_weight,
):
    devices = lax.axis_size(BOTH)
    height, cells, width = atm_state.shape
    blocks, sources = remap_owner.shape
    pairs = blocks * sources
    courant = zonal_courant.reshape(height, 1)
    layers, ocean_cells, ocean_width = ocean_state.shape
    ocean_rows = ocean_state.reshape(layers * ocean_cells, ocean_width)
    owner, block = remap_owner.T, remap_block.T
    odd = is_odd()
    dma = pltpu.SemaphoreType.DMA
    held = [pltpu.VMEM(remap_weight.shape, BF16), dma((PARTS,))]
    whole = pltpu.VMEM((cells, height, width), BF16)

    head, place = call(
        plan_kernel,
        (shape((devices, HEAD, 128), BF16), shape((8, pairs), jnp.int32)),
        owner, block, ocean_state,
        specs={0: ANY, 1: ANY, 2: ANY},
        scratch=[
            pltpu.VMEM((devices * 8, 128), F32),
            pltpu.VMEM((pairs, 128), F32),
            pltpu.VMEM(owner.shape, jnp.int32),
            pltpu.VMEM(owner.shape, jnp.int32),
            pltpu.VMEM((ocean_cells, ocean_width), F32),
            dma((3,)),
        ],
        limit=58,
        touched=1 << 20,
    )
    gathered = lax.all_to_all(head, BOTH, split_axis=0, concat_axis=0, tiled=True)

    tiles = 2 * sources
    columns_sent = shape((2, height, width), BF16)
    load = shape((tiles + 2 * PACK // 128, 128, 128), BF16)
    state_a, state_b, load_a, load_b, goal = call(
        edges_kernel,
        (columns_sent, columns_sent, load, load, shape((8, 128), F32)),
        odd, atm_state, ocean_state, remap_weight.reshape(pairs, 128, 128), owner, block, atm_sea,
        specs={
            0: SCALAR,
            1: ANY,
            2: ANY,
            3: ANY,
        },
        scratch=[
            pltpu.VMEM(atm_state.shape, BF16),
            pltpu.VMEM((layers, ocean_width), F32),
            pltpu.VMEM((layers, ocean_width), F32),
            dma((EDGE_PARTS,)),
            dma((4,)),
        ],
        limit=54,
        touched=6 << 20,
    )
    state_near = swap(state_a, state_b)
    load_near = swap(load_a, load_b)
    mixed, rows, ocean_inside = call(
        first_step_kernel,
        (
            shape((cells + 4, height, width), BF16),
            shape((4, cells, width), F32),
            shape(ocean_rows.shape, F32),
        ),
        atm_state, courant, atm_vertical, ocean_rows, ocean_sea, flux_in, ocean_vertical,
        specs={0: ANY, 3: ANY},
        out_specs={0: ANY, 2: ANY},
        scratch=[
            pltpu.VMEM(ocean_rows.shape, F32),
            pltpu.VMEM(ocean_rows.shape, F32),
            dma((2,)),
            pltpu.VMEM(atm_state.shape, BF16), whole, whole,
            dma((LEVEL_PARTS,)), dma((cells // GROUP,)),
        ],
        limit=53,
        touched=16 << 20,
    )
    coupled, slots, outgoing, mixed, ocean_halo = call(
        functools.partial(couple_kernel, layers),
        (
            shape((3 * cells + 8, width), F32),
            shape((8, devices), F32),
            shape((devices * 8, 128), BF16),
            shape(mixed.shape, BF16),
            shape((2, layers, ocean_width), F32),
        ),
        odd, gathered, goal, *load_near, remap_weight, atm_sea, place,
        rows, *state_near, state_a, state_b, courant, atm_vertical, mixed,
        specs={0: SCALAR, 5: ANY, 15: ANY},
        aliases={15: 3},
        out_specs={3: ANY, 4: ANY},
        scratch=[
            pltpu.VMEM((devices * 8, 128), F32),
            pltpu.VMEM((128, 128), F32),
            pltpu.VMEM((blocks * 8, 128), F32),
            pltpu.VMEM((pairs * 4, 128), F32),
            pltpu.VMEM((4, 8, width), F32),
            pltpu.VMEM((4, height, width), BF16),
            pltpu.VMEM((2, layers, ocean_width), F32),
            dma((2,)),
            *held,
        ],
        limit=50,
        touched=16 << 20,
    )
    incoming = lax.all_to_all(
        outgoing.reshape(devices, 8, 128), BOTH, split_axis=0, concat_axis=0, tiled=True
    )
    state, new_ocean = call(
        second_step_kernel,
        (shape(atm_state.shape, BF16), shape(ocean_state.shape, F32)),
        mixed, courant, atm_vertical, atm_sea, coupled,
        ocean_state, ocean_inside.reshape(ocean_state.shape), ocean_halo, ocean_sea, flux_in, ocean_vertical,
        specs={0: ANY, 5: ANY, 6: ANY, 7: ANY},
        out_specs={0: ANY, 1: ANY},
        aliases={6: 1},
        scratch=[
            whole,
            pltpu.VMEM((4, height, width), BF16),
            pltpu.VMEM((cells + 2, height, width), BF16),
            whole,
            pltpu.VMEM(atm_state.shape, BF16),
            pltpu.VMEM((4, layers, ocean_width), F32),
            pltpu.VMEM((2, layers, ocean_width), F32),
            pltpu.VMEM((2, layers, ocean_width), F32),
            dma((cells // GROUP,)),
            dma,
            dma((7,)),
            dma((2,)),
        ],
        limit=53,
        touched=24 << 20,
    )
    ocean_flux = call(
        land_kernel,
        shape((2, ocean_cells, ocean_width), F32),
        incoming.reshape(devices * 8, 128), slots, ocean_sea,
        scratch=[pltpu.VMEM((devices * 8, 128), F32)],
        touched=1 << 20,
    )
    return state, new_ocean, ocean_flux


def solution(mesh):
    return jax.shard_map(
        per_device,
        mesh=mesh,
        in_specs=(
            P(None, BOTH, None), P(BOTH, None), P(), P(), P(None, BOTH, None), P(BOTH, None),
            P(None, BOTH, None), P(), P(BOTH, None), P(BOTH, None), P(BOTH, None, None, None),
        ),
        out_specs=(P(None, BOTH, None), P(None, BOTH, None), P(None, BOTH, None)),
        check_vma=False,
    )
```

```python
import functools

import jax
import jax.numpy as jnp
from jax import lax
from jax.experimental import pallas as pl
from jax.experimental.pallas import tpu as pltpu
from jax.sharding import PartitionSpec as P

ATM_DIFFUSION = 0.1
OCEAN_DIFFUSION = 0.15
EXCHANGE_RATE = 0.3
FLUX_GAIN = 0.5

F32 = jnp.float32
BF16 = jnp.bfloat16
VM = pltpu.VMEM
BOTH = ("comp", "tile")
HEAD = 24


def call(kernel, outs, *args, scratch=(), specs=None, out_specs=None, limit=50, touched=0, grid=(), aliases=None):
    specs, out_specs = specs or {}, out_specs or {}
    single = not isinstance(outs, tuple)
    placed = [
        out_specs.get(i, pl.BlockSpec(memory_space=VM)) for i in range(1 if single else len(outs))
    ]
    return pl.pallas_call(
        kernel,
        out_shape=outs,
        grid=grid,
        in_specs=[specs.get(i, pl.BlockSpec(memory_space=VM)) for i in range(len(args))],
        out_specs=placed[0] if single else tuple(placed),
        scratch_shapes=list(scratch),
        input_output_aliases=aliases or {},
        compiler_params=pltpu.CompilerParams(vmem_limit_bytes=limit << 20),
        cost_estimate=pl.CostEstimate(flops=0, bytes_accessed=touched, transcendentals=0),
    )(*args)


SCALAR = pl.BlockSpec(memory_space=pltpu.SMEM)
ANY = pl.BlockSpec(memory_space=pltpu.HBM)


def start_all(copies):
    for c in copies:
        c.start()
    return copies


def wait_all(copies):
    for c in copies:
        c.wait()


def shape(dims, dtype):
    return jax.ShapeDtypeStruct(dims, dtype)


def iota(dims, axis):
    return lax.broadcasted_iota(jnp.int32, dims, axis)


def columns(ref):
    count, rows = ref.shape
    wide = [jnp.broadcast_to(ref[k : k + 1, :], (128, rows)) for k in range(count)]
    return jnp.concatenate([jnp.transpose(w) for w in wide], axis=0)


def is_odd():
    return jnp.bitwise_and(lax.axis_index("tile"), 1).astype(jnp.int32).reshape(1)


def plan_kernel(
    owner_hbm, block_hbm, ocean_hbm, head_ref, place_ref, slot_rows, places, owner_ref, block_ref, surface_ref, sems
):
    copies = start_all([
        pltpu.make_async_copy(owner_hbm, owner_ref, sems.at[0]),
        pltpu.make_async_copy(block_hbm, block_ref, sems.at[1]),
        pltpu.make_async_copy(ocean_hbm.at[0], surface_ref, sems.at[2]),
    ])
    devices = head_ref.shape[0]
    slot_rows[...] = jnp.zeros_like(slot_rows)
    wait_all(copies)
    owner, block = columns(owner_ref), columns(block_ref)
    pairs = owner.shape[0]
    hits = (owner == iota((pairs, devices), 1)).astype(F32)
    earlier = (iota((pairs, pairs), 1) < iota((pairs, pairs), 0)).astype(F32)
    before = jnp.dot(earlier.astype(BF16), hits.astype(BF16), preferred_element_type=F32)
    slot = jnp.sum(before * hits, axis=1, keepdims=True)
    marked = jnp.where(
        slot == iota((pairs, 128), 1).astype(F32), (block + 1).astype(F32), 0.0
    )
    wanted = jnp.dot(
        jnp.transpose(hits).astype(BF16), marked.astype(BF16), preferred_element_type=F32
    )
    places[...] = owner.astype(F32) * 8.0 + slot
    spread = jnp.transpose(
        jnp.concatenate([places[pl.ds(h, pairs // 2, stride=2), :] for h in range(2)], axis=0)
    )
    place_ref[...] = spread[:8].astype(jnp.int32)
    slot_rows[pl.ds(0, devices, stride=8), :] = wanted
    surface = surface_ref[...].astype(BF16)
    head_ref[:, 0:16, :] = jnp.broadcast_to(surface[None], (devices, 16, 128))
    head_ref[:, 16:24, :] = slot_rows[...].reshape(devices, 8, 128).astype(BF16)


EDGE_PARTS = 8


def edges_kernel(
    odd_ref, state_hbm, ocean_hbm, weight_hbm, owner_ref, block_ref, sea_ref,
    state_a_ref, state_b_ref, load_a_ref, load_b_ref, goal_ref,
    state_ref, ocean_first, ocean_last, names, state_sems, sems,
):
    odd = odd_ref[0]
    levels = state_ref.shape[0] // EDGE_PARTS
    coming = start_all([
        pltpu.make_async_copy(
            state_hbm.at[pl.ds(n * levels, levels)],
            state_ref.at[pl.ds(n * levels, levels)],
            state_sems.at[n],
        )
        for n in range(EDGE_PARTS)
    ])
    size = 2 * owner_ref.shape[0] * 128
    at_a = pl.multiple_of((1 - odd) * (weight_hbm.shape[0] - size), 128)
    at_b = pl.multiple_of(odd * (weight_hbm.shape[0] - size), 128)
    copies = [
        pltpu.make_async_copy(weight_hbm.at[pl.ds(at_a, size)], load_a_ref.at[0:size], sems.at[0]),
        pltpu.make_async_copy(weight_hbm.at[pl.ds(at_b, size)], load_b_ref.at[0:size], sems.at[1]),
        pltpu.make_async_copy(ocean_hbm.at[:, 0], ocean_first, sems.at[2]),
        pltpu.make_async_copy(ocean_hbm.at[:, ocean_hbm.shape[1] - 1], ocean_last, sems.at[3]),
    ]
    start_all(copies)
    cells = state_ref.shape[1]
    count, blocks = owner_ref.shape
    names[...] = jnp.zeros_like(names)
    names[0:count, 0:blocks] = owner_ref[...].astype(F32)
    names[count : 2 * count, 0:blocks] = block_ref[...].astype(F32)
    goal_ref[...] = goal_of(names[...])
    sea = sea_ref[...].astype(F32)
    width = sea.shape[1] // 2
    row = iota((8, width), 0)
    for n, c in enumerate(coming):
        c.wait()
        at = slice(n * levels, (n + 1) * levels)
        first = jnp.swapaxes(state_ref[at, 0:8, :], 0, 1)[0:2]
        last = jnp.swapaxes(state_ref[at, cells - 8 : cells, :], 0, 1)[6:8]
        state_a_ref[:, at, :], state_b_ref[:, at, :] = sides(odd_ref, first, last)
    wait_all(copies)
    oceans = sides(odd_ref, ocean_first[...], ocean_last[...])
    lines = sides(odd_ref, sea[0:1], sea[cells - 1 : cells])
    for ref, ocean, line in zip((load_a_ref, load_b_ref), oceans, lines):
        halves = jnp.where(row == 0, line[:, :width], jnp.where(row == 1, line[:, width:], 0.0))
        pack = jnp.concatenate([ocean, halves, names[...]], axis=0)
        ref[size:, :] = pack.astype(BF16)


def goal_of(names):
    return 16.0 * names + pltpu.roll(names, names.shape[0] // 2, 0)


def sides(odd_ref, within, across):
    odd = odd_ref[0] == 1
    return jnp.where(odd, within, across), jnp.where(odd, across, within)


def lateral_matrix(size):
    row, col = iota((size, size), 0), iota((size, size), 1)
    near = jnp.where(jnp.abs(row - col) == 1, 1.0, 0.0)
    edge = jnp.where((row == 0) | (row == size - 1), -3.0, -4.0)
    return (near + jnp.where(row == col, edge, 0.0)).astype(BF16)


def without_forced(vertical):
    height = vertical.shape[0]
    col = iota(vertical.shape, 1)
    keep = (col != height // 2 - 1) & (col != height - 1)
    return jnp.where(keep, vertical.astype(F32), 0.0).astype(BF16)


def stencil(west, center, east, lateral, courant):
    w, c, e = west.astype(F32), center.astype(F32), east.astype(F32)
    side = jnp.dot(center, lateral, preferred_element_type=F32)
    return c + courant * (w - c) + ATM_DIFFUSION * (w + e + side)


GROUP = 8
LEVEL_PARTS = 4


def groups(hbm, held, sems, out=False):
    copies = []
    for g in range(held.shape[0] // GROUP):
        at = pl.ds(g * GROUP, GROUP)
        ends = (held.at[at], hbm.at[at]) if out else (hbm.at[at], held.at[at])
        copies.append(pltpu.make_async_copy(*ends, sems.at[g]))
    return copies


def keep_rows(ref, x, updated, mixed):
    height = updated.shape[0]
    for n, (field, r) in enumerate(
        ((updated, height // 2), (updated, height), (mixed, height // 2), (mixed, height))
    ):
        ref[n, x : x + 1, :] = field[r - 1 : r]


def first_step_kernel(
    state_hbm, courant_ref, vertical_ref, ocean_hbm, ocean_sea_ref, flux_ref, ocean_vertical_ref,
    mixed_hbm, rows_ref, new_ocean_hbm, ocean_ref, new_ocean_ref, ocean_sems, state, turned, mixed_out, in_sems, out_sems,
):
    levels = state.shape[0] // LEVEL_PARTS
    coming = start_all([
        pltpu.make_async_copy(
            state_hbm.at[pl.ds(n * levels, levels)], state.at[pl.ds(n * levels, levels)], in_sems.at[n]
        )
        for n in range(LEVEL_PARTS)
    ])
    ocean_coming = pltpu.make_async_copy(ocean_hbm, ocean_ref, ocean_sems.at[0])
    ocean_coming.start()
    going = groups(mixed_hbm, mixed_out, out_sems, out=True)
    cells, height = turned.shape[0], turned.shape[1]
    lateral = lateral_matrix(turned.shape[2])
    vertical = without_forced(vertical_ref[...])
    courant = courant_ref[...]

    def body(x):
        updated = stencil(turned[x - 1], turned[x], turned[x + 1], lateral, courant)
        mixed = jnp.dot(vertical, updated.astype(BF16), preferred_element_type=F32)
        keep_rows(rows_ref, x, updated, mixed)
        mixed_out[x] = mixed.astype(BF16)

    for x in (0, cells - 1):
        mixed_out[x] = jnp.zeros_like(mixed_out[x])
        rows_ref[:, x : x + 1, :] = jnp.zeros_like(rows_ref[:, x : x + 1, :])
    step = 32
    for n, c in enumerate(coming):
        c.wait()
        for at in range(n * levels, (n + 1) * levels, step):
            turned[:, at : at + step, :] = jnp.swapaxes(state[at : at + step], 0, 1)
    for g in range(cells // GROUP):
        for x in range(max(1, g * GROUP), min(cells - 1, (g + 1) * GROUP)):
            body(x)
        going[g].start()
        if (g + 1) * GROUP != cells // 2:
            continue
        ocean_coming.wait()
        ocean_cells = ocean_sea_ref.shape[0]
        layers = ocean_ref.shape[0] // ocean_cells

        def column(x):
            return pl.ds(x, layers, stride=ocean_cells), slice(None)

        def store(x, value):
            new_ocean_ref[column(x)] = value

        for x in (0, ocean_cells - 1):
            store(x, jnp.zeros((layers, ocean_ref.shape[1]), F32))
        ocean_step(
            [(x, x + 1) for x in range(1, ocean_cells - 1, 2)],
            lambda x: ocean_ref[column(x)],
            ocean_sea_ref, flux_ref, ocean_vertical_ref, store,
        )
        going.append(pltpu.make_async_copy(new_ocean_ref, new_ocean_hbm, ocean_sems.at[1]))
        going[-1].start()
    wait_all(going)


def edge_columns(left, right, first, last, courant, vertical, keep, mixed_out):
    lateral = lateral_matrix(first.shape[2])
    vertical = without_forced(vertical)
    before = [left[0], left[1], first[0], first[1]]
    after = [last[0], last[1], right[0], right[1]]
    keep[...] = jnp.zeros_like(keep)
    for i, columns_of in enumerate((before[:3], before[1:], after[:3], after[1:])):
        updated = stencil(*columns_of, lateral, courant)
        mixed = jnp.dot(vertical, updated.astype(BF16), preferred_element_type=F32)
        keep_rows(keep, i, updated, mixed)
        mixed_out[i] = mixed.astype(BF16)


def with_edges(main, edges):
    cells = main.shape[0]
    at = iota(main.shape, 0)
    return jnp.where(at == 0, edges[1:2], jnp.where(at == cells - 1, edges[2:3], main))


def ocean_step(pairs, column, sea_ref, flux_ref, vertical_ref, store):
    width = sea_ref.shape[1]
    height = vertical_ref.shape[0]
    vertical = vertical_ref[...]
    high = vertical.astype(BF16)
    low = (vertical - high.astype(F32)).astype(BF16)
    both = jnp.concatenate([high, low], axis=0)
    lane = iota((height, width), 1)
    row = iota((height, width), 0)

    def forced(x):
        west, center, east = column(x - 1), column(x), column(x + 1)
        north = jnp.where(lane == width - 1, center, pltpu.roll(center, width - 1, 1))
        south = jnp.where(lane == 0, center, pltpu.roll(center, 1, 1))
        wet = sea_ref[x : x + 1, :].astype(F32)
        near = east + west + (north + south) - 4.0 * center
        heat = FLUX_GAIN * wet * flux_ref[0, x : x + 1, :]
        fresh = FLUX_GAIN * wet * flux_ref[1, x : x + 1, :]
        added = jnp.where(row == 0, heat, jnp.where(row == height // 2, fresh, 0.0))
        return (center + OCEAN_DIFFUSION * near) * wet + added

    for pair in pairs:
        updated = jnp.concatenate([forced(x) for x in pair], axis=1)
        upper = updated.astype(BF16)
        rest = (updated - upper.astype(F32)).astype(BF16)
        mixed = jnp.dot(both, upper, preferred_element_type=F32)
        mixed = mixed[:height] + mixed[height:]
        mixed += jnp.dot(high, rest, preferred_element_type=F32)
        for n, x in enumerate(pair):
            store(x, mixed[:, n * width : (n + 1) * width])


PARTS = 8


def weight_copies(weight_hbm, held, sems):
    step = weight_hbm.shape[0] // PARTS
    return start_all([
        pltpu.make_async_copy(
            weight_hbm.at[pl.ds(i * step, step)], held.at[pl.ds(i * step, step)], sems.at[i]
        )
        for i in range(PARTS)
    ])


def couple_kernel(
    layers,
    odd_ref, head_ref, goal_ref, within_ref, across_ref, weight_hbm, sea_ref, place_ref,
    rows_ref, near_within_ref, near_across_ref, own_a_ref, own_b_ref, courant_ref, vertical_ref, _,
    coupled_ref, slots_ref, out_ref, mixed_hbm, ocean_hbm,
    slot_rows, by_block, flux_rows, shares, edges_ref, mixed_out, ocean_out, out_sems, held, sems,
):
    copies = weight_copies(weight_hbm, held, sems)
    edge_columns(
        *sides(odd_ref, near_within_ref[...], near_across_ref[...]),
        *sides(odd_ref, own_a_ref[...], own_b_ref[...]),
        courant_ref[...], vertical_ref[...], edges_ref, mixed_out,
    )
    going = [pltpu.make_async_copy(
        mixed_out, mixed_hbm.at[pl.ds(sea_ref.shape[0], 4)], out_sems.at[0]
    )]
    going[0].start()
    devices = head_ref.shape[0]
    blocks, sources = held.shape[0], held.shape[1]
    surface = head_ref[:, 0:16, :].reshape(devices * 16, 128)
    slot_rows[...] = head_ref[:, 16:24, :].astype(F32).reshape(devices * 8, 128)
    slots_ref[...] = jnp.transpose(slot_rows[pl.ds(0, devices, stride=8), :])[:8]

    size = 2 * sources * 128
    packs = sides(
        odd_ref, within_ref[size:, :].astype(F32), across_ref[size:, :].astype(F32)
    )
    for n in range(2):
        ocean_out[n] = packs[n][:layers]
    going.append(pltpu.make_async_copy(ocean_out, ocean_hbm, out_sems.at[1]))
    going[1].start()
    left_pack, right_pack = (p[layers : layers + 16] for p in packs)
    lane = iota((8, 128), 1)
    goals = jnp.where(
        lane < blocks,
        goal_ref[...],
        jnp.where(
            lane < blocks + 2,
            pltpu.roll(goal_of(left_pack[8:]), 2, 1),
            jnp.where(lane < blocks + 4, pltpu.roll(goal_of(right_pack[8:]), blocks + 2, 1), -1.0),
        ),
    )
    count = blocks + 8
    goal = jnp.concatenate(
        [
            jnp.transpose(jnp.broadcast_to(goals[k : k + 1], (128, 128)))[:count, :1]
            for k in range(sources)
        ],
        axis=0,
    ).astype(jnp.int32)
    pick = (goal == iota((sources * count, devices * 16), 1)).astype(F32).astype(BF16)
    fetched = jnp.dot(pick, surface, preferred_element_type=F32)
    empty = jnp.zeros((128 - count, 128), F32)
    wanted = jnp.concatenate(
        [
            jnp.transpose(jnp.concatenate([fetched[k * count : (k + 1) * count], empty], axis=0))
            for k in range(sources)
        ],
        axis=0,
    ).astype(BF16)
    lane = iota((128, 128), 1)

    def add(j, weights, total):
        rows = jnp.concatenate(weights, axis=1)
        return jnp.where(lane == j, jnp.dot(rows, wanted, preferred_element_type=F32), total)

    total = jnp.zeros((128, 128), F32)
    for n, weights in enumerate(sides(odd_ref, within_ref[0:size, :], across_ref[0:size, :])):
        tiles = [weights[t * 128 : (t + 1) * 128] for t in range(2 * sources)]
        for b in range(2):
            total = add(blocks + 2 * n + b, tiles[b * sources : (b + 1) * sources], total)
    step = blocks // PARTS
    for i, c in enumerate(copies):
        c.wait()
        for j in range(i * step, (i + 1) * step):
            total = add(j, [held[j, k] for k in range(sources)], total)
    by_block[...] = jnp.transpose(total)

    half = blocks // 2
    temp = jnp.concatenate([by_block[pl.ds(h, half, stride=2), :] for h in range(2)], axis=1)
    coupled_ref[0:half, :] = temp
    exchange = EXCHANGE_RATE * sea_ref[...].astype(F32)
    upper = with_edges(rows_ref[0], edges_ref[0])
    lower = with_edges(rows_ref[1], edges_ref[1])
    heat, moist = exchange * (temp - upper), exchange * (0.5 * temp - lower)
    upper = (upper + heat).astype(BF16).astype(F32)
    lower = (lower + moist).astype(BF16).astype(F32)
    coupled_ref[half : 2 * half, :] = upper
    coupled_ref[2 * half : 3 * half, :] = lower
    halo = []
    for n, (edge, pack) in enumerate(((0, left_pack), (3, right_pack))):
        at = blocks + 2 * n
        warm = jnp.concatenate([by_block[at : at + 1, :], by_block[at + 1 : at + 2, :]], axis=1)
        rate = EXCHANGE_RATE * jnp.concatenate([pack[0:1], pack[1:2]], axis=1)
        u, w = edges_ref[0, edge : edge + 1, :], edges_ref[1, edge : edge + 1, :]
        halo.append((u + rate * (warm - u)).astype(BF16).astype(F32))
        halo.append((w + rate * (0.5 * warm - w)).astype(BF16).astype(F32))
    coupled_ref[3 * half :, :] = jnp.zeros_like(coupled_ref[3 * half :, :])
    for n, line in enumerate(halo):
        coupled_ref[3 * half + n : 3 * half + n + 1, :] = line

    height = vertical_ref.shape[0]
    top, low = height // 2 - 1, height - 1
    cells, width = sea_ref.shape
    sub, lane = iota((cells, width), 0), iota((cells, width), 1)

    def row_of(r, mix, upper, lower):
        a = vertical_ref[pl.ds(r - 7, 8), :].astype(F32)[7:8]
        kept = mix.astype(BF16).astype(F32)
        return (kept + a[:, top : top + 1] * upper + a[:, low : low + 1] * lower).astype(BF16).astype(F32)

    def updated(r, n):
        edges = edges_ref[n]
        center = row_of(r, with_edges(rows_ref[n], edges), upper, lower)
        left = row_of(r, edges[0:1], halo[0], halo[1])
        right = row_of(r, edges[3:4], halo[2], halo[3])
        west = jnp.where(sub == 0, left, pltpu.roll(center, 1, 0))
        east = jnp.where(sub == cells - 1, right, pltpu.roll(center, cells - 1, 0))
        north = jnp.where(lane == width - 1, center, pltpu.roll(center, width - 1, 1))
        south = jnp.where(lane == 0, center, pltpu.roll(center, 1, 1))
        near = east + west + (north + south) - 4.0 * center
        courant = courant_ref[pl.ds(r - 7, 8), :][7:8]
        return center - courant * (center - west) + ATM_DIFFUSION * near

    heat = 0.5 * heat + 0.5 * (exchange * (temp - updated(top, 2)))
    moist = 0.5 * moist + 0.5 * (
        exchange * (0.5 * temp - updated(low, 3))
    )
    flux_rows[...] = jnp.zeros_like(flux_rows)
    for v, flux in enumerate((heat, moist)):
        for h in range(2):
            flux_rows[pl.ds(h * 10 + v, cells, stride=16), :] = flux[:, h * 128 : (h + 1) * 128]
    for x in range(half):
        rows = jnp.concatenate(
            [flux_rows[(2 * x + h) * 8 : (2 * x + h + 1) * 8, :] for h in range(2)], axis=1
        ).astype(BF16)
        weights = jnp.concatenate(
            [
                jnp.concatenate([held[2 * x + h, k] for k in range(sources)], axis=1)
                for h in range(2)
            ],
            axis=0,
        )
        got = jnp.dot(rows, weights, preferred_element_type=F32)
        for k in range(sources):
            at = (k * half + x) * 8
            shares[at : at + 8, :] = got[:, k * 128 : (k + 1) * 128]

    pairs = blocks * sources
    place = place_ref[0:1, :]
    rows = iota((out_ref.shape[0], pairs), 0)
    total = jnp.zeros(out_ref.shape, F32)
    for v in range(2):
        pick = (rows == place + 4 * v).astype(F32).astype(BF16)
        share = jnp.concatenate(
            [shares[pl.ds(2 * h + v, pairs // 2, stride=8), :] for h in range(2)], axis=0
        ).astype(BF16)
        total += jnp.dot(pick, share, preferred_element_type=F32)
    out_ref[...] = total.astype(BF16)
    wait_all(going)


def second_step_kernel(
    mixed_hbm, courant_ref, vertical_ref, sea_ref, coupled_ref,
    ocean_hbm, _, ocean_halo_hbm, ocean_sea_ref, flux_ref, ocean_vertical_ref,
    out_hbm, new_ocean_hbm,
    mixed_ref, edge_ref, state, result, out_ref, ocean_ref, ocean_halo_ref, new_ocean_ref,
    in_sems, edge_sem, ocean_sems, out_sems,
):
    edge_copy = pltpu.make_async_copy(
        mixed_hbm.at[pl.ds(mixed_ref.shape[0], 4)], edge_ref, edge_sem
    )
    edge_copy.start()
    coming = start_all(groups(mixed_hbm, mixed_ref, in_sems))
    ocean_cells = ocean_sea_ref.shape[0]
    near_ends = (0, 1, ocean_cells - 2, ocean_cells - 1)
    ocean_coming = start_all([
        pltpu.make_async_copy(ocean_hbm.at[:, x], ocean_ref.at[n], ocean_sems.at[n])
        for n, x in enumerate(near_ends)
    ] + [pltpu.make_async_copy(ocean_halo_hbm, ocean_halo_ref, ocean_sems.at[6])])
    cells, height = mixed_ref.shape[0], mixed_ref.shape[1]
    top, low = height // 2 - 1, height - 1
    lateral = lateral_matrix(mixed_ref.shape[2])
    vertical = vertical_ref[...]
    upper_column = vertical[:, top : top + 1].astype(F32)
    lower_column = vertical[:, low : low + 1].astype(F32)
    courant = courant_ref[...]
    halo = 3 * cells

    def complete(to, mixed, upper_at, lower_at):
        upper = coupled_ref[upper_at : upper_at + 1, :]
        lower = coupled_ref[lower_at : lower_at + 1, :]
        done = mixed.astype(F32) + upper_column * upper + lower_column * lower
        state[to] = done.astype(BF16)

    last = iota((8, mixed_ref.shape[2]), 0) == 7

    def advance(x):
        updated = stencil(state[x], state[x + 1], state[x + 2], lateral, courant)
        exchange = EXCHANGE_RATE * sea_ref[x : x + 1, :].astype(F32)
        temp = coupled_ref[x : x + 1, :]
        upper = updated[top - 7 : top + 1]
        lower = updated[low - 7 : low + 1]
        upper = jnp.where(last, upper + exchange * (temp - upper), upper)
        lower = jnp.where(last, lower + exchange * (0.5 * temp - lower), lower)
        forced = jnp.concatenate(
            [updated[: top - 7], upper, updated[top + 1 : low - 7], lower], axis=0
        ).astype(BF16)
        result[x] = jnp.dot(vertical, forced, preferred_element_type=F32).astype(BF16)

    edge_copy.wait()
    coming[0].wait()
    complete(0, edge_ref[0], halo, halo + 1)
    complete(1, edge_ref[1], cells, 2 * cells)
    going = []
    step, half = 32, cells // 2
    for x in range(cells):
        ahead = x + 1
        if ahead % GROUP == 0 and ahead < cells:
            coming[ahead // GROUP].wait()
        if ahead < cells - 1:
            complete(ahead + 1, mixed_ref[ahead], cells + ahead, 2 * cells + ahead)
        elif ahead == cells - 1:
            complete(cells, edge_ref[2], 2 * cells - 1, 3 * cells - 1)
        else:
            complete(cells + 1, edge_ref[3], halo + 2, halo + 3)
        advance(x)
        if (x + 1) % half:
            continue
        across = slice(x + 1 - half, x + 1)
        for i in range(height // step):
            at = slice(i * step, (i + 1) * step)
            out_ref[at, across, :] = jnp.swapaxes(result[across, at, :], 0, 1)
        ends = out_ref.at[:, across], out_hbm.at[:, across]
        going.append(pltpu.make_async_copy(*ends, out_sems.at[(x + 1) // half - 1]))
        going[-1].start()
        if x + 1 == cells:
            break
        wait_all(ocean_coming)
        known = {-1: ocean_halo_ref[0], ocean_cells: ocean_halo_ref[1]}
        known.update((at, ocean_ref[n]) for n, at in enumerate(near_ends))

        def store(x, value):
            new_ocean_ref[min(x, 1)] = value

        ocean_step(
            [(0, ocean_cells - 1)], known.get, ocean_sea_ref, flux_ref, ocean_vertical_ref, store
        )
        for n, at in enumerate((0, ocean_cells - 1)):
            ends = new_ocean_ref.at[n], new_ocean_hbm.at[:, at]
            going.append(pltpu.make_async_copy(*ends, ocean_sems.at[4 + n]))
            going[-1].start()
    wait_all(going)


def land_kernel(incoming_ref, slots_ref, sea_ref, out_ref, wide):
    devices = slots_ref.shape[1]
    cells = sea_ref.shape[0]
    wide[...] = incoming_ref[...].astype(F32)
    wet = sea_ref[...].astype(F32)
    here = (iota((cells, devices), 0) + 1).astype(F32)
    picks = [(slots_ref[s : s + 1, :] == here).astype(F32).astype(BF16) for s in range(4)]
    for v in range(2):
        total = jnp.zeros((cells, 128), F32)
        for s in range(4):
            part = wide[pl.ds(v * 4 + s, devices, stride=8), :].astype(BF16)
            total += jnp.dot(picks[s], part, preferred_element_type=F32)
        out_ref[v] = total * wet


def swap(within, across):
    peers = lax.axis_size(BOTH)
    pair = [(i, i ^ 1) for i in range(peers)]
    other = [(i, ((i + 1) ^ 1) - 1) for i in range(peers)]
    other = [(i, j % peers) for i, j in other]
    return lax.ppermute(within, BOTH, pair), lax.ppermute(across, BOTH, other)


def per_device(
    atm_state, atm_sea, zonal_courant, atm_vertical, ocean_state, ocean_sea,
    flux_in, ocean_vertical, remap_owner, remap_block, remap_weight,
):
    devices = lax.axis_size(BOTH)
    height, cells, width = atm_state.shape
    blocks, sources = remap_owner.shape
    pairs = blocks * sources
    courant = zonal_courant.reshape(height, 1)
    layers, ocean_cells, ocean_width = ocean_state.shape
    ocean_rows = ocean_state.reshape(layers * ocean_cells, ocean_width)
    owner, block = remap_owner.T, remap_block.T
    odd = is_odd()
    dma = pltpu.SemaphoreType.DMA
    held = [pltpu.VMEM(remap_weight.shape, BF16), dma((PARTS,))]
    whole = pltpu.VMEM((cells, height, width), BF16)

    head, place = call(
        plan_kernel,
        (shape((devices, HEAD, 128), BF16), shape((8, pairs), jnp.int32)),
        owner, block, ocean_state,
        specs={0: ANY, 1: ANY, 2: ANY},
        scratch=[
            pltpu.VMEM((devices * 8, 128), F32),
            pltpu.VMEM((pairs, 128), F32),
            pltpu.VMEM(owner.shape, jnp.int32),
            pltpu.VMEM(owner.shape, jnp.int32),
            pltpu.VMEM((ocean_cells, ocean_width), F32),
            dma((3,)),
        ],
        limit=58,
        touched=1 << 20,
    )
    gathered = lax.all_to_all(head, BOTH, split_axis=0, concat_axis=0, tiled=True)

    columns_sent = shape((2, height, width), BF16)
    load = shape((2 * sources * 128 + layers + 16, 128), BF16)
    state_a, state_b, load_a, load_b, goal = call(
        edges_kernel,
        (columns_sent, columns_sent, load, load, shape((8, 128), F32)),
        odd, atm_state, ocean_state, remap_weight.reshape(pairs * 128, 128), owner, block, atm_sea,
        specs={
            0: SCALAR,
            1: ANY,
            2: ANY,
            3: ANY,
        },
        scratch=[
            pltpu.VMEM(atm_state.shape, BF16),
            pltpu.VMEM((layers, ocean_width), F32),
            pltpu.VMEM((layers, ocean_width), F32),
            pltpu.VMEM((8, 128), F32),
            dma((EDGE_PARTS,)),
            dma((4,)),
        ],
        limit=54,
        touched=6 << 20,
    )
    state_near = swap(state_a, state_b)
    load_near = swap(load_a, load_b)
    mixed, rows, ocean_inside = call(
        first_step_kernel,
        (
            shape((cells + 4, height, width), BF16),
            shape((4, cells, width), F32),
            shape(ocean_rows.shape, F32),
        ),
        atm_state, courant, atm_vertical, ocean_rows, ocean_sea, flux_in, ocean_vertical,
        specs={0: ANY, 3: ANY},
        out_specs={0: ANY, 2: ANY},
        scratch=[
            pltpu.VMEM(ocean_rows.shape, F32),
            pltpu.VMEM(ocean_rows.shape, F32),
            dma((2,)),
            pltpu.VMEM(atm_state.shape, BF16), whole, whole,
            dma((LEVEL_PARTS,)), dma((cells // GROUP,)),
        ],
        limit=53,
        touched=16 << 20,
    )
    coupled, slots, outgoing, mixed, ocean_halo = call(
        functools.partial(couple_kernel, layers),
        (
            shape((3 * cells + 8, width), F32),
            shape((8, devices), F32),
            shape((devices * 8, 128), BF16),
            shape(mixed.shape, BF16),
            shape((2, layers, ocean_width), F32),
        ),
        odd, gathered, goal, *load_near, remap_weight, atm_sea, place,
        rows, *state_near, state_a, state_b, courant, atm_vertical, mixed,
        specs={0: SCALAR, 5: ANY, 15: ANY},
        aliases={15: 3},
        out_specs={3: ANY, 4: ANY},
        scratch=[
            pltpu.VMEM((devices * 8, 128), F32),
            pltpu.VMEM((128, 128), F32),
            pltpu.VMEM((blocks * 8, 128), F32),
            pltpu.VMEM((pairs * 4, 128), F32),
            pltpu.VMEM((4, 8, width), F32),
            pltpu.VMEM((4, height, width), BF16),
            pltpu.VMEM((2, layers, ocean_width), F32),
            dma((2,)),
            *held,
        ],
        limit=50,
        touched=16 << 20,
    )
    incoming = lax.all_to_all(
        outgoing.reshape(devices, 8, 128), BOTH, split_axis=0, concat_axis=0, tiled=True
    )
    state, new_ocean = call(
        second_step_kernel,
        (shape(atm_state.shape, BF16), shape(ocean_state.shape, F32)),
        mixed, courant, atm_vertical, atm_sea, coupled,
        ocean_state, ocean_inside.reshape(ocean_state.shape), ocean_halo, ocean_sea, flux_in, ocean_vertical,
        specs={0: ANY, 5: ANY, 6: ANY, 7: ANY},
        out_specs={0: ANY, 1: ANY},
        aliases={6: 1},
        scratch=[
            whole,
            pltpu.VMEM((4, height, width), BF16),
            pltpu.VMEM((cells + 2, height, width), BF16),
            whole,
            pltpu.VMEM(atm_state.shape, BF16),
            pltpu.VMEM((4, layers, ocean_width), F32),
            pltpu.VMEM((2, layers, ocean_width), F32),
            pltpu.VMEM((2, layers, ocean_width), F32),
            dma((cells // GROUP,)),
            dma,
            dma((7,)),
            dma((2,)),
        ],
        limit=53,
        touched=24 << 20,
    )
    ocean_flux = call(
        land_kernel,
        shape((2, ocean_cells, ocean_width), F32),
        incoming.reshape(devices * 8, 128), slots, ocean_sea,
        scratch=[pltpu.VMEM((devices * 8, 128), F32)],
        touched=1 << 20,
    )
    return state, new_ocean, ocean_flux


def solution(mesh):
    return jax.shard_map(
        per_device,
        mesh=mesh,
        in_specs=(
            P(None, BOTH, None), P(BOTH, None), P(), P(), P(None, BOTH, None), P(BOTH, None),
            P(None, BOTH, None), P(), P(BOTH, None), P(BOTH, None), P(BOTH, None, None, None),
        ),
        out_specs=(P(None, BOTH, None), P(None, BOTH, None), P(None, BOTH, None)),
        check_vma=False,
    )
```

```python
import functools

import jax
import jax.numpy as jnp
from jax import lax
from jax.experimental import pallas as pl
from jax.experimental.pallas import tpu as pltpu
from jax.sharding import PartitionSpec as P

ATM_DIFFUSION = 0.1
OCEAN_DIFFUSION = 0.15
EXCHANGE_RATE = 0.3
FLUX_GAIN = 0.5

F32 = jnp.float32
BF16 = jnp.bfloat16
VM = pltpu.VMEM
BOTH = ("comp", "tile")
HEAD = 24


def call(kernel, outs, *args, scratch=(), specs=None, out_specs=None, limit=50, touched=0, grid=()):
    specs, out_specs = specs or {}, out_specs or {}
    single = not isinstance(outs, tuple)
    placed = [
        out_specs.get(i, pl.BlockSpec(memory_space=VM)) for i in range(1 if single else len(outs))
    ]
    return pl.pallas_call(
        kernel,
        out_shape=outs,
        grid=grid,
        in_specs=[specs.get(i, pl.BlockSpec(memory_space=VM)) for i in range(len(args))],
        out_specs=placed[0] if single else tuple(placed),
        scratch_shapes=list(scratch),
        compiler_params=pltpu.CompilerParams(vmem_limit_bytes=limit << 20),
        cost_estimate=pl.CostEstimate(flops=0, bytes_accessed=touched, transcendentals=0),
    )(*args)


SCALAR = pl.BlockSpec(memory_space=pltpu.SMEM)
ANY = pl.BlockSpec(memory_space=pltpu.HBM)


def start_all(copies):
    for c in copies:
        c.start()
    return copies


def wait_all(copies):
    for c in copies:
        c.wait()


def shape(dims, dtype):
    return jax.ShapeDtypeStruct(dims, dtype)


def iota(dims, axis):
    return lax.broadcasted_iota(jnp.int32, dims, axis)


def columns(ref):
    count, rows = ref.shape
    wide = [jnp.broadcast_to(ref[k : k + 1, :], (128, rows)) for k in range(count)]
    return jnp.concatenate([jnp.transpose(w) for w in wide], axis=0)


def is_odd():
    return jnp.bitwise_and(lax.axis_index("tile"), 1).astype(jnp.int32).reshape(1)


def plan_kernel(
    owner_hbm, block_hbm, ocean_hbm, head_ref, place_ref, slot_rows, places, owner_ref, block_ref, surface_ref, sems
):
    copies = start_all([
        pltpu.make_async_copy(owner_hbm, owner_ref, sems.at[0]),
        pltpu.make_async_copy(block_hbm, block_ref, sems.at[1]),
        pltpu.make_async_copy(ocean_hbm.at[0], surface_ref, sems.at[2]),
    ])
    devices = head_ref.shape[0]
    slot_rows[...] = jnp.zeros_like(slot_rows)
    wait_all(copies)
    owner, block = columns(owner_ref), columns(block_ref)
    pairs = owner.shape[0]
    hits = (owner == iota((pairs, devices), 1)).astype(F32)
    earlier = (iota((pairs, pairs), 1) < iota((pairs, pairs), 0)).astype(F32)
    before = jnp.dot(earlier.astype(BF16), hits.astype(BF16), preferred_element_type=F32)
    slot = jnp.sum(before * hits, axis=1, keepdims=True)
    marked = jnp.where(
        slot == iota((pairs, 128), 1).astype(F32), (block + 1).astype(F32), 0.0
    )
    wanted = jnp.dot(
        jnp.transpose(hits).astype(BF16), marked.astype(BF16), preferred_element_type=F32
    )
    places[...] = owner.astype(F32) * 8.0 + slot
    spread = jnp.transpose(
        jnp.concatenate([places[pl.ds(h, pairs // 2, stride=2), :] for h in range(2)], axis=0)
    )
    place_ref[...] = spread[:8].astype(jnp.int32)
    slot_rows[pl.ds(0, devices, stride=8), :] = wanted
    surface = surface_ref[...].astype(BF16)
    head_ref[:, 0:16, :] = jnp.broadcast_to(surface[None], (devices, 16, 128))
    head_ref[:, 16:24, :] = slot_rows[...].reshape(devices, 8, 128).astype(BF16)


PACK = 192


def edges_kernel(
    odd_ref, state_ref, ocean_hbm, weight_hbm, owner_ref, block_ref, sea_ref,
    state_a_ref, state_b_ref, load_a_ref, load_b_ref, goal_ref,
    ocean_first, ocean_last, sems,
):
    i, odd = pl.program_id(0), odd_ref[0]
    tiles = 2 * owner_ref.shape[0]
    at_a = (1 - odd) * (weight_hbm.shape[0] - tiles)
    at_b = odd * (weight_hbm.shape[0] - tiles)
    copies = [
        pltpu.make_async_copy(weight_hbm.at[pl.ds(at_a, tiles)], load_a_ref.at[0:tiles], sems.at[0]),
        pltpu.make_async_copy(weight_hbm.at[pl.ds(at_b, tiles)], load_b_ref.at[0:tiles], sems.at[1]),
        pltpu.make_async_copy(ocean_hbm.at[:, 0], ocean_first, sems.at[2]),
        pltpu.make_async_copy(ocean_hbm.at[:, ocean_hbm.shape[1] - 1], ocean_last, sems.at[3]),
    ]
    pl.when(i == 0)(lambda: (start_all(copies), None)[1])
    rows, cells = state_ref.shape[0], state_ref.shape[1]
    first = jnp.swapaxes(state_ref[:, 0:8, :], 0, 1)[0:2]
    last = jnp.swapaxes(state_ref[:, cells - 8 : cells, :], 0, 1)[6:8]
    at = pl.ds(pl.multiple_of(i * rows, rows), rows)
    state_a_ref[:, at, :], state_b_ref[:, at, :] = sides(odd_ref, first, last)

    @pl.when(i == pl.num_programs(0) - 1)
    def _():
        layers = ocean_first.shape[0]
        goal = (owner_ref[...] * 16 + block_ref[...]).astype(F32)
        goal_ref[...] = jnp.zeros_like(goal_ref)
        goal_ref[0 : goal.shape[0], 0 : goal.shape[1]] = goal
        sea = sea_ref[...].astype(F32)
        width = sea.shape[1] // 2
        row = iota((8, width), 0)
        wait_all(copies)
        oceans = sides(odd_ref, ocean_first[...], ocean_last[...])
        lines = sides(odd_ref, sea[0:1], sea[cells - 1 : cells])
        for ref, ocean, line in zip((load_a_ref, load_b_ref), oceans, lines):
            halves = jnp.where(row == 0, line[:, :width], jnp.where(row == 1, line[:, width:], 0.0))
            empty = jnp.zeros((PACK - layers - 16, width), F32)
            pack = jnp.concatenate([ocean, halves, goal_ref[...], empty], axis=0)
            high = pack.astype(BF16)
            low = (pack - high.astype(F32)).astype(BF16)
            ref[tiles:] = jnp.concatenate([high, low], axis=0).reshape(
                2 * PACK // width, width, width
            )


def unpack(load):
    both = load.reshape(2 * PACK, load.shape[2]).astype(F32)
    return both[:PACK] + both[PACK:]


def sides(odd_ref, within, across):
    odd = odd_ref[0] == 1
    return jnp.where(odd, within, across), jnp.where(odd, across, within)


def lateral_matrix(size):
    row, col = iota((size, size), 0), iota((size, size), 1)
    near = jnp.where(jnp.abs(row - col) == 1, 1.0, 0.0)
    edge = jnp.where((row == 0) | (row == size - 1), -3.0, -4.0)
    return (near + jnp.where(row == col, edge, 0.0)).astype(BF16)


def without_forced(vertical):
    height = vertical.shape[0]
    col = iota(vertical.shape, 1)
    keep = (col != height // 2 - 1) & (col != height - 1)
    return jnp.where(keep, vertical.astype(F32), 0.0).astype(BF16)


def stencil(west, center, east, lateral, courant):
    w, c, e = west.astype(F32), center.astype(F32), east.astype(F32)
    side = jnp.dot(center, lateral, preferred_element_type=F32)
    return c + courant * (w - c) + ATM_DIFFUSION * (w + e + side)


GROUP = 8
LEVEL_PARTS = 4


def groups(hbm, held, sems, out=False):
    copies = []
    for g in range(held.shape[0] // GROUP):
        at = pl.ds(g * GROUP, GROUP)
        ends = (held.at[at], hbm.at[at]) if out else (hbm.at[at], held.at[at])
        copies.append(pltpu.make_async_copy(*ends, sems.at[g]))
    return copies


def keep_rows(ref, x, updated, mixed):
    height = updated.shape[0]
    for n, (field, r) in enumerate(
        ((updated, height // 2), (updated, height), (mixed, height // 2), (mixed, height))
    ):
        ref[n, x : x + 1, :] = field[r - 1 : r]


def first_step_kernel(
    state_hbm, courant_ref, vertical_ref, mixed_hbm, rows_ref, state, turned, mixed_out, in_sems, out_sems,
):
    levels = state.shape[0] // LEVEL_PARTS
    coming = start_all([
        pltpu.make_async_copy(
            state_hbm.at[pl.ds(n * levels, levels)], state.at[pl.ds(n * levels, levels)], in_sems.at[n]
        )
        for n in range(LEVEL_PARTS)
    ])
    going = groups(mixed_hbm, mixed_out, out_sems, out=True)
    cells, height = turned.shape[0], turned.shape[1]
    lateral = lateral_matrix(turned.shape[2])
    vertical = without_forced(vertical_ref[...])
    courant = courant_ref[...]

    def body(x):
        updated = stencil(turned[x - 1], turned[x], turned[x + 1], lateral, courant)
        mixed = jnp.dot(vertical, updated.astype(BF16), preferred_element_type=F32)
        keep_rows(rows_ref, x, updated, mixed)
        mixed_out[x] = mixed.astype(BF16)

    for x in (0, cells - 1):
        mixed_out[x] = jnp.zeros_like(mixed_out[x])
        rows_ref[:, x : x + 1, :] = jnp.zeros_like(rows_ref[:, x : x + 1, :])
    step = 32
    for n, c in enumerate(coming):
        c.wait()
        for at in range(n * levels, (n + 1) * levels, step):
            turned[:, at : at + step, :] = jnp.swapaxes(state[at : at + step], 0, 1)
    for g in range(cells // GROUP):
        for x in range(max(1, g * GROUP), min(cells - 1, (g + 1) * GROUP)):
            body(x)
        going[g].start()
    wait_all(going)


def first_edges_kernel(
    odd_ref, within_ref, across_ref, own_a_ref, own_b_ref, courant_ref, vertical_ref,
    mixed_hbm, rows_ref, mixed_out, sem,
):
    height = own_a_ref.shape[1]
    lateral = lateral_matrix(own_a_ref.shape[2])
    vertical = without_forced(vertical_ref[...])
    courant = courant_ref[...]
    left, right = sides(odd_ref, within_ref[...], across_ref[...])
    first, last = sides(odd_ref, own_a_ref[...], own_b_ref[...])
    rows_ref[...] = jnp.zeros_like(rows_ref)
    before = [left[0], left[1], first[0], first[1]]
    after = [last[0], last[1], right[0], right[1]]
    for i, columns_of in enumerate((before[:3], before[1:], after[:3], after[1:])):
        updated = stencil(*columns_of, lateral, courant)
        mixed = jnp.dot(vertical, updated.astype(BF16), preferred_element_type=F32)
        keep_rows(rows_ref, i, updated, mixed)
        mixed_out[i] = mixed.astype(BF16)
    copy = pltpu.make_async_copy(mixed_out, mixed_hbm, sem)
    copy.start()
    copy.wait()


def with_edges(main, edges):
    cells = main.shape[0]
    at = iota(main.shape, 0)
    return jnp.where(at == 0, edges[1:2], jnp.where(at == cells - 1, edges[2:3], main))


def ocean_step(ocean_ref, left, right, sea_ref, flux_ref, vertical_ref, out_ref):
    cells, width = sea_ref.shape
    height = ocean_ref.shape[0] // cells
    vertical = vertical_ref[...]
    high = vertical.astype(BF16)
    low = (vertical - high.astype(F32)).astype(BF16)
    both = jnp.concatenate([high, low], axis=0)
    lane = iota((height, width), 1)
    row = iota((height, width), 0)

    def column(x):
        if x < 0:
            return left
        if x >= cells:
            return right
        return ocean_ref[pl.ds(x, height, stride=cells), :]

    parts = []
    for x in range(cells):
        west, center, east = column(x - 1), column(x), column(x + 1)
        north = jnp.where(lane == width - 1, center, pltpu.roll(center, width - 1, 1))
        south = jnp.where(lane == 0, center, pltpu.roll(center, 1, 1))
        wet = sea_ref[x : x + 1, :].astype(F32)
        near = east + west + (north + south) - 4.0 * center
        heat = FLUX_GAIN * wet * flux_ref[0, x : x + 1, :]
        fresh = FLUX_GAIN * wet * flux_ref[1, x : x + 1, :]
        added = jnp.where(row == 0, heat, jnp.where(row == height // 2, fresh, 0.0))
        updated = (center + OCEAN_DIFFUSION * near) * wet + added
        upper = updated.astype(BF16)
        rest = (updated - upper.astype(F32)).astype(BF16)
        parts.append((upper, rest))
        if x % 2 == 0:
            continue
        upper, rest = (jnp.concatenate(p, axis=1) for p in zip(*parts))
        parts = []
        mixed = jnp.dot(both, upper, preferred_element_type=F32)
        mixed = mixed[:height] + mixed[height:]
        mixed += jnp.dot(high, rest, preferred_element_type=F32)
        out_ref[pl.ds(x - 1, height, stride=cells), :] = mixed[:, :width]
        out_ref[pl.ds(x, height, stride=cells), :] = mixed[:, width:]


PARTS = 8


def weight_copies(weight_hbm, held, sems):
    step = weight_hbm.shape[0] // PARTS
    return start_all([
        pltpu.make_async_copy(
            weight_hbm.at[pl.ds(i * step, step)], held.at[pl.ds(i * step, step)], sems.at[i]
        )
        for i in range(PARTS)
    ])


def couple_kernel(
    layers,
    odd_ref, head_ref, goal_ref, within_ref, across_ref, weight_hbm, sea_ref, place_ref,
    rows_ref, edges_ref, courant_ref, vertical_ref, coupled_ref, slots_ref, out_ref,
    slot_rows, by_block, flux_rows, shares, held, sems,
):
    copies = weight_copies(weight_hbm, held, sems)
    devices = head_ref.shape[0]
    blocks, sources = held.shape[0], held.shape[1]
    surface = head_ref[:, 0:16, :].reshape(devices * 16, 128)
    slot_rows[...] = head_ref[:, 16:24, :].astype(F32).reshape(devices * 8, 128)
    slots_ref[...] = jnp.transpose(slot_rows[pl.ds(0, devices, stride=8), :])[:8]

    tiles = 2 * sources
    left_pack, right_pack = (
        p[layers : layers + 16]
        for p in sides(odd_ref, unpack(within_ref[tiles:]), unpack(across_ref[tiles:]))
    )
    lane = iota((8, 128), 1)
    goals = jnp.where(
        lane < blocks,
        goal_ref[...],
        jnp.where(
            lane < blocks + 2,
            pltpu.roll(left_pack[8:], 2, 1),
            jnp.where(lane < blocks + 4, pltpu.roll(right_pack[8:], blocks + 2, 1), -1.0),
        ),
    )
    count = blocks + 8
    goal = jnp.concatenate(
        [
            jnp.transpose(jnp.broadcast_to(goals[k : k + 1], (128, 128)))[:count, :1]
            for k in range(sources)
        ],
        axis=0,
    ).astype(jnp.int32)
    pick = (goal == iota((sources * count, devices * 16), 1)).astype(F32).astype(BF16)
    fetched = jnp.dot(pick, surface, preferred_element_type=F32)
    empty = jnp.zeros((128 - count, 128), F32)
    wanted = jnp.concatenate(
        [
            jnp.transpose(jnp.concatenate([fetched[k * count : (k + 1) * count], empty], axis=0))
            for k in range(sources)
        ],
        axis=0,
    ).astype(BF16)
    lane = iota((128, 128), 1)

    def add(j, weights, total):
        rows = jnp.concatenate(weights, axis=1)
        return jnp.where(lane == j, jnp.dot(rows, wanted, preferred_element_type=F32), total)

    total = jnp.zeros((128, 128), F32)
    for n, weights in enumerate(sides(odd_ref, within_ref[0:tiles], across_ref[0:tiles])):
        for b in range(2):
            total = add(
                blocks + 2 * n + b, [weights[b * sources + k] for k in range(sources)], total
            )
    step = blocks // PARTS
    for i, c in enumerate(copies):
        c.wait()
        for j in range(i * step, (i + 1) * step):
            total = add(j, [held[j, k] for k in range(sources)], total)
    by_block[...] = jnp.transpose(total)

    half = blocks // 2
    temp = jnp.concatenate([by_block[pl.ds(h, half, stride=2), :] for h in range(2)], axis=1)
    coupled_ref[0:half, :] = temp
    exchange = EXCHANGE_RATE * sea_ref[...].astype(F32)
    upper = with_edges(rows_ref[0], edges_ref[0])
    lower = with_edges(rows_ref[1], edges_ref[1])
    heat, moist = exchange * (temp - upper), exchange * (0.5 * temp - lower)
    upper = (upper + heat).astype(BF16).astype(F32)
    lower = (lower + moist).astype(BF16).astype(F32)
    coupled_ref[half : 2 * half, :] = upper
    coupled_ref[2 * half : 3 * half, :] = lower
    halo = []
    for n, (edge, pack) in enumerate(((0, left_pack), (3, right_pack))):
        at = blocks + 2 * n
        warm = jnp.concatenate([by_block[at : at + 1, :], by_block[at + 1 : at + 2, :]], axis=1)
        rate = EXCHANGE_RATE * jnp.concatenate([pack[0:1], pack[1:2]], axis=1)
        u, w = edges_ref[0, edge : edge + 1, :], edges_ref[1, edge : edge + 1, :]
        halo.append((u + rate * (warm - u)).astype(BF16).astype(F32))
        halo.append((w + rate * (0.5 * warm - w)).astype(BF16).astype(F32))
    coupled_ref[3 * half :, :] = jnp.zeros_like(coupled_ref[3 * half :, :])
    for n, line in enumerate(halo):
        coupled_ref[3 * half + n : 3 * half + n + 1, :] = line

    height = vertical_ref.shape[0]
    top, low = height // 2 - 1, height - 1
    cells, width = sea_ref.shape
    sub, lane = iota((cells, width), 0), iota((cells, width), 1)

    def row_of(r, mix, upper, lower):
        a = vertical_ref[pl.ds(r - 7, 8), :].astype(F32)[7:8]
        kept = mix.astype(BF16).astype(F32)
        return (kept + a[:, top : top + 1] * upper + a[:, low : low + 1] * lower).astype(BF16).astype(F32)

    def updated(r, n):
        edges = edges_ref[n]
        center = row_of(r, with_edges(rows_ref[n], edges), upper, lower)
        left = row_of(r, edges[0:1], halo[0], halo[1])
        right = row_of(r, edges[3:4], halo[2], halo[3])
        west = jnp.where(sub == 0, left, pltpu.roll(center, 1, 0))
        east = jnp.where(sub == cells - 1, right, pltpu.roll(center, cells - 1, 0))
        north = jnp.where(lane == width - 1, center, pltpu.roll(center, width - 1, 1))
        south = jnp.where(lane == 0, center, pltpu.roll(center, 1, 1))
        near = east + west + (north + south) - 4.0 * center
        courant = courant_ref[pl.ds(r - 7, 8), :][7:8]
        return center - courant * (center - west) + ATM_DIFFUSION * near

    heat = 0.5 * heat + 0.5 * (exchange * (temp - updated(top, 2)))
    moist = 0.5 * moist + 0.5 * (
        exchange * (0.5 * temp - updated(low, 3))
    )
    flux_rows[...] = jnp.zeros_like(flux_rows)
    for v, flux in enumerate((heat, moist)):
        for h in range(2):
            flux_rows[pl.ds(h * 10 + v, cells, stride=16), :] = flux[:, h * 128 : (h + 1) * 128]
    for x in range(half):
        rows = jnp.concatenate(
            [flux_rows[(2 * x + h) * 8 : (2 * x + h + 1) * 8, :] for h in range(2)], axis=1
        ).astype(BF16)
        weights = jnp.concatenate(
            [
                jnp.concatenate([held[2 * x + h, k] for k in range(sources)], axis=1)
                for h in range(2)
            ],
            axis=0,
        )
        got = jnp.dot(rows, weights, preferred_element_type=F32)
        for k in range(sources):
            at = (k * half + x) * 8
            shares[at : at + 8, :] = got[:, k * 128 : (k + 1) * 128]

    pairs = blocks * sources
    place = place_ref[0:1, :]
    rows = iota((out_ref.shape[0], pairs), 0)
    total = jnp.zeros(out_ref.shape, F32)
    for v in range(2):
        pick = (rows == place + 4 * v).astype(F32).astype(BF16)
        share = jnp.concatenate(
            [shares[pl.ds(2 * h + v, pairs // 2, stride=8), :] for h in range(2)], axis=0
        ).astype(BF16)
        total += jnp.dot(pick, share, preferred_element_type=F32)
    out_ref[...] = total.astype(BF16)


def second_step_kernel(
    tiles, odd_ref, mixed_hbm, edge_hbm, courant_ref, vertical_ref, sea_ref, coupled_ref,
    ocean_hbm, within_ref, across_ref, ocean_sea_ref, flux_ref, ocean_vertical_ref,
    out_hbm, new_ocean_hbm,
    mixed_ref, edge_ref, state, result, out_ref, ocean_ref, new_ocean_ref,
    in_sems, edge_sem, ocean_sems, out_sems,
):
    edge_copy = pltpu.make_async_copy(edge_hbm, edge_ref, edge_sem)
    edge_copy.start()
    coming = start_all(groups(mixed_hbm, mixed_ref, in_sems))
    ocean_coming = pltpu.make_async_copy(ocean_hbm, ocean_ref, ocean_sems.at[0])
    ocean_coming.start()
    cells, height = mixed_ref.shape[0], mixed_ref.shape[1]
    top, low = height // 2 - 1, height - 1
    lateral = lateral_matrix(mixed_ref.shape[2])
    vertical = vertical_ref[...]
    upper_column = vertical[:, top : top + 1].astype(F32)
    lower_column = vertical[:, low : low + 1].astype(F32)
    courant = courant_ref[...]
    halo = 3 * cells

    def complete(to, mixed, upper_at, lower_at):
        upper = coupled_ref[upper_at : upper_at + 1, :]
        lower = coupled_ref[lower_at : lower_at + 1, :]
        done = mixed.astype(F32) + upper_column * upper + lower_column * lower
        state[to] = done.astype(BF16)

    last = iota((8, mixed_ref.shape[2]), 0) == 7

    def advance(x):
        updated = stencil(state[x], state[x + 1], state[x + 2], lateral, courant)
        exchange = EXCHANGE_RATE * sea_ref[x : x + 1, :].astype(F32)
        temp = coupled_ref[x : x + 1, :]
        upper = updated[top - 7 : top + 1]
        lower = updated[low - 7 : low + 1]
        upper = jnp.where(last, upper + exchange * (temp - upper), upper)
        lower = jnp.where(last, lower + exchange * (0.5 * temp - lower), lower)
        forced = jnp.concatenate(
            [updated[: top - 7], upper, updated[top + 1 : low - 7], lower], axis=0
        ).astype(BF16)
        result[x] = jnp.dot(vertical, forced, preferred_element_type=F32).astype(BF16)

    edge_copy.wait()
    coming[0].wait()
    complete(0, edge_ref[0], halo, halo + 1)
    complete(1, edge_ref[1], cells, 2 * cells)
    going = []
    step, half = 32, cells // 2
    for x in range(cells):
        ahead = x + 1
        if ahead % GROUP == 0 and ahead < cells:
            coming[ahead // GROUP].wait()
        if ahead < cells - 1:
            complete(ahead + 1, mixed_ref[ahead], cells + ahead, 2 * cells + ahead)
        elif ahead == cells - 1:
            complete(cells, edge_ref[2], 2 * cells - 1, 3 * cells - 1)
        else:
            complete(cells + 1, edge_ref[3], halo + 2, halo + 3)
        advance(x)
        if (x + 1) % half:
            continue
        across = slice(x + 1 - half, x + 1)
        for i in range(height // step):
            at = slice(i * step, (i + 1) * step)
            out_ref[at, across, :] = jnp.swapaxes(result[across, at, :], 0, 1)
        ends = out_ref.at[:, across], out_hbm.at[:, across]
        going.append(pltpu.make_async_copy(*ends, out_sems.at[(x + 1) // half - 1]))
        going[-1].start()
        if x + 1 == cells:
            break
        ocean_coming.wait()
        layers = ocean_ref.shape[0] // ocean_sea_ref.shape[0]
        left, right = (
            p[:layers]
            for p in sides(odd_ref, unpack(within_ref[tiles:]), unpack(across_ref[tiles:]))
        )
        ocean_step(
            ocean_ref, left, right, ocean_sea_ref, flux_ref, ocean_vertical_ref, new_ocean_ref
        )
        going.append(pltpu.make_async_copy(new_ocean_ref, new_ocean_hbm, ocean_sems.at[1]))
        going[-1].start()
    wait_all(going)


def land_kernel(incoming_ref, slots_ref, sea_ref, out_ref, wide):
    devices = slots_ref.shape[1]
    cells = sea_ref.shape[0]
    wide[...] = incoming_ref[...].astype(F32)
    wet = sea_ref[...].astype(F32)
    here = (iota((cells, devices), 0) + 1).astype(F32)
    picks = [(slots_ref[s : s + 1, :] == here).astype(F32).astype(BF16) for s in range(4)]
    for v in range(2):
        total = jnp.zeros((cells, 128), F32)
        for s in range(4):
            part = wide[pl.ds(v * 4 + s, devices, stride=8), :].astype(BF16)
            total += jnp.dot(picks[s], part, preferred_element_type=F32)
        out_ref[v] = total * wet


def swap(within, across):
    peers = lax.axis_size(BOTH)
    pair = [(i, i ^ 1) for i in range(peers)]
    other = [(i, ((i + 1) ^ 1) - 1) for i in range(peers)]
    other = [(i, j % peers) for i, j in other]
    return lax.ppermute(within, BOTH, pair), lax.ppermute(across, BOTH, other)


def per_device(
    atm_state, atm_sea, zonal_courant, atm_vertical, ocean_state, ocean_sea,
    flux_in, ocean_vertical, remap_owner, remap_block, remap_weight,
):
    devices = lax.axis_size(BOTH)
    height, cells, width = atm_state.shape
    blocks, sources = remap_owner.shape
    pairs = blocks * sources
    courant = zonal_courant.reshape(height, 1)
    layers, ocean_cells, ocean_width = ocean_state.shape
    ocean_rows = ocean_state.reshape(layers * ocean_cells, ocean_width)
    owner, block = remap_owner.T, remap_block.T
    odd = is_odd()
    dma = pltpu.SemaphoreType.DMA
    held = [pltpu.VMEM(remap_weight.shape, BF16), dma((PARTS,))]
    whole = pltpu.VMEM((cells, height, width), BF16)
    levels = 128

    head, place = call(
        plan_kernel,
        (shape((devices, HEAD, 128), BF16), shape((8, pairs), jnp.int32)),
        owner, block, ocean_state,
        specs={0: ANY, 1: ANY, 2: ANY},
        scratch=[
            pltpu.VMEM((devices * 8, 128), F32),
            pltpu.VMEM((pairs, 128), F32),
            pltpu.VMEM(owner.shape, jnp.int32),
            pltpu.VMEM(owner.shape, jnp.int32),
            pltpu.VMEM((ocean_cells, ocean_width), F32),
            dma((3,)),
        ],
        limit=58,
        touched=1 << 20,
    )
    gathered = lax.all_to_all(head, BOTH, split_axis=0, concat_axis=0, tiled=True)

    tiles = 2 * sources
    columns_sent = shape((2, height, width), BF16)
    load = shape((tiles + 2 * PACK // 128, 128, 128), BF16)
    state_a, state_b, load_a, load_b, goal = call(
        edges_kernel,
        (columns_sent, columns_sent, load, load, shape((8, 128), F32)),
        odd, atm_state, ocean_state, remap_weight.reshape(pairs, 128, 128), owner, block, atm_sea,
        specs={
            0: SCALAR,
            1: pl.BlockSpec((levels, cells, width), lambda i: (i, 0, 0)),
            2: ANY,
            3: ANY,
        },
        scratch=[pltpu.VMEM((layers, ocean_width), F32)] * 2 + [dma((4,))],
        grid=(height // levels,),
        limit=54,
        touched=6 << 20,
    )
    state_near = swap(state_a, state_b)
    load_near = swap(load_a, load_b)
    mixed, rows = call(
        first_step_kernel,
        (shape((cells, height, width), BF16), shape((4, cells, width), F32)),
        atm_state, courant, atm_vertical,
        specs={0: ANY},
        out_specs={0: ANY},
        scratch=[
            pltpu.VMEM(atm_state.shape, BF16), whole, whole,
            dma((LEVEL_PARTS,)), dma((cells // GROUP,)),
        ],
        touched=16 << 20,
    )
    mixed_edge, edge_rows = call(
        first_edges_kernel,
        (shape((4, height, width), BF16), shape((4, 8, width), F32)),
        odd, *state_near, state_a, state_b, courant, atm_vertical,
        specs={0: SCALAR},
        out_specs={0: ANY},
        scratch=[pltpu.VMEM((4, height, width), BF16), dma],
        limit=50,
        touched=2 << 20,
    )

    coupled, slots, outgoing = call(
        functools.partial(couple_kernel, layers),
        (
            shape((3 * cells + 8, width), F32),
            shape((8, devices), F32),
            shape((devices * 8, 128), BF16),
        ),
        odd, gathered, goal, *load_near, remap_weight, atm_sea, place,
        rows, edge_rows, courant, atm_vertical,
        specs={0: SCALAR, 5: ANY},
        scratch=[
            pltpu.VMEM((devices * 8, 128), F32),
            pltpu.VMEM((128, 128), F32),
            pltpu.VMEM((blocks * 8, 128), F32),
            pltpu.VMEM((pairs * 4, 128), F32),
            *held,
        ],
        limit=50,
        touched=16 << 20,
    )
    incoming = lax.all_to_all(
        outgoing.reshape(devices, 8, 128), BOTH, split_axis=0, concat_axis=0, tiled=True
    )
    state, new_ocean = call(
        functools.partial(second_step_kernel, tiles),
        (shape(atm_state.shape, BF16), shape(ocean_rows.shape, F32)),
        odd, mixed, mixed_edge, courant, atm_vertical, atm_sea, coupled,
        ocean_rows, *load_near, ocean_sea, flux_in, ocean_vertical,
        specs={0: SCALAR, 1: ANY, 2: ANY, 7: ANY},
        out_specs={0: ANY, 1: ANY},
        scratch=[
            whole,
            pltpu.VMEM((4, height, width), BF16),
            pltpu.VMEM((cells + 2, height, width), BF16),
            whole,
            pltpu.VMEM(atm_state.shape, BF16),
            pltpu.VMEM(ocean_rows.shape, F32),
            pltpu.VMEM(ocean_rows.shape, F32),
            dma((cells // GROUP,)),
            dma,
            dma((2,)),
            dma((2,)),
        ],
        limit=52,
        touched=24 << 20,
    )
    ocean_flux = call(
        land_kernel,
        shape((2, ocean_cells, ocean_width), F32),
        incoming.reshape(devices * 8, 128), slots, ocean_sea,
        scratch=[pltpu.VMEM((devices * 8, 128), F32)],
        touched=1 << 20,
    )
    return state, new_ocean.reshape(ocean_state.shape), ocean_flux


def solution(mesh):
    return jax.shard_map(
        per_device,
        mesh=mesh,
        in_specs=(
            P(None, BOTH, None), P(BOTH, None), P(), P(), P(None, BOTH, None), P(BOTH, None),
            P(None, BOTH, None), P(), P(BOTH, None), P(BOTH, None), P(BOTH, None, None, None),
        ),
        out_specs=(P(None, BOTH, None), P(None, BOTH, None), P(None, BOTH, None)),
        check_vma=False,
    )
```
